512 devices in a mesh: gz: 128 (over z, y, core), pa: 4 (over x).
Axes of the slice: x: 4, y: 4, z: 16, core: 2. Of those that a mesh axis runs over, the one named last changes fastest.
Arguments:
- velocity: float32 [3, 128, 192, 512], P(None, 'gz', None, 'pa'), may hold values from -4 to 4
- viscosity: float32 [128, 192, 512], P('gz', None, 'pa'), may hold values from 0.2 to 2
- parcels: float32 [524288, 16], P(('gz', 'pa')), may hold values from -4 to 4, as said below
- dest_rank: int32 [524288, 1], P(('gz', 'pa')), may hold values from 0 to 127; in each aligned block of 1024 rows (0 to 1023, 1024 to 2047, ...) at most 24 rows name the same one
- dest_cell: int32 [524288], P(('gz', 'pa')), may hold values from 0 to 24575
- counts: int32 [512], P(('gz', 'pa')), may hold values from 1 to 1024, 393216 in all
Outputs:
- velocity_out: float32 [3, 128, 192, 512], P(None, 'gz', None, 'pa')
- parcels_out: float32 [1572864, 16], P(('gz', 'pa'))
The draws below stay inside these ranges and needn't reach their ends.
Inputs may be any that keep to these rules, and one draw needn't show every extreme that they name: `dest_rank`: among the 1024 rows of one device no slab is named more than 24 times, and some block names one slab exactly 24 times. `counts`: some device has all 1024 rows live. `parcels`: columns 4 k + 3 hold positive drag rates.
All inputs are finite; a program needn't handle non-finite values.
Results may differ from the reference program's by a relative error of at most 0.0011.
Values sent between devices are 32-bit elements; how exact they have to be, the bound alone decides.
No kernel may reach another device: no remote copies, remote signals or barrier semaphores. Data moves between devices by JAX's collectives and lax.ppermute only.
A program may use at most 64 MiB of HBM per device.

```python
import math
import jax
import jax.numpy as jnp
import numpy as np
from jax import lax

NR = 192
NTH = 512
CZ = 1
PAR_DEV = 1024
CAP = 24
NZ = 128
CT = 128
CELLS_DEV = 24576
PARCELS = 524288
N_GZ = 128
N_PA = 4
DEVICES = 512


def draw_velocity(key, part):
    key = jax.random.fold_in(key, 5)
    shape = (3, NZ, NR, NTH)
    values = jnp.clip(jax.random.normal(key, shape, jnp.float32), -4.0, 4.0)
    return values


def draw_parcels(key, part):
    key = jax.random.fold_in(key, 9)
    speed_key, rate_key = jax.random.split(key)
    speeds = jnp.clip(jax.random.normal(speed_key, (PARCELS, 4, 3), jnp.float32), -4.0, 4.0)
    rates = jnp.exp(jax.random.uniform(rate_key, (PARCELS, 4, 1), jnp.float32, math.log(0.2), math.log(3.0)))
    return jnp.concatenate([speeds, rates], -1).reshape(PARCELS, 16)


def set_ends(result, rng, least, top_value):
    longest = result.shape.index(max(result.shape))
    spots = []
    for shift in (0, 1):
        where = [jax.random.randint(jax.random.fold_in(rng, axis), (), 0, length) for axis, length in enumerate(result.shape)]
        where[longest] = (where[longest] + shift) % result.shape[longest]
        spots.append(tuple(where))
    return result.at[spots[0]].set(least).at[spots[1]].set(top_value)


def levels(key, extent, cuts, least, largest):
    level, own = 1.0, jax.random.fold_in(key, 6)
    for position, blocks in cuts:
        steps = jnp.exp(jax.random.uniform(jax.random.fold_in(own, position), (blocks,), jnp.float32, least / len(cuts), largest / len(cuts)))
        level = level * jnp.repeat(steps, extent[position] // blocks).reshape([-1 if axis == position else 1 for axis in range(len(extent))])
    return level


def split_up(number_of, total, bound, slope):
    weights = [(1 << 20) // math.isqrt(grade ** slope) + 1 for grade in range(2, number_of + 1)]
    spare, given = total - bound - (number_of - 1), [1] * (number_of - 1)
    while spare > 0:
        movable = [i for i in range(number_of - 1) if given[i] < bound]
        mass, left = sum([weights[i] for i in movable]), spare
        for i in movable:
            more = min(bound - given[i], max(1, left * weights[i] // mass), spare)
            given[i] = given[i] + more
            spare = spare - more
    return np.array([bound] + given)


def uneven(key, amount, total, most, slope):
    if amount == 2:
        one = jax.random.randint(key, (), max(1, total - most), min(most, total - 1) + 1)
        return jnp.stack([one, total - one])
    sizes = jnp.asarray(split_up(amount, total, most, slope), jnp.int32)
    pairs = (amount - 1) // 2
    donor, taker = sizes[1:1 + 2 * pairs:2], sizes[2:2 + 2 * pairs:2]
    room = jnp.minimum(donor - 1, most - taker)
    shifted = jax.random.randint(jax.random.fold_in(key, 1), (pairs,), 0, 1 << 20) % (room + 1)
    sizes = sizes.at[1:1 + 2 * pairs:2].set(donor - shifted).at[2:2 + 2 * pairs:2].set(taker + shifted)
    return sizes[jax.random.permutation(jax.random.fold_in(key, 2), amount)]


def shared_out(key, own, number, rows, number_of, top, bound, slope):
    order = jax.random.permutation(key, number_of)
    crowded, ordinary = portions_of(number_of, rows * top, bound, slope, True), portions_of(number_of, rows * top, bound, slope, False)
    places = jnp.arange(number_of)

    def named(sizes, offset_by):
        used = int((sizes > 0).sum())
        fixed = max(1, used // 4)
        moved = fixed + (places - fixed + offset_by * (used - fixed)) % max(1, number_of - fixed)
        return jnp.zeros((number_of,), jnp.int32).at[order[jnp.where(places < fixed, places, moved)]].set(jnp.asarray(sizes, jnp.int32))

    sizes = jnp.where(number % 4 == 0, named(crowded, number // 4), named(ordinary, number - number // 4 - 1))
    mixed = jax.random.permutation(jax.random.fold_in(own, 3), number_of)
    giver, taker = mixed[0:number_of // 2 * 2:2], mixed[1:number_of // 2 * 2:2]
    room = jnp.minimum(sizes[giver] - 1, bound - sizes[taker]) // 2
    room = jnp.where((giver == order[0]) | (taker == order[0]) | (sizes[taker] == 0), 0, jnp.maximum(room, 0))
    moved = jax.random.randint(jax.random.fold_in(own, 4), (number_of // 2,), 0, 1 << 20) % (room + 1)
    sizes = sizes.at[giver].add(-moved).at[taker].add(moved)
    members = jnp.searchsorted(jnp.cumsum(sizes), jnp.arange(rows * top), side="right").astype(jnp.int32)
    listing = members.reshape(top, rows).T
    listing = listing[jax.random.permutation(jax.random.fold_in(own, 1), rows)]
    offset_by = jax.random.randint(jax.random.fold_in(own, 2), (rows, 1), 0, top)
    return jnp.take_along_axis(listing, (jnp.arange(top)[None, :] + offset_by) % top, axis=1)


def portions_of(amount, total, limit, slope, full):
    portions = [(1 << 20) // math.isqrt(grade ** slope) + 1 for grade in range(1, amount + 1)]
    largest = limit if full else min(limit, max(-(-total // amount), total * portions[0] // sum(portions)))
    least = 1 if total - largest >= amount - 1 else 0
    holding, surplus = [largest] + [least] * (amount - 1), total - largest - least * (amount - 1)
    while surplus > 0:
        free = [i for i in range(1, amount) if holding[i] < largest] or [i for i in range(1, amount) if holding[i] < limit]
        pool, budget = sum([portions[i] for i in free]), surplus
        for i in free:
            extra = min(limit - holding[i], max(1, budget * portions[i] // pool), surplus)
            holding[i] = holding[i] + extra
            surplus = surplus - extra
    return np.array(holding)


def setup_inputs(seed: int = 0) -> dict:
    key_list = jax.random.split(jax.random.key(seed), 7)
    velocity = draw_velocity(jax.random.fold_in(key_list[6], 71), 0)
    viscosity = jnp.clip(jnp.exp(math.log(2.0) - 2.3025851 * jax.random.uniform(key_list[1], (NZ, NR, NTH), jnp.float32) ** levels(key_list[1], (NZ, NR, NTH), ((0, 128), (2, 4)), -0.2, 0.2)), 0.2, 2.0)
    parcels = draw_parcels(jax.random.fold_in(key_list[6], 71), 0)
    dest_rank_keys = jax.random.split(jax.random.fold_in(key_list[3], 1), PARCELS // PAR_DEV)
    dest_rank_turns = jax.random.permutation(jax.random.fold_in(key_list[3], 3), PARCELS // PAR_DEV)
    dest_rank = jax.vmap(lambda own, number: shared_out(jax.random.fold_in(key_list[3], 2), own, number, PAR_DEV, N_GZ, 1, CAP, 2))(dest_rank_keys, dest_rank_turns).reshape((PARCELS, 1))
    dest_cell = set_ends(jax.random.randint(key_list[4], (PARCELS,), 0, CELLS_DEV), jax.random.fold_in(key_list[4], 1), 0, CELLS_DEV - 1).astype(jnp.int32)
    counts = uneven(key_list[5], DEVICES, 3 * PAR_DEV * DEVICES // 4, PAR_DEV, 0).astype(jnp.int32)
    return dict(velocity=velocity, viscosity=viscosity, parcels=parcels, dest_rank=dest_rank, dest_cell=dest_cell, counts=counts)


time_step = 0.1
shift_plane = 0.0001

def radius_column(first, number):
    return (NR + first + jnp.arange(number) + 0.5).astype(jnp.float32)[:, None]

def viscous(extended, speeds, viscosity):
    planes, radii, columns = viscosity.shape
    radius = radius_column(0, radii)
    step_angle = 2.0 * math.pi / NTH
    arc_weight = 1.0 / (radius * step_angle) ** 2
    offsets = ((1, 0, 0, 1.0), (-1, 0, 0, 1.0), (0, 1, 0, (radius + 0.5) / radius), (0, -1, 0, (radius - 0.5) / radius), (0, 0, 1, arc_weight), (0, 0, -1, arc_weight))
    total = jnp.zeros_like(speeds)
    for shift_z, shift_r, shift_t, weight in offsets:
        beside = extended[:, 1 + shift_z:1 + shift_z + planes, 1 + shift_r:1 + shift_r + radii, 1 + shift_t:1 + shift_t + columns]
        face_mean = 0.5 * (viscosity + beside[3])
        total = total + weight * face_mean * (beside[:3] - speeds)
    return total

def radial_divergence(radial_speed):
    radii = radial_speed.shape[-2]
    radius = radius_column(0, radii)
    mean_face = 0.5 * (radial_speed[..., 1:, :] + radial_speed[..., :-1, :])
    inner = (radius[1:] - 0.5) * mean_face
    zeros = jnp.zeros_like(radial_speed[..., :1, :])
    flux = jnp.concatenate([zeros, inner, zeros], axis=-2)
    return (flux[..., 1:, :] - flux[..., :-1, :]) / radius

def theta_difference(values, radius):
    step_angle = 2.0 * math.pi / NTH
    return (jnp.roll(values, -1, -1) - jnp.roll(values, 1, -1)) / (2.0 * step_angle * radius)

def radial_system(modes):
    radius = radius_column(0, NR)[:, 0]
    step_angle = 2.0 * math.pi / NTH
    arc_weight = 1.0 / (radius * step_angle) ** 2
    nothing = jnp.zeros((1,), jnp.float32)
    upper = jnp.concatenate([(radius[:-1] + 0.5) / radius[:-1], nothing])
    lower = jnp.concatenate([nothing, (radius[1:] - 0.5) / radius[1:]])
    spectrum = 2.0 - 2.0 * jnp.cos(step_angle * modes.astype(jnp.float32))
    diagonal = shift_plane + arc_weight[None, :] * spectrum[:, None] + upper[None, :] + lower[None, :]
    return (jnp.broadcast_to(-lower, diagonal.shape), diagonal, jnp.broadcast_to(-upper, diagonal.shape))

def mirror_gradient(values):
    padded = jnp.concatenate([values[..., :1, :], values, values[..., -1:, :]], axis=-2)
    return 0.5 * (padded[..., 2:, :] - padded[..., :-2, :])

def hartley(values):
    spectrum = jnp.fft.fft(values, axis=-1)
    return spectrum.real - spectrum.imag

def block_slots(pair):
    target_block, live_block = pair
    marks = ((target_block[:, None] == jnp.arange(N_GZ)[None, :]) & live_block[:, None]).astype(jnp.int32)
    before = jnp.cumsum(marks, axis=0) - marks
    return jnp.sum(before * marks, axis=1)

def reference(velocity, viscosity, parcels, dest_rank, dest_cell, counts):
    positions = jnp.arange(DEVICES * PAR_DEV)
    owner_block = positions // PAR_DEV
    live = positions % PAR_DEV < counts[owner_block]
    target = dest_rank[:, 0]
    slot = lax.map(block_slots, (target.reshape(DEVICES, PAR_DEV), live.reshape(DEVICES, PAR_DEV))).reshape(-1)
    source_gz = owner_block // N_PA
    source_pa = owner_block % N_PA
    receiver = target * N_PA + source_pa
    row_index = (receiver * N_GZ + source_gz) * CAP + slot
    row_index = jnp.where(live, row_index, DEVICES * N_GZ * CAP)
    axial = target * CZ + dest_cell // (NR * CT)
    radial = dest_cell // CT % NR
    azimuth = source_pa * CT + dest_cell % CT
    fluid = velocity[:, axial, radial, azimuth].T
    classes = parcels.reshape(-1, 4, 4)
    speed = classes[..., :3]
    rate = classes[..., 3:]
    moved = (speed + time_step * rate * fluid[:, None, :]) / (1.0 + time_step * rate)
    drag = jnp.sum(rate * (moved - fluid[:, None, :]), axis=1).astype(jnp.bfloat16)
    drag = lax.optimization_barrier(drag).astype(jnp.float32)
    drag = jnp.where(live[:, None], drag, 0.0)
    updated = jnp.concatenate([moved, rate], -1).reshape(-1, 16)
    parcels_out = jnp.zeros((DEVICES * N_GZ * CAP, 16), jnp.float32).at[row_index].set(updated, mode='drop')
    deposit = jnp.zeros_like(velocity).at[:, axial, radial, azimuth].add(drag.T)
    fields = jnp.concatenate([velocity, viscosity[None]], 0)
    fields = jnp.pad(fields, ((0, 0), (1, 1), (1, 1), (0, 0)))
    extended = jnp.concatenate([fields[..., -1:], fields, fields[..., :1]], -1)
    ustar = velocity + time_step * (viscous(extended, velocity, viscosity) + deposit)
    radius = radius_column(0, NR)
    source = -(radial_divergence(ustar[1]) + theta_difference(ustar[2], radius))
    spectral = jnp.transpose(hartley(source), (2, 1, 0))
    weights = radius[:, 0]
    correction = jnp.sum(weights[:, None] * spectral[0], axis=0) / jnp.sum(weights)
    spectral = spectral.at[0].add(-correction[None, :])
    lower, diagonal, upper = radial_system(jnp.arange(NTH))
    potential_hat = lax.linalg.tridiagonal_solve(lower, diagonal, upper, spectral)
    radial_hat = mirror_gradient(potential_hat)
    both = jnp.transpose(jnp.stack([radial_hat, potential_hat]), (0, 3, 2, 1))
    physical = hartley(both) / NTH
    grad_r = physical[0]
    grad_t = theta_difference(physical[1], radius)
    velocity_out = jnp.stack([ustar[0], ustar[1] - grad_r, ustar[2] - grad_t])
    return (velocity_out, parcels_out)
```

```python
import functools
import math

import jax
import jax.numpy as jnp
import numpy as np
from jax import lax
from jax.experimental import pallas as pl
from jax.experimental.pallas import tpu as pltpu
from jax.sharding import PartitionSpec as P

NR = 192
NTH = 512
time_step = 0.1
shift_plane = 0.0001
step_angle = 2.0 * math.pi / NTH
LANES = 128
FEATURES = 16
f32 = jnp.float32
bf16 = jnp.bfloat16


def cas(numbers):
    phase = 2.0 * np.pi / NTH * (numbers % NTH)
    return np.cos(phase) + np.sin(phase)


def split_table(table):
    high = table.astype(jnp.bfloat16)
    low = (table - high.astype(np.float64)).astype(jnp.bfloat16)
    return high, low


@functools.cache
def forward_tables(ring, columns):
    out = []
    for me in range(ring):
        angles = me * columns + np.arange(columns)
        modes = np.concatenate([(me + hop) % ring * columns + np.arange(columns) for hop in range(ring)])
        plain = cas(angles[:, None] * modes[None, :])
        ahead = cas((angles[:, None] + 1) * modes[None, :])
        behind = cas((angles[:, None] - 1) * modes[None, :])
        out.append(np.concatenate(split_table(np.concatenate([plain, behind - ahead], 0)), 1))
    return np.stack(out)


@functools.cache
def inverse_tables(ring, columns):
    out = []
    for me in range(ring):
        angles = me * columns + np.arange(columns)
        modes = np.concatenate([(me - hop) % ring * columns + np.arange(columns) for hop in range(ring)])
        plain = cas(modes[:, None] * angles[None, :]) * (0.5 / NTH)
        ahead = cas(modes[:, None] * (angles[None, :] + 1)) / NTH
        behind = cas(modes[:, None] * (angles[None, :] - 1)) / NTH
        out.append(np.concatenate(split_table(plain) + split_table(ahead - behind), 1))
    return np.stack(out)


@functools.cache
def reduction_tables(ring, columns):
    radius = NR + np.arange(NR) + 0.5
    arc = 1.0 / (radius * step_angle) ** 2
    up = (radius + 0.5) / radius
    down = (radius - 0.5) / radius
    up[-1] = 0.0
    down[0] = 0.0
    modes = np.arange(NTH)
    spectrum = 2.0 - 2.0 * np.cos(step_angle * modes)
    diagonal = shift_plane + arc[:, None] * spectrum[None, :] + up[:, None] + down[:, None]
    lower = np.broadcast_to(-down[:, None], diagonal.shape)
    upper = np.broadcast_to(-up[:, None], diagonal.shape)

    def moved(x, by, fill):
        filled = np.full((abs(by),) + x.shape[1:], fill)
        return np.concatenate([filled, x[:-by]], 0) if by > 0 else np.concatenate([x[-by:], filled], 0)

    tables, stride = [], 1
    while stride < NR:
        low = lower / moved(diagonal, stride, 1.0)
        high = upper / moved(diagonal, -stride, 1.0)
        diagonal = diagonal - low * moved(upper, stride, 0.0) - high * moved(lower, -stride, 0.0)
        lower = -low * moved(lower, stride, 0.0)
        upper = -high * moved(upper, -stride, 0.0)
        tables += [low, high]
        stride *= 2
    tables.append(1.0 / diagonal)
    stacked = np.stack(tables).astype(np.float32)
    return np.ascontiguousarray(stacked.reshape(len(tables), NR, ring, columns).transpose(2, 0, 1, 3))


def pieces(x, count):
    out = []
    for _ in range(count):
        part = x.astype(bf16).astype(f32)
        out.append(part)
        x = x - part
    return out


def dot(a, b, contract):
    return lax.dot_general(a, b, (contract, ((), ())), preferred_element_type=f32)


def iota(shape, dim):
    return lax.broadcasted_iota(jnp.int32, shape, dim)


def pack_kernel(capacity, slabs, counts, parcels, target, cell, velocity, viscosity, send, first, last, spread, hot):
    rows = parcels.shape[1]
    width = 256
    live = iota((1, rows), 1) < counts[0]
    wanted = jnp.where(live, target[...], -1)
    cells = cell[...]
    line = (cells // LANES + 1).astype(f32)
    column = (cells % LANES).astype(f32)
    earlier = (iota((width, width), 0) < iota((width, width), 1)).astype(bf16)
    ones = jnp.ones((width, width), bf16)
    features = FEATURES * capacity
    total = features + 2 * capacity
    passed = None
    for block in range(rows // width):
        here = slice(block * width, (block + 1) * width)
        mine = iota((slabs, width), 0) == wanted[:, here]
        mark = mine.astype(f32)
        before = dot(mark.astype(bf16), earlier, ((1,), (0,)))
        if passed is not None:
            before = before + dot(passed.astype(bf16), ones, ((1,), (0,)))
        passed = mark if passed is None else passed + mark
        slot = jnp.sum(mark * before, axis=0, keepdims=True).astype(jnp.int32)
        chosen = iota((capacity, width), 0) == slot
        hot[:, here] = mark.astype(bf16)
        split = pieces(parcels[:, here], 3)

        def placed(row):
            return jnp.where(chosen, row, 0.0)

        for k, part in enumerate(split):
            base = 0 if k == 0 else total + (k - 1) * features
            for f in range(0, FEATURES, 2):
                pair = jnp.concatenate([placed(part[f : f + 1]), placed(part[f + 1 : f + 2])], 0)
                spread[base + f * capacity : base + (f + 2) * capacity, here] = pair.astype(bf16)
        pair = jnp.concatenate([placed(line[:, here]), placed(column[:, here])], 0)
        spread[features:total, here] = pair.astype(bf16)
    out = dot(spread[...], hot[...], ((1,), (1,)))
    values = out[:features] + (out[total : total + features] + out[total + features :])
    filler = jnp.zeros((send.shape[0] // slabs * LANES - total, slabs), f32)
    whole = jnp.concatenate([values, out[features:total], filler], 0)
    lines = send.shape[0] // slabs
    for c in range(lines):
        send[pl.ds(c, slabs, stride=lines), :] = whole[c * LANES : (c + 1) * LANES].T
    fields = jnp.concatenate([velocity[...], viscosity[...]], 0)
    for b in range(fields.shape[0] // LANES):
        turned = fields[b * LANES : (b + 1) * LANES].T
        first[b : b + 1, :] = turned[:1]
        last[b : b + 1, :] = turned[LANES - 1 :]


def shifted(x, by):
    length = x.shape[0]
    if by % 8 == 0:
        filled = jnp.zeros((abs(by),) + x.shape[1:], x.dtype)
        return jnp.concatenate([filled, x[:-by]], 0) if by > 0 else jnp.concatenate([x[-by:], filled], 0)
    rolled = pltpu.roll(x, by % length, 0)
    row = iota(x.shape, 0)
    inside = row >= by if by > 0 else row < length + by
    return jnp.where(inside, rolled, 0.0)


def momentum_kernel(
    capacity, slabs, received, velocity, viscosity, below_u, above_u, below_n, above_n, left, right, tables,
    ustar, outgoing, moved, table, line_hot, pulled, pushed, sem,
):
    me = lax.axis_index("pa")
    fetch = pltpu.make_async_copy(tables.at[me], table, sem)
    fetch.start()
    lines = received.shape[0] // slabs
    radii, columns = viscosity.shape
    turned = jnp.concatenate([received[pl.ds(c, slabs, stride=lines), :].T for c in range(lines)], 0)
    features = FEATURES * capacity
    line_of = turned[features : features + capacity].astype(jnp.int32) - 1
    column_of = turned[features + capacity : features + 2 * capacity].astype(jnp.int32)
    speeds = [velocity[c * radii : (c + 1) * radii, :] for c in range(3)]
    across = jnp.concatenate([s.T for s in speeds], 0)
    halves = jnp.concatenate([p.astype(bf16) for p in pieces(across, 2)], 1)
    group = 2
    for j in range(0, capacity, group):
        here = slice(j * LANES, (j + group) * LANES)
        lane_line = jnp.concatenate([line_of[s : s + 1] for s in range(j, j + group)], 1)
        lane_column = jnp.concatenate([column_of[s : s + 1] for s in range(j, j + group)], 1)
        hot = (iota((radii, group * LANES), 0) == lane_line).astype(bf16)
        line_hot[:, here] = hot
        picked = dot(halves, jnp.concatenate([hot, hot], 0), ((1,), (0,)))
        match = iota((columns, group * LANES), 0) == lane_column
        for c in range(3):
            got = jnp.sum(jnp.where(match, picked[c * columns : (c + 1) * columns], 0.0), axis=0, keepdims=True)
            for s in range(group):
                pulled[c, j + s : j + s + 1, :] = got[:, s * LANES : (s + 1) * LANES]
    fluid = [pulled[c] for c in range(3)]
    drag = [jnp.zeros_like(fluid[0]) for _ in range(3)]
    for k in range(4):
        rate = turned[(4 * k + 3) * capacity : (4 * k + 4) * capacity]
        weight = time_step * rate
        scale = 1.0 / (1.0 + weight)
        moved[(4 * k + 3) * capacity : (4 * k + 4) * capacity, :] = rate
        for c in range(3):
            at = (4 * k + c) * capacity
            after = (turned[at : at + capacity] + weight * fluid[c]) * scale
            moved[at : at + capacity, :] = after
            drag[c] = drag[c] + rate * (after - fluid[c])
    drag = [d.astype(bf16).astype(f32) for d in drag]
    for j in range(capacity):
        match = iota((columns, LANES), 0) == column_of[j : j + 1]
        for c in range(3):
            pushed[c * columns : (c + 1) * columns, j * LANES : (j + 1) * LANES] = jnp.where(
                match, drag[c][j : j + 1], 0.0
            ).astype(bf16)
    deposit = dot(line_hot[...], pushed[...], ((1,), (1,)))

    radius = iota((radii, columns), 0).astype(f32) + (NR + 0.5)
    arc = 1.0 / (radius * step_angle) ** 2
    lane = iota((radii, columns), 1)
    edges = [e[...].T for e in (left, right)]

    def column(side, field):
        parts, row = [], field * radii
        while row < (field + 1) * radii:
            block, inner = divmod(row, LANES)
            stop = min(LANES, inner + (field + 1) * radii - row)
            parts.append(edges[side][inner:stop, block : block + 1])
            row += stop - inner
        return jnp.concatenate(parts, 0)

    def around(field, x, below, above):
        return (
            above,
            below,
            shifted(x, -1),
            shifted(x, 1),
            jnp.where(lane == columns - 1, column(1, field), pltpu.roll(x, columns - 1, 1)),
            jnp.where(lane == 0, column(0, field), pltpu.roll(x, 1, 1)),
        )

    weights = (0.5, 0.5, 0.5 * (radius + 0.5) / radius, 0.5 * (radius - 0.5) / radius, 0.5 * arc, 0.5 * arc)
    nu = viscosity[...]
    faces = [w * (nu + n) for w, n in zip(weights, around(3, nu, below_n[...], above_n[...]))]
    stars = []
    for c in range(3):
        rows = slice(c * radii, (c + 1) * radii)
        u = speeds[c]
        total = deposit[:, c * columns : (c + 1) * columns]
        for face, beside in zip(faces, around(c, u, below_u[rows, :], above_u[rows, :])):
            total = total + face * (beside - u)
        star = u + time_step * total
        ustar[rows, :] = star
        stars.append(star)
    row = iota((radii, columns), 0)
    flux = jnp.where(row < radii - 1, (radius + 0.5) * 0.5 * (stars[1] + shifted(stars[1], -1)), 0.0)
    inverse = 1.0 / radius
    outward = (shifted(flux, 1) - flux) * inverse
    turning = stars[2] * (inverse * (-0.5 / step_angle))
    high, low = [p.astype(bf16) for p in pieces(jnp.concatenate([outward, turning], 1), 2)]
    fetch.wait()
    wide = table.shape[1] // 2
    contract = ((1,), (0,))
    modes = dot(high, table[:, :wide], contract) + (
        dot(high, table[:, wide:], contract) + dot(low, table[:, :wide], contract)
    )
    for hop in range(wide // columns):
        outgoing[hop] = modes[:, hop * columns : (hop + 1) * columns]


def solve_kernel(own, one, two, three, tables, out, table, sem):
    me = lax.axis_index("pa")
    count = table.shape[0]
    fetches = [pltpu.make_async_copy(tables.at[me, k], table.at[k], sem.at[k]) for k in range(count)]
    for fetch in fetches:
        fetch.start()
    x = (own[...] + one[...]) + (two[...] + three[...])
    radii, columns = x.shape
    radius = iota((radii, columns), 0).astype(f32) + (NR + 0.5)
    total = sum(NR + i + 0.5 for i in range(NR))
    mean = jnp.sum(radius * x, axis=0, keepdims=True) * (1.0 / total)
    constant = (lax.broadcasted_iota(jnp.int32, (1, columns), 1) == 0) & (me == 0)
    x = x - jnp.where(constant, mean, 0.0)
    stride, k = 1, 0
    while stride < radii:
        fetches[k].wait()
        fetches[k + 1].wait()
        x = x - table[k] * shifted(x, stride) - table[k + 1] * shifted(x, -stride)
        stride *= 2
        k += 2
    fetches[k].wait()
    out[...] = x * table[k]


def project_kernel(own, one, two, three, ustar, tables, out, table, sem):
    me = lax.axis_index("pa")
    fetch = pltpu.make_async_copy(tables.at[me], table, sem)
    fetch.start()
    radii, columns = own.shape
    row = iota((radii, columns), 0)

    def gradient(x):
        above = jnp.where(row == radii - 1, x, pltpu.roll(x, radii - 1, 0))
        below = jnp.where(row == 0, x, pltpu.roll(x, 1, 0))
        return above - below

    values = [r[...] for r in (own, one, two, three)]
    slopes = [gradient(x) for x in values]
    contract = ((1,), (0,))

    def product(parts, at):
        high, low = [p.astype(bf16) for p in pieces(jnp.concatenate(parts, 1), 2)]
        table_high = table[:, at : at + columns]
        table_low = table[:, at + columns : at + 2 * columns]
        return dot(high, table_high, contract) + (dot(high, table_low, contract) + dot(low, table_high, contract))

    fetch.wait()
    out[:radii, :] = ustar[:radii, :]
    out[radii : 2 * radii, :] = ustar[radii : 2 * radii, :] - product(slopes, 0)
    radius = row.astype(f32) + (NR + 0.5)
    out[2 * radii :, :] = ustar[2 * radii :, :] - product(values, 2 * columns) * (0.5 / step_angle / radius)


def place_kernel(capacity, slabs, moved, out):
    rows = slabs * capacity
    width = 768
    split = jnp.concatenate([p.astype(bf16) for p in pieces(moved[...], 3)], 1)
    for start in range(0, rows, width):
        place = start + iota((slabs, width), 1)
        hot = (place // capacity == iota((slabs, width), 0)).astype(bf16)
        spread = dot(split, jnp.concatenate([hot, hot, hot], 0), ((1,), (0,)))
        match = (start + iota((capacity, width), 1)) % capacity == iota((capacity, width), 0)
        for f in range(FEATURES):
            block = spread[f * capacity : (f + 1) * capacity]
            out[f : f + 1, start : start + width] = jnp.sum(jnp.where(match, block, 0.0), axis=0, keepdims=True)


def shape(*dims):
    return jax.ShapeDtypeStruct(dims, f32)


def params(mib):
    return pltpu.CompilerParams(vmem_limit_bytes=mib * 1024 * 1024)


def body(velocity, viscosity, parcels, dest_rank, dest_cell, counts):
    slabs = lax.axis_size("gz")
    ring = lax.axis_size("pa")
    planes, radii, columns = viscosity.shape
    block = parcels.shape[0]
    capacity = 3 * block // slabs
    lines = -(-(FEATURES + 2) * capacity // LANES)
    vmem = pl.BlockSpec(memory_space=pltpu.VMEM)
    smem = pl.BlockSpec(memory_space=pltpu.SMEM)
    anywhere = pl.BlockSpec(memory_space=pl.ANY)
    upward = [(i, i + 1) for i in range(slabs - 1)]
    downward = [(i + 1, i) for i in range(slabs - 1)]
    u = velocity.reshape(3 * radii, columns)
    nu = viscosity.reshape(radii, columns)
    below_u = lax.ppermute(u, "gz", upward)
    above_u = lax.ppermute(u, "gz", downward)
    below_n = lax.ppermute(nu, "gz", upward)
    above_n = lax.ppermute(nu, "gz", downward)

    edge_rows = 8
    features = FEATURES * capacity
    send, first, last = pl.pallas_call(
        functools.partial(pack_kernel, capacity, slabs),
        out_shape=(shape(slabs * lines, LANES), shape(edge_rows, LANES), shape(edge_rows, LANES)),
        in_specs=[smem] + [vmem] * 5,
        out_specs=(vmem,) * 3,
        scratch_shapes=[pltpu.VMEM((3 * features + 2 * capacity, block), bf16), pltpu.VMEM((slabs, block), bf16)],
        compiler_params=params(32),
        name="pack",
    )(counts, parcels.T, dest_rank.reshape(1, block), dest_cell.reshape(1, block), u, nu)

    def turn(x, hop):
        return lax.ppermute(x, "pa", [(i, (i + hop) % ring) for i in range(ring)])

    left = turn(last, 1)
    right = turn(first, ring - 1)
    received = lax.all_to_all(
        send.reshape(slabs, lines, LANES), "gz", split_axis=0, concat_axis=0, tiled=True
    ).reshape(slabs * lines, LANES)

    forward = jnp.asarray(forward_tables(ring, columns))
    ustar, outgoing, moved = pl.pallas_call(
        functools.partial(momentum_kernel, capacity, slabs),
        out_shape=(shape(3 * radii, columns), shape(ring, radii, columns), shape(features, slabs)),
        in_specs=[vmem] * 9 + [anywhere],
        out_specs=(vmem,) * 3,
        scratch_shapes=[
            pltpu.VMEM(forward.shape[1:], bf16),
            pltpu.VMEM((radii, capacity * slabs), bf16),
            pltpu.VMEM((3, capacity, slabs), f32),
            pltpu.VMEM((3 * columns, capacity * slabs), bf16),
            pltpu.SemaphoreType.DMA,
        ],
        compiler_params=params(40),
        name="momentum",
    )(received, u, nu, below_u, above_u, below_n, above_n, left, right, forward)

    parts = [outgoing[0]] + [turn(outgoing[hop], hop) for hop in range(1, ring)]
    factors = jnp.asarray(reduction_tables(ring, columns))
    potential = pl.pallas_call(
        solve_kernel,
        out_shape=shape(radii, columns),
        in_specs=[vmem] * 4 + [anywhere],
        out_specs=vmem,
        scratch_shapes=[pltpu.VMEM(factors.shape[1:], f32), pltpu.SemaphoreType.DMA((factors.shape[1],))],
        compiler_params=params(24),
        name="solve",
    )(*parts, factors)

    gathered = [potential] + [turn(potential, hop) for hop in range(1, ring)]
    parcels_out = pl.pallas_call(
        functools.partial(place_kernel, capacity, slabs),
        out_shape=shape(FEATURES, slabs * capacity),
        in_specs=[vmem],
        out_specs=vmem,
        compiler_params=params(32),
        name="place",
    )(moved)
    backward = jnp.asarray(inverse_tables(ring, columns))
    velocity_out = pl.pallas_call(
        project_kernel,
        out_shape=shape(3 * radii, columns),
        in_specs=[vmem] * 5 + [anywhere],
        out_specs=vmem,
        scratch_shapes=[pltpu.VMEM(backward.shape[1:], bf16), pltpu.SemaphoreType.DMA],
        compiler_params=params(24),
        name="project",
    )(*gathered, ustar, backward)
    return velocity_out.reshape(velocity.shape), parcels_out.T


def solution(mesh):
    in_specs = (
        P(None, "gz", None, "pa"),
        P("gz", None, "pa"),
        P(("gz", "pa"), None),
        P(("gz", "pa"), None),
        P(("gz", "pa")),
        P(("gz", "pa")),
    )
    out_specs = (P(None, "gz", None, "pa"), P(("gz", "pa"), None))
    return jax.shard_map(body, mesh=mesh, in_specs=in_specs, out_specs=out_specs, check_vma=False)
```

```python
import functools
import math

import jax
import jax.numpy as jnp
import numpy as np
from jax import lax
from jax.experimental import pallas as pl
from jax.experimental.pallas import tpu as pltpu
from jax.sharding import PartitionSpec as P

NR = 192
NTH = 512
time_step = 0.1
shift_plane = 0.0001
step_angle = 2.0 * math.pi / NTH
LANES = 128
FEATURES = 16
SUBLANES = 8
EDGE_ROWS = 12
f32 = jnp.float32
bf16 = jnp.bfloat16


def cas(numbers):
    phase = 2.0 * np.pi / NTH * (numbers % NTH)
    return np.cos(phase) + np.sin(phase)


def paired_modes():
    half = NTH // 2
    return np.concatenate([np.arange(half), [half], NTH - np.arange(1, half)])


@functools.cache
def transform_table(ring, columns):
    modes = paired_modes()[None, :]
    plain = cas(np.arange(NTH)[:, None] * modes)
    last = np.arange(ring)[:, None] * columns + columns - 1

    def wave(offset):
        return cas((last + offset) * modes)

    faces = np.zeros((LANES, NTH))
    faces[ring : 2 * ring] = wave(0) - wave(1)
    faces[2 * ring : 3 * ring] = wave(-1) - wave(1) - wave(0) + wave(2)
    faces[8 * ring : 9 * ring] = wave(0)
    faces[9 * ring : 10 * ring] = wave(1)
    table = np.concatenate([plain, faces], 0)
    high = table.astype(jnp.bfloat16)
    low = (table - high.astype(np.float64)).astype(jnp.bfloat16)
    return np.concatenate([high, low], 1)


@functools.cache
def solve_tables():
    radius = NR + np.arange(NR) + 0.5
    arc = 1.0 / (radius * step_angle) ** 2
    up = (radius + 0.5) / radius
    down = (radius - 0.5) / radius
    up[-1] = 0.0
    down[0] = 0.0
    spectrum = 2.0 - 2.0 * np.cos(step_angle * paired_modes())
    diagonal = shift_plane + arc[:, None] * spectrum[None, :] + up[:, None] + down[:, None]
    lower = np.broadcast_to(-down[:, None], diagonal.shape)
    upper = np.broadcast_to(-up[:, None], diagonal.shape)

    def moved(x, by, fill):
        filled = np.full((abs(by),) + x.shape[1:], fill)
        return np.concatenate([filled, x[:-by]], 0) if by > 0 else np.concatenate([x[-by:], filled], 0)

    tables, stride = [], 1
    while stride < SUBLANES:
        low = lower / moved(diagonal, stride, 1.0)
        high = upper / moved(diagonal, -stride, 1.0)
        diagonal = diagonal - low * moved(upper, stride, 0.0) - high * moved(lower, -stride, 0.0)
        lower = -low * moved(lower, stride, 0.0)
        upper = -high * moved(upper, -stride, 0.0)
        tables += [low, high]
        stride *= 2
    multiplier = np.zeros_like(diagonal)
    pivot = diagonal.copy()
    for i in range(SUBLANES, NR):
        multiplier[i] = lower[i] / pivot[i - SUBLANES]
        pivot[i] = diagonal[i] - multiplier[i] * upper[i - SUBLANES]
    tables += [multiplier, 1.0 / pivot, upper / pivot]
    return np.ascontiguousarray(np.stack(tables)[:, :, : 3 * NTH // 4]).astype(np.float32)


@functools.cache
def sine_row():
    row = 2.0 * np.sin(step_angle * np.arange(NTH // 2))
    return np.broadcast_to(row, (SUBLANES, NTH // 2)).astype(np.float32)


def pieces(x, count):
    out = []
    for _ in range(count):
        part = x.astype(bf16).astype(f32)
        out.append(part)
        x = x - part
    return out


def dot(a, b, contract=((1,), (0,))):
    return lax.dot_general(a, b, (contract, ((), ())), preferred_element_type=f32)


def iota(shape, dim):
    return lax.broadcasted_iota(jnp.int32, shape, dim)


def shifted(x, by):
    length = x.shape[0]
    rolled = pltpu.roll(x, by % length, 0)
    row = iota(x.shape, 0)
    return jnp.where(row >= by if by > 0 else row < length + by, rolled, 0.0)


def pack_kernel(
    capacity, slabs, counts_in, parcels_in, target_in, cell_in, velocity_in, viscosity_in, send, fields,
    counts, parcels, target, cell, spread, hot, sems,
):
    radii3 = velocity_in.shape[0]
    copies = [
        pltpu.make_async_copy(source, target_ref, sems.at[k])
        for k, (source, target_ref) in enumerate(
            (
                (counts_in, counts),
                (target_in, target),
                (parcels_in, parcels),
                (cell_in, cell),
                (velocity_in, fields.at[:radii3]),
                (viscosity_in, fields.at[radii3:]),
            )
        )
    ]
    for copy in copies:
        copy.start()
    rows = parcels.shape[1]
    width = 256
    earlier = (iota((width, width), 0) < iota((width, width), 1)).astype(bf16)
    ones = jnp.ones((width, width), bf16)
    features = FEATURES * capacity
    total = features + 2 * capacity
    copies[0].wait()
    copies[1].wait()
    live = iota((1, rows), 1) < counts[0]
    wanted = jnp.where(live, target[...], -1)
    copies[2].wait()
    copies[3].wait()
    cells = cell[...]
    line = (cells // LANES + 1).astype(f32)
    column = (cells % LANES).astype(f32)
    passed = None
    for block in range(rows // width):
        here = slice(block * width, (block + 1) * width)
        mine = iota((slabs, width), 0) == wanted[:, here]
        mark = mine.astype(f32)
        before = dot(mark.astype(bf16), earlier)
        if passed is not None:
            before = before + dot(passed.astype(bf16), ones)
        passed = mark if passed is None else passed + mark
        slot = jnp.sum(mark * before, axis=0, keepdims=True).astype(jnp.int32)
        chosen = iota((capacity, width), 0) == slot
        hot[:, here] = mark.astype(bf16)
        split = pieces(parcels[:, here], 3)

        def placed(row):
            return jnp.where(chosen, row, 0.0)

        for k, part in enumerate(split):
            base = 0 if k == 0 else total + (k - 1) * features
            for f in range(0, FEATURES, 2):
                pair = jnp.concatenate([placed(part[f : f + 1]), placed(part[f + 1 : f + 2])], 0)
                spread[base + f * capacity : base + (f + 2) * capacity, here] = pair.astype(bf16)
        pair = jnp.concatenate([placed(line[:, here]), placed(column[:, here])], 0)
        spread[features:total, here] = pair.astype(bf16)
    out = dot(spread[...], hot[...], ((1,), (1,)))
    values = out[:features] + (out[total : total + features] + out[total + features :])
    filler = jnp.zeros((send.shape[0] // slabs * LANES - total, slabs), f32)
    whole = jnp.concatenate([values, out[features:total], filler], 0)
    lines = send.shape[0] // slabs
    for c in range(lines):
        send[pl.ds(c, slabs, stride=lines), :] = whole[c * LANES : (c + 1) * LANES].T
    copies[4].wait()
    copies[5].wait()


def stencil_kernel(fields, near, far, partial, across, edges):
    radii = fields.shape[0] // 4
    columns = fields.shape[1]
    radius = iota((radii, columns), 0).astype(f32) + (NR + 0.5)
    arc = 1.0 / (radius * step_angle) ** 2
    lane = iota((radii, columns), 1)
    own = [fields[c * radii : (c + 1) * radii, :] for c in range(4)]

    def around(c):
        x = own[c]
        return (
            near[c * radii : (c + 1) * radii, :],
            far[c * radii : (c + 1) * radii, :],
            shifted(x, -1),
            shifted(x, 1),
            pltpu.roll(x, columns - 1, 1),
            pltpu.roll(x, 1, 1),
        )

    weights = (
        0.5,
        0.5,
        0.5 * (radius + 0.5) / radius,
        0.5 * (radius - 0.5) / radius,
        jnp.where(lane == columns - 1, 0.0, 0.5 * arc),
        jnp.where(lane == 0, 0.0, 0.5 * arc),
    )
    faces = [w * (own[3] + n) for w, n in zip(weights, around(3))]
    for c in range(3):
        u = own[c]
        total = jnp.zeros_like(u)
        for face, beside in zip(faces, around(c)):
            total = total + face * (beside - u)
        partial[c * radii : (c + 1) * radii, :] = u + time_step * total
    edges[...] = jnp.zeros_like(edges)
    for c in range(4):
        put_edges(edges, own[c], c, 4 + c)
        if c < 3:
            across[c * columns : (c + 1) * columns, :] = own[c].T


def put_edges(edges, x, first, last):
    turned = x.T
    for part in range(2):
        piece = turned[:, part * LANES : min((part + 1) * LANES, x.shape[0])]
        width = piece.shape[1]
        edges[part * EDGE_ROWS + first : part * EDGE_ROWS + first + 1, :width] = piece[:1]
        edges[part * EDGE_ROWS + last : part * EDGE_ROWS + last + 1, :width] = piece[LANES - 1 :]


def momentum_kernel(
    capacity, slabs, received, partial, across, edges_in, ustar, payload, moved, line_hot, pulled, pushed, edges
):
    lines = received.shape[0] // slabs
    radii = partial.shape[0] // 3
    columns = partial.shape[1]
    turned = jnp.concatenate([received[pl.ds(c, slabs, stride=lines), :].T for c in range(lines)], 0)
    features = FEATURES * capacity
    line_of = turned[features : features + capacity].astype(jnp.int32) - 1
    column_of = turned[features + capacity : features + 2 * capacity].astype(jnp.int32)
    halves = jnp.concatenate([p.astype(bf16) for p in pieces(across[...], 2)], 1)
    group = 2
    for j in range(0, capacity, group):
        here = slice(j * LANES, (j + group) * LANES)
        lane_line = jnp.concatenate([line_of[s : s + 1] for s in range(j, j + group)], 1)
        lane_column = jnp.concatenate([column_of[s : s + 1] for s in range(j, j + group)], 1)
        hot = (iota((radii, group * LANES), 0) == lane_line).astype(bf16)
        line_hot[:, here] = hot
        picked = dot(halves, jnp.concatenate([hot, hot], 0))
        match = iota((columns, group * LANES), 0) == lane_column
        for c in range(3):
            got = jnp.sum(jnp.where(match, picked[c * columns : (c + 1) * columns], 0.0), axis=0, keepdims=True)
            for s in range(group):
                pulled[c, j + s : j + s + 1, :] = got[:, s * LANES : (s + 1) * LANES]
    fluid = [pulled[c] for c in range(3)]
    drag = [jnp.zeros_like(fluid[0]) for _ in range(3)]
    for k in range(4):
        rate = turned[(4 * k + 3) * capacity : (4 * k + 4) * capacity]
        weight = time_step * rate
        scale = 1.0 / (1.0 + weight)
        moved[(4 * k + 3) * capacity : (4 * k + 4) * capacity, :] = rate
        for c in range(3):
            at = (4 * k + c) * capacity
            after = (turned[at : at + capacity] + weight * fluid[c]) * scale
            moved[at : at + capacity, :] = after
            drag[c] = drag[c] + rate * (after - fluid[c])
    drag = [d.astype(bf16).astype(f32) for d in drag]
    for j in range(capacity):
        match = iota((columns, LANES), 0) == column_of[j : j + 1]
        for c in range(3):
            pushed[c * columns : (c + 1) * columns, j * LANES : (j + 1) * LANES] = jnp.where(
                match, drag[c][j : j + 1], 0.0
            ).astype(bf16)
    deposit = dot(line_hot[...], pushed[...], ((1,), (1,)))
    stars = []
    for c in range(3):
        rows = slice(c * radii, (c + 1) * radii)
        star = partial[rows, :] + time_step * deposit[:, c * columns : (c + 1) * columns]
        ustar[rows, :] = star
        stars.append(star)
    row = iota((radii, columns), 0)
    lane = iota((radii, columns), 1)
    radius = row.astype(f32) + (NR + 0.5)
    flux = jnp.where(row < radii - 1, (radius + 0.5) * 0.5 * (stars[1] + shifted(stars[1], -1)), 0.0)
    ahead = jnp.where(lane == columns - 1, 0.0, pltpu.roll(stars[2], columns - 1, 1))
    behind = jnp.where(lane == 0, 0.0, pltpu.roll(stars[2], 1, 1))
    source = (shifted(flux, 1) - flux - (0.5 / step_angle) * (ahead - behind)) / radius
    edges[...] = edges_in[...]
    put_edges(edges, stars[2], 8, 9)
    for q in range(payload.shape[0]):
        payload[q, :radii, :] = source
        payload[q, radii:, :] = edges[...]


def project_kernel(gathered, ustar, transform_in, solve_in, sines_in, out, transform, solve, sines, state, sems):
    me = lax.axis_index("pa")
    fetches = [pltpu.make_async_copy(transform_in, transform, sems.at[0])]
    fetches += [pltpu.make_async_copy(solve_in.at[k], solve.at[k], sems.at[1 + k]) for k in range(solve.shape[0])]
    fetches.append(pltpu.make_async_copy(sines_in, sines, sems.at[1 + solve.shape[0]]))
    for fetch in fetches:
        fetch.start()
    ring = gathered.shape[0]
    radii = out.shape[0] // 3
    columns = out.shape[1]

    def turned(part):
        base = radii + part * EDGE_ROWS
        rows = []
        for c in range(10):
            for q in range(ring):
                source = (q + 1) % ring if c < 4 or c == 8 else q
                rows.append(gathered[source, base + c : base + c + 1, :])
        rows.append(jnp.zeros((LANES - len(rows), LANES), f32))
        return jnp.concatenate(rows, 0).T

    sides = jnp.concatenate([turned(0), turned(1)[: radii - LANES]], 0)
    row = iota((radii, LANES), 0)
    lane = iota((radii, LANES), 1)
    radius = row.astype(f32) + (NR + 0.5)
    inverse = 1.0 / radius

    def lanes_from(x, by):
        return pltpu.roll(x, LANES - by, 1)

    other = lanes_from(sides, 4 * ring)
    both = sides + other
    face = jnp.where(
        lane < ring, lanes_from(both, 3 * ring), jnp.where(lane < 2 * ring, lanes_from(both, 2 * ring), lanes_from(both, ring))
    )
    arc = inverse * inverse * (0.5 * time_step / step_angle**2)
    crossing = jnp.where(lane < 3 * ring, arc * face * (sides - other), 0.0)
    flux = jnp.where(row < radii - 1, (radius + 0.5) * 0.5 * (crossing + shifted(crossing, -1)), 0.0)
    outward = (shifted(flux, 1) - flux) * inverse
    turning = inverse * (0.5 / step_angle)
    coefficients = jnp.where(
        lane < 2 * ring,
        outward,
        jnp.where(lane < 3 * ring, -crossing * turning, jnp.where(lane < 9 * ring, -sides * turning, sides * turning)),
    )
    used = ((lane >= ring) & (lane < 3 * ring)) | ((lane >= 8 * ring) & (lane < 10 * ring))
    coefficients = jnp.where(used, coefficients, 0.0)

    width = 3 * columns
    wide_row = iota((LANES, width), 0)
    wide_lane = iota((LANES, width), 1)
    before = lax.rem(me + ring - 1, ring)
    inside = wide_lane % columns
    at = wide_lane // columns * ring
    pick = jnp.where((inside == columns - 1) & (wide_row == at + me), 1.0, 0.0) - jnp.where(
        (inside == 0) & (wide_row == at + before), 1.0, 0.0
    )
    pick = pick.astype(bf16)
    crossing_parts = [p.astype(bf16) for p in pieces(crossing, 2)]
    delta = dot(crossing_parts[0], pick) + dot(crossing_parts[1], pick)

    values = jnp.concatenate([gathered[q, :radii, :] for q in range(ring)] + [coefficients], 1)
    high, low = [p.astype(bf16) for p in pieces(values, 2)]
    fetches[0].wait()
    table_high = transform[:, :NTH]
    table_low = transform[:, NTH:]
    modes = dot(high, table_high) + (dot(high, table_low) + dot(low, table_high))

    total = sum(NR + i + 0.5 for i in range(NR))
    blocks = [modes[:, b * LANES : (b + 1) * LANES] for b in range(ring)]
    mean = jnp.sum(radius * blocks[0], axis=0, keepdims=True) * (1.0 / total)
    blocks[0] = blocks[0] - jnp.where(iota((1, LANES), 1) == 0, mean, 0.0)
    held = (0, 1, 2, 1)
    for fetch in fetches[1:7]:
        fetch.wait()
    for b in range(ring):
        x = blocks[b]
        cols = slice(held[b] * LANES, (held[b] + 1) * LANES)
        stride, k = 1, 0
        while stride < SUBLANES:
            x = (
                x
                - solve[k, :, cols] * pltpu.roll(x, stride, 0)
                - solve[k + 1, :, cols] * pltpu.roll(x, radii - stride, 0)
            )
            stride *= 2
            k += 2
        state[:, b * LANES : (b + 1) * LANES] = x
    for fetch in fetches[7:]:
        fetch.wait()

    def factors(k, rows):
        return jnp.concatenate([solve[k, rows, : 3 * LANES], solve[k, rows, LANES : 2 * LANES]], 1)

    steps = radii // SUBLANES
    y = state[:SUBLANES, :]
    for v in range(1, steps):
        rows = slice(v * SUBLANES, (v + 1) * SUBLANES)
        y = state[rows, :] - factors(6, rows) * y
        state[rows, :] = y
    x = y * factors(7, slice((steps - 1) * SUBLANES, steps * SUBLANES))
    state[(steps - 1) * SUBLANES :, :] = x
    for v in range(steps - 2, -1, -1):
        rows = slice(v * SUBLANES, (v + 1) * SUBLANES)
        x = state[rows, :] * factors(7, rows) - factors(8, rows) * x
        state[rows, :] = x

    potential = [state[:, b * LANES : (b + 1) * LANES] for b in range(ring)]

    def gradient(x):
        above = jnp.where(row == radii - 1, x, pltpu.roll(x, radii - 1, 0))
        below = jnp.where(row == 0, x, pltpu.roll(x, 1, 0))
        return above - below

    half = ring // 2
    sine = [sines[:1, b * LANES : (b + 1) * LANES] for b in range(half)]
    turns = [-sine[b] * potential[b + half] for b in range(half)] + [sine[b] * potential[b] for b in range(half)]
    both = jnp.concatenate(
        [jnp.concatenate([gradient(x) for x in potential], 1), jnp.concatenate(turns, 1)], 0
    )
    high, low = [p.astype(bf16) for p in pieces(both, 2)]
    mine = pl.ds(pl.multiple_of(me * columns, columns), columns)
    own_high = transform[mine, :NTH]
    own_low = transform[mine, NTH:]
    across = ((1,), (1,))
    result = dot(high, own_high, across) + (dot(high, own_low, across) + dot(low, own_high, across))
    out[:radii, :] = ustar[:radii, :] + delta[:, :columns]
    out[radii : 2 * radii, :] = ustar[radii : 2 * radii, :] + delta[:, columns : 2 * columns] - result[:radii] * (0.5 / NTH)
    out[2 * radii :, :] = ustar[2 * radii :, :] + delta[:, 2 * columns :] - result[radii:] * (turning * (1.0 / NTH))


def place_kernel(capacity, slabs, moved, out):
    rows = slabs * capacity
    width = 768
    split = jnp.concatenate([p.astype(bf16) for p in pieces(moved[...], 3)], 1)
    for start in range(0, rows, width):
        place = start + iota((slabs, width), 1)
        hot = (place // capacity == iota((slabs, width), 0)).astype(bf16)
        spread = dot(split, jnp.concatenate([hot, hot, hot], 0))
        match = (start + iota((capacity, width), 1)) % capacity == iota((capacity, width), 0)
        for f in range(FEATURES):
            block = spread[f * capacity : (f + 1) * capacity]
            out[f : f + 1, start : start + width] = jnp.sum(jnp.where(match, block, 0.0), axis=0, keepdims=True)


def shape(*dims):
    return jax.ShapeDtypeStruct(dims, f32)


def params(mib):
    return pltpu.CompilerParams(vmem_limit_bytes=mib * 1024 * 1024)


def cost(microseconds):
    return pl.CostEstimate(flops=0, bytes_accessed=int(microseconds * 3.0e6), transcendentals=0)


def body(velocity, viscosity, parcels, dest_rank, dest_cell, counts):
    slabs = lax.axis_size("gz")
    ring = lax.axis_size("pa")
    planes, radii, columns = viscosity.shape
    block = parcels.shape[0]
    capacity = 3 * block // slabs
    lines = -(-(FEATURES + 2) * capacity // LANES)
    vmem = pl.BlockSpec(memory_space=pltpu.VMEM)
    hbm = pl.BlockSpec(memory_space=pltpu.HBM)
    u = velocity.reshape(3 * radii, columns)
    nu = viscosity.reshape(radii, columns)
    features = FEATURES * capacity
    send, fields = pl.pallas_call(
        functools.partial(pack_kernel, capacity, slabs),
        out_shape=(shape(slabs * lines, LANES), shape(4 * radii, columns)),
        in_specs=[hbm] * 6,
        out_specs=(vmem,) * 2,
        scratch_shapes=[
            pltpu.SMEM((1,), jnp.int32),
            pltpu.VMEM((FEATURES, block), f32),
            pltpu.VMEM((1, block), jnp.int32),
            pltpu.VMEM((1, block), jnp.int32),
            pltpu.VMEM((3 * features + 2 * capacity, block), bf16),
            pltpu.VMEM((slabs, block), bf16),
            pltpu.SemaphoreType.DMA((6,)),
        ],
        compiler_params=params(32),
        cost_estimate=cost(3),
        name="pack",
    )(counts, parcels.T, dest_rank.reshape(1, block), dest_cell.reshape(1, block), u, nu)
    received = lax.all_to_all(
        send.reshape(slabs, lines, LANES), "gz", split_axis=0, concat_axis=0, tiled=True
    ).reshape(slabs * lines, LANES)

    near = lax.ppermute(fields, "gz", [(i, i ^ 1) for i in range(slabs)])
    pairs = [(i, i + 1) for i in range(1, slabs - 1, 2)]
    far = lax.ppermute(fields, "gz", pairs + [(j, i) for i, j in pairs])
    partial, across, edges = pl.pallas_call(
        stencil_kernel,
        out_shape=(shape(3 * radii, columns), shape(3 * columns, radii), shape(2 * EDGE_ROWS, LANES)),
        in_specs=[vmem] * 3,
        out_specs=(vmem,) * 3,
        compiler_params=params(16),
        cost_estimate=cost(2),
        name="stencil",
    )(fields, near, far)

    ustar, payload, moved = pl.pallas_call(
        functools.partial(momentum_kernel, capacity, slabs),
        out_shape=(
            shape(3 * radii, columns),
            shape(ring, radii + 2 * EDGE_ROWS, columns),
            shape(features, slabs),
        ),
        in_specs=[vmem] * 4,
        out_specs=(vmem,) * 3,
        scratch_shapes=[
            pltpu.VMEM((radii, capacity * slabs), bf16),
            pltpu.VMEM((3, capacity, slabs), f32),
            pltpu.VMEM((3 * columns, capacity * slabs), bf16),
            pltpu.VMEM((2 * EDGE_ROWS, LANES), f32),
        ],
        compiler_params=params(32),
        cost_estimate=cost(4),
        name="momentum",
    )(received, partial, across, edges)

    gathered = lax.all_to_all(payload, "pa", split_axis=0, concat_axis=0, tiled=True)
    parcels_out = pl.pallas_call(
        functools.partial(place_kernel, capacity, slabs),
        out_shape=shape(FEATURES, slabs * capacity),
        in_specs=[vmem],
        out_specs=vmem,
        compiler_params=params(32),
        cost_estimate=cost(3),
        name="place",
    )(moved)
    transform = jnp.asarray(transform_table(ring, columns))
    factors = jnp.asarray(solve_tables())
    sines = jnp.asarray(sine_row())
    velocity_out = pl.pallas_call(
        project_kernel,
        out_shape=shape(3 * radii, columns),
        in_specs=[vmem] * 2 + [hbm] * 3,
        out_specs=vmem,
        scratch_shapes=[
            pltpu.VMEM(transform.shape, bf16),
            pltpu.VMEM(factors.shape, f32),
            pltpu.VMEM(sines.shape, f32),
            pltpu.VMEM((radii, NTH), f32),
            pltpu.SemaphoreType.DMA((factors.shape[0] + 2,)),
        ],
        compiler_params=params(32),
        cost_estimate=cost(5),
        name="project",
    )(gathered, ustar, transform, factors, sines)
    return velocity_out.reshape(velocity.shape), parcels_out.T


def solution(mesh):
    in_specs = (
        P(None, "gz", None, "pa"),
        P("gz", None, "pa"),
        P(("gz", "pa"), None),
        P(("gz", "pa"), None),
        P(("gz", "pa")),
        P(("gz", "pa")),
    )
    out_specs = (P(None, "gz", None, "pa"), P(("gz", "pa"), None))
    return jax.shard_map(body, mesh=mesh, in_specs=in_specs, out_specs=out_specs, check_vma=False)
```

```python
import functools
import math

import jax
import jax.numpy as jnp
import numpy as np
from jax import lax
from jax.experimental import pallas as pl
from jax.experimental.pallas import tpu as pltpu
from jax.sharding import PartitionSpec as P

NR = 192
NTH = 512
time_step = 0.1
shift_plane = 0.0001
step_angle = 2.0 * math.pi / NTH
LANES = 128
FEATURES = 16
SUBLANES = 8
EDGE_ROWS = 12
f32 = jnp.float32
bf16 = jnp.bfloat16


def cas(numbers):
    phase = 2.0 * np.pi / NTH * (numbers % NTH)
    return np.cos(phase) + np.sin(phase)


def paired_modes():
    half = NTH // 2
    return np.concatenate([np.arange(half), [half], NTH - np.arange(1, half)])


@functools.cache
def transform_table(ring, columns):
    modes = paired_modes()[None, :]
    plain = cas(np.arange(NTH)[:, None] * modes)
    last = np.arange(ring)[:, None] * columns + columns - 1

    def wave(offset):
        return cas((last + offset) * modes)

    faces = np.zeros((LANES, NTH))
    faces[ring : 2 * ring] = wave(0) - wave(1)
    faces[2 * ring : 3 * ring] = wave(-1) - wave(1) - wave(0) + wave(2)
    faces[8 * ring : 9 * ring] = wave(0)
    faces[9 * ring : 10 * ring] = wave(1)
    table = np.concatenate([plain, faces], 0)
    high = table.astype(jnp.bfloat16)
    low = (table - high.astype(np.float64)).astype(jnp.bfloat16)
    return np.concatenate([high, low], 1)


@functools.cache
def solve_tables():
    radius = NR + np.arange(NR) + 0.5
    arc = 1.0 / (radius * step_angle) ** 2
    up = (radius + 0.5) / radius
    down = (radius - 0.5) / radius
    up[-1] = 0.0
    down[0] = 0.0
    spectrum = 2.0 - 2.0 * np.cos(step_angle * paired_modes())
    diagonal = shift_plane + arc[:, None] * spectrum[None, :] + up[:, None] + down[:, None]
    lower = np.broadcast_to(-down[:, None], diagonal.shape)
    upper = np.broadcast_to(-up[:, None], diagonal.shape)

    def moved(x, by, fill):
        filled = np.full((abs(by),) + x.shape[1:], fill)
        return np.concatenate([filled, x[:-by]], 0) if by > 0 else np.concatenate([x[-by:], filled], 0)

    tables, stride = [], 1
    while stride < SUBLANES:
        low = lower / moved(diagonal, stride, 1.0)
        high = upper / moved(diagonal, -stride, 1.0)
        diagonal = diagonal - low * moved(upper, stride, 0.0) - high * moved(lower, -stride, 0.0)
        lower = -low * moved(lower, stride, 0.0)
        upper = -high * moved(upper, -stride, 0.0)
        tables += [low, high]
        stride *= 2
    multiplier = np.zeros_like(diagonal)
    pivot = diagonal.copy()
    for i in range(SUBLANES, NR):
        multiplier[i] = lower[i] / pivot[i - SUBLANES]
        pivot[i] = diagonal[i] - multiplier[i] * upper[i - SUBLANES]
    tables += [multiplier, 1.0 / pivot, upper / pivot]
    return np.ascontiguousarray(np.stack(tables)[:, :, : 3 * NTH // 4]).astype(np.float32)


@functools.cache
def sine_row():
    row = 2.0 * np.sin(step_angle * np.arange(NTH // 2))
    return np.broadcast_to(row, (SUBLANES, NTH // 2)).astype(np.float32)


def pieces(x, count):
    out = []
    for _ in range(count):
        part = x.astype(bf16).astype(f32)
        out.append(part)
        x = x - part
    return out


def dot(a, b, contract=((1,), (0,))):
    return lax.dot_general(a, b, (contract, ((), ())), preferred_element_type=f32)


def iota(shape, dim):
    return lax.broadcasted_iota(jnp.int32, shape, dim)


def shifted(x, by):
    length = x.shape[0]
    rolled = pltpu.roll(x, by % length, 0)
    row = iota(x.shape, 0)
    return jnp.where(row >= by if by > 0 else row < length + by, rolled, 0.0)


def pack_kernel(
    capacity, slabs, counts_in, parcels_in, target_in, cell_in, velocity_in, viscosity_in, send, fields,
    counts, parcels, target, cell, spread, hot, sems,
):
    radii3 = velocity_in.shape[0]
    copies = [
        pltpu.make_async_copy(source, target_ref, sems.at[k])
        for k, (source, target_ref) in enumerate(
            (
                (counts_in, counts),
                (target_in, target),
                (parcels_in, parcels),
                (cell_in, cell),
                (velocity_in, fields.at[:radii3]),
                (viscosity_in, fields.at[radii3:]),
            )
        )
    ]
    for copy in copies:
        copy.start()
    rows = parcels.shape[1]
    width = 256
    earlier = (iota((width, width), 0) < iota((width, width), 1)).astype(bf16)
    ones = jnp.ones((width, width), bf16)
    features = FEATURES * capacity
    total = features + 2 * capacity
    copies[0].wait()
    copies[1].wait()
    live = iota((1, rows), 1) < counts[0]
    wanted = jnp.where(live, target[...], -1)
    copies[2].wait()
    copies[3].wait()
    cells = cell[...]
    line = (cells // LANES + 1).astype(f32)
    column = (cells % LANES).astype(f32)
    passed = None
    for block in range(rows // width):
        here = slice(block * width, (block + 1) * width)
        mine = iota((slabs, width), 0) == wanted[:, here]
        mark = mine.astype(f32)
        before = dot(mark.astype(bf16), earlier)
        if passed is not None:
            before = before + dot(passed.astype(bf16), ones)
        passed = mark if passed is None else passed + mark
        slot = jnp.sum(mark * before, axis=0, keepdims=True).astype(jnp.int32)
        chosen = iota((capacity, width), 0) == slot
        hot[:, here] = mark.astype(bf16)
        split = pieces(parcels[:, here], 3)

        def placed(row):
            return jnp.where(chosen, row, 0.0)

        for k, part in enumerate(split):
            base = 0 if k == 0 else total + (k - 1) * features
            for f in range(0, FEATURES, 2):
                pair = jnp.concatenate([placed(part[f : f + 1]), placed(part[f + 1 : f + 2])], 0)
                spread[base + f * capacity : base + (f + 2) * capacity, here] = pair.astype(bf16)
        pair = jnp.concatenate([placed(line[:, here]), placed(column[:, here])], 0)
        spread[features:total, here] = pair.astype(bf16)
    out = dot(spread[...], hot[...], ((1,), (1,)))
    values = out[:features] + (out[total : total + features] + out[total + features :])
    filler = jnp.zeros((send.shape[0] // slabs * LANES - total, slabs), f32)
    whole = jnp.concatenate([values, out[features:total], filler], 0)
    lines = send.shape[0] // slabs
    for c in range(lines):
        send[pl.ds(c, slabs, stride=lines), :] = whole[c * LANES : (c + 1) * LANES].T
    copies[4].wait()
    copies[5].wait()


def stencil_kernel(fields, near, far, partial, across, edges):
    radii = fields.shape[0] // 4
    columns = fields.shape[1]
    radius = iota((radii, columns), 0).astype(f32) + (NR + 0.5)
    arc = 1.0 / (radius * step_angle) ** 2
    lane = iota((radii, columns), 1)
    own = [fields[c * radii : (c + 1) * radii, :] for c in range(4)]

    def around(c):
        x = own[c]
        return (
            near[c * radii : (c + 1) * radii, :],
            far[c * radii : (c + 1) * radii, :],
            shifted(x, -1),
            shifted(x, 1),
            pltpu.roll(x, columns - 1, 1),
            pltpu.roll(x, 1, 1),
        )

    weights = (
        0.5,
        0.5,
        0.5 * (radius + 0.5) / radius,
        0.5 * (radius - 0.5) / radius,
        jnp.where(lane == columns - 1, 0.0, 0.5 * arc),
        jnp.where(lane == 0, 0.0, 0.5 * arc),
    )
    faces = [w * (own[3] + n) for w, n in zip(weights, around(3))]
    for c in range(3):
        u = own[c]
        total = jnp.zeros_like(u)
        for face, beside in zip(faces, around(c)):
            total = total + face * (beside - u)
        partial[c * radii : (c + 1) * radii, :] = u + time_step * total
    edges[...] = jnp.zeros_like(edges)
    for c in range(4):
        put_edges(edges, own[c], c, 4 + c)
        if c < 3:
            across[c * columns : (c + 1) * columns, :] = own[c].T


def put_edges(edges, x, first, last):
    turned = x.T
    for part in range(2):
        piece = turned[:, part * LANES : min((part + 1) * LANES, x.shape[0])]
        width = piece.shape[1]
        edges[part * EDGE_ROWS + first : part * EDGE_ROWS + first + 1, :width] = piece[:1]
        edges[part * EDGE_ROWS + last : part * EDGE_ROWS + last + 1, :width] = piece[LANES - 1 :]


def momentum_kernel(
    capacity, slabs, received, partial, across, edges_in, ustar, payload, moved, line_hot, pulled, pushed, edges
):
    lines = received.shape[0] // slabs
    radii = partial.shape[0] // 3
    columns = partial.shape[1]
    turned = jnp.concatenate([received[pl.ds(c, slabs, stride=lines), :].T for c in range(lines)], 0)
    features = FEATURES * capacity
    line_of = turned[features : features + capacity].astype(jnp.int32) - 1
    column_of = turned[features + capacity : features + 2 * capacity].astype(jnp.int32)
    halves = jnp.concatenate([p.astype(bf16) for p in pieces(across[...], 2)], 1)
    group = 2
    for j in range(0, capacity, group):
        here = slice(j * LANES, (j + group) * LANES)
        lane_line = jnp.concatenate([line_of[s : s + 1] for s in range(j, j + group)], 1)
        lane_column = jnp.concatenate([column_of[s : s + 1] for s in range(j, j + group)], 1)
        hot = (iota((radii, group * LANES), 0) == lane_line).astype(bf16)
        line_hot[:, here] = hot
        picked = dot(halves, jnp.concatenate([hot, hot], 0))
        match = iota((columns, group * LANES), 0) == lane_column
        for c in range(3):
            got = jnp.sum(jnp.where(match, picked[c * columns : (c + 1) * columns], 0.0), axis=0, keepdims=True)
            for s in range(group):
                pulled[c, j + s : j + s + 1, :] = got[:, s * LANES : (s + 1) * LANES]
    fluid = [pulled[c] for c in range(3)]
    drag = [jnp.zeros_like(fluid[0]) for _ in range(3)]
    for k in range(4):
        rate = turned[(4 * k + 3) * capacity : (4 * k + 4) * capacity]
        weight = time_step * rate
        scale = 1.0 / (1.0 + weight)
        moved[(4 * k + 3) * capacity : (4 * k + 4) * capacity, :] = rate
        for c in range(3):
            at = (4 * k + c) * capacity
            after = (turned[at : at + capacity] + weight * fluid[c]) * scale
            moved[at : at + capacity, :] = after
            drag[c] = drag[c] + rate * (after - fluid[c])
    drag = [d.astype(bf16).astype(f32) for d in drag]
    for j in range(capacity):
        match = iota((columns, LANES), 0) == column_of[j : j + 1]
        for c in range(3):
            pushed[c * columns : (c + 1) * columns, j * LANES : (j + 1) * LANES] = jnp.where(
                match, drag[c][j : j + 1], 0.0
            ).astype(bf16)
    deposit = dot(line_hot[...], pushed[...], ((1,), (1,)))
    stars = []
    for c in range(3):
        rows = slice(c * radii, (c + 1) * radii)
        star = partial[rows, :] + time_step * deposit[:, c * columns : (c + 1) * columns]
        ustar[rows, :] = star
        stars.append(star)
    row = iota((radii, columns), 0)
    lane = iota((radii, columns), 1)
    radius = row.astype(f32) + (NR + 0.5)
    flux = jnp.where(row < radii - 1, (radius + 0.5) * 0.5 * (stars[1] + shifted(stars[1], -1)), 0.0)
    ahead = jnp.where(lane == columns - 1, 0.0, pltpu.roll(stars[2], columns - 1, 1))
    behind = jnp.where(lane == 0, 0.0, pltpu.roll(stars[2], 1, 1))
    source = (shifted(flux, 1) - flux - (0.5 / step_angle) * (ahead - behind)) / radius
    edges[...] = edges_in[...]
    put_edges(edges, stars[2], 8, 9)
    for q in range(payload.shape[0]):
        payload[q, :radii, :] = source
        payload[q, radii:, :] = edges[...]


def project_kernel(gathered, ustar, transform_in, solve_in, sines_in, out, transform, solve, sines, state, sems):
    me = lax.axis_index("pa")
    fetches = [pltpu.make_async_copy(transform_in, transform, sems.at[0])]
    fetches += [pltpu.make_async_copy(solve_in.at[k], solve.at[k], sems.at[1 + k]) for k in range(solve.shape[0])]
    fetches.append(pltpu.make_async_copy(sines_in, sines, sems.at[1 + solve.shape[0]]))
    for fetch in fetches:
        fetch.start()
    ring = gathered.shape[0]
    radii = out.shape[0] // 3
    columns = out.shape[1]

    def turned(part):
        base = radii + part * EDGE_ROWS
        rows = []
        for c in range(10):
            for q in range(ring):
                source = (q + 1) % ring if c < 4 or c == 8 else q
                rows.append(gathered[source, base + c : base + c + 1, :])
        rows.append(jnp.zeros((LANES - len(rows), LANES), f32))
        return jnp.concatenate(rows, 0).T

    sides = jnp.concatenate([turned(0), turned(1)[: radii - LANES]], 0)
    row = iota((radii, LANES), 0)
    lane = iota((radii, LANES), 1)
    radius = row.astype(f32) + (NR + 0.5)
    inverse = 1.0 / radius

    def lanes_from(x, by):
        return pltpu.roll(x, LANES - by, 1)

    other = lanes_from(sides, 4 * ring)
    both = sides + other
    face = jnp.where(
        lane < ring, lanes_from(both, 3 * ring), jnp.where(lane < 2 * ring, lanes_from(both, 2 * ring), lanes_from(both, ring))
    )
    arc = inverse * inverse * (0.5 * time_step / step_angle**2)
    crossing = jnp.where(lane < 3 * ring, arc * face * (sides - other), 0.0)
    flux = jnp.where(row < radii - 1, (radius + 0.5) * 0.5 * (crossing + shifted(crossing, -1)), 0.0)
    outward = (shifted(flux, 1) - flux) * inverse
    turning = inverse * (0.5 / step_angle)
    coefficients = jnp.where(
        lane < 2 * ring,
        outward,
        jnp.where(lane < 3 * ring, -crossing * turning, jnp.where(lane < 9 * ring, -sides * turning, sides * turning)),
    )
    used = ((lane >= ring) & (lane < 3 * ring)) | ((lane >= 8 * ring) & (lane < 10 * ring))
    coefficients = jnp.where(used, coefficients, 0.0)

    width = 3 * columns
    wide_row = iota((LANES, width), 0)
    wide_lane = iota((LANES, width), 1)
    before = lax.rem(me + ring - 1, ring)
    inside = wide_lane % columns
    at = wide_lane // columns * ring
    pick = jnp.where((inside == columns - 1) & (wide_row == at + me), 1.0, 0.0) - jnp.where(
        (inside == 0) & (wide_row == at + before), 1.0, 0.0
    )
    pick = pick.astype(bf16)
    crossing_parts = [p.astype(bf16) for p in pieces(crossing, 2)]
    delta = dot(crossing_parts[0], pick) + dot(crossing_parts[1], pick)

    values = jnp.concatenate([gathered[q, :radii, :] for q in range(ring)] + [coefficients], 1)
    high, low = [p.astype(bf16) for p in pieces(values, 2)]
    fetches[0].wait()
    table_high = transform[:, :NTH]
    table_low = transform[:, NTH:]
    modes = dot(high, table_high) + (dot(high, table_low) + dot(low, table_high))

    total = sum(NR + i + 0.5 for i in range(NR))
    blocks = [modes[:, b * LANES : (b + 1) * LANES] for b in range(ring)]
    mean = jnp.sum(radius * blocks[0], axis=0, keepdims=True) * (1.0 / total)
    blocks[0] = blocks[0] - jnp.where(iota((1, LANES), 1) == 0, mean, 0.0)
    held = (0, 1, 2, 1)
    for fetch in fetches[1:7]:
        fetch.wait()
    for b in range(ring):
        x = blocks[b]
        cols = slice(held[b] * LANES, (held[b] + 1) * LANES)
        stride, k = 1, 0
        while stride < SUBLANES:
            x = (
                x
                - solve[k, :, cols] * pltpu.roll(x, stride, 0)
                - solve[k + 1, :, cols] * pltpu.roll(x, radii - stride, 0)
            )
            stride *= 2
            k += 2
        state[:, b * LANES : (b + 1) * LANES] = x
    for fetch in fetches[7:]:
        fetch.wait()

    def factors(k, rows):
        return jnp.concatenate([solve[k, rows, : 3 * LANES], solve[k, rows, LANES : 2 * LANES]], 1)

    steps = radii // SUBLANES
    y = state[:SUBLANES, :]
    for v in range(1, steps):
        rows = slice(v * SUBLANES, (v + 1) * SUBLANES)
        y = state[rows, :] - factors(6, rows) * y
        state[rows, :] = y
    x = y * factors(7, slice((steps - 1) * SUBLANES, steps * SUBLANES))
    state[(steps - 1) * SUBLANES :, :] = x
    for v in range(steps - 2, -1, -1):
        rows = slice(v * SUBLANES, (v + 1) * SUBLANES)
        x = state[rows, :] * factors(7, rows) - factors(8, rows) * x
        state[rows, :] = x

    potential = [state[:, b * LANES : (b + 1) * LANES] for b in range(ring)]

    def gradient(x):
        above = jnp.where(row == radii - 1, x, pltpu.roll(x, radii - 1, 0))
        below = jnp.where(row == 0, x, pltpu.roll(x, 1, 0))
        return above - below

    half = ring // 2
    sine = [sines[:1, b * LANES : (b + 1) * LANES] for b in range(half)]
    turns = [-sine[b] * potential[b + half] for b in range(half)] + [sine[b] * potential[b] for b in range(half)]
    both = jnp.concatenate(
        [jnp.concatenate([gradient(x) for x in potential], 1), jnp.concatenate(turns, 1)], 0
    )
    high, low = [p.astype(bf16) for p in pieces(both, 2)]
    mine = pl.ds(pl.multiple_of(me * columns, columns), columns)
    own_high = transform[mine, :NTH]
    own_low = transform[mine, NTH:]
    across = ((1,), (1,))
    result = dot(high, own_high, across) + (dot(high, own_low, across) + dot(low, own_high, across))
    out[:radii, :] = ustar[:radii, :] + delta[:, :columns]
    out[radii : 2 * radii, :] = ustar[radii : 2 * radii, :] + delta[:, columns : 2 * columns] - result[:radii] * (0.5 / NTH)
    out[2 * radii :, :] = ustar[2 * radii :, :] + delta[:, 2 * columns :] - result[radii:] * (turning * (1.0 / NTH))


def place_kernel(capacity, slabs, moved, out):
    rows = slabs * capacity
    width = 768
    split = jnp.concatenate([p.astype(bf16) for p in pieces(moved[...], 3)], 1)
    for start in range(0, rows, width):
        place = start + iota((slabs, width), 1)
        hot = (place // capacity == iota((slabs, width), 0)).astype(bf16)
        spread = dot(split, jnp.concatenate([hot, hot, hot], 0))
        match = (start + iota((capacity, width), 1)) % capacity == iota((capacity, width), 0)
        for f in range(FEATURES):
            block = spread[f * capacity : (f + 1) * capacity]
            out[f : f + 1, start : start + width] = jnp.sum(jnp.where(match, block, 0.0), axis=0, keepdims=True)


def shape(*dims):
    return jax.ShapeDtypeStruct(dims, f32)


def params(mib):
    return pltpu.CompilerParams(vmem_limit_bytes=int(mib * 1024 * 1024))


def cost(microseconds):
    return pl.CostEstimate(flops=0, bytes_accessed=int(microseconds * 3.0e6), transcendentals=0)


def body(velocity, viscosity, parcels, dest_rank, dest_cell, counts):
    slabs = lax.axis_size("gz")
    ring = lax.axis_size("pa")
    planes, radii, columns = viscosity.shape
    block = parcels.shape[0]
    capacity = 3 * block // slabs
    lines = -(-(FEATURES + 2) * capacity // LANES)
    vmem = pl.BlockSpec(memory_space=pltpu.VMEM)
    hbm = pl.BlockSpec(memory_space=pltpu.HBM)
    u = velocity.reshape(3 * radii, columns)
    nu = viscosity.reshape(radii, columns)
    features = FEATURES * capacity
    send, fields = pl.pallas_call(
        functools.partial(pack_kernel, capacity, slabs),
        out_shape=(shape(slabs * lines, LANES), shape(4 * radii, columns)),
        in_specs=[hbm] * 6,
        out_specs=(vmem,) * 2,
        scratch_shapes=[
            pltpu.SMEM((1,), jnp.int32),
            pltpu.VMEM((FEATURES, block), f32),
            pltpu.VMEM((1, block), jnp.int32),
            pltpu.VMEM((1, block), jnp.int32),
            pltpu.VMEM((3 * features + 2 * capacity, block), bf16),
            pltpu.VMEM((slabs, block), bf16),
            pltpu.SemaphoreType.DMA((6,)),
        ],
        compiler_params=params(60),
        cost_estimate=cost(3),
        name="pack",
    )(counts, parcels.T, dest_rank.reshape(1, block), dest_cell.reshape(1, block), u, nu)
    received = lax.all_to_all(
        send.reshape(slabs, lines, LANES), "gz", split_axis=0, concat_axis=0, tiled=True
    ).reshape(slabs * lines, LANES)

    near = lax.ppermute(fields, "gz", [(i, i ^ 1) for i in range(slabs)])
    pairs = [(i, i + 1) for i in range(1, slabs - 1, 2)]
    far = lax.ppermute(fields, "gz", pairs + [(j, i) for i, j in pairs])
    partial, across, edges = pl.pallas_call(
        stencil_kernel,
        out_shape=(shape(3 * radii, columns), shape(3 * columns, radii), shape(2 * EDGE_ROWS, LANES)),
        in_specs=[vmem] * 3,
        out_specs=(vmem,) * 3,
        compiler_params=params(16),
        cost_estimate=cost(2),
        name="stencil",
    )(fields, near, far)

    ustar, payload, moved = pl.pallas_call(
        functools.partial(momentum_kernel, capacity, slabs),
        out_shape=(
            shape(3 * radii, columns),
            shape(ring, radii + 2 * EDGE_ROWS, columns),
            shape(features, slabs),
        ),
        in_specs=[vmem] * 4,
        out_specs=(vmem,) * 3,
        scratch_shapes=[
            pltpu.VMEM((radii, capacity * slabs), bf16),
            pltpu.VMEM((3, capacity, slabs), f32),
            pltpu.VMEM((3 * columns, capacity * slabs), bf16),
            pltpu.VMEM((2 * EDGE_ROWS, LANES), f32),
        ],
        compiler_params=params(16),
        cost_estimate=cost(4),
        name="momentum",
    )(received, partial, across, edges)

    gathered = lax.all_to_all(payload, "pa", split_axis=0, concat_axis=0, tiled=True)
    parcels_out = pl.pallas_call(
        functools.partial(place_kernel, capacity, slabs),
        out_shape=shape(FEATURES, slabs * capacity),
        in_specs=[vmem],
        out_specs=vmem,
        compiler_params=params(16),
        cost_estimate=cost(3),
        name="place",
    )(moved)
    transform = jnp.asarray(transform_table(ring, columns))
    factors = jnp.asarray(solve_tables())
    sines = jnp.asarray(sine_row())
    velocity_out = pl.pallas_call(
        project_kernel,
        out_shape=shape(3 * radii, columns),
        in_specs=[vmem] * 2 + [hbm] * 3,
        out_specs=vmem,
        scratch_shapes=[
            pltpu.VMEM(transform.shape, bf16),
            pltpu.VMEM(factors.shape, f32),
            pltpu.VMEM(sines.shape, f32),
            pltpu.VMEM((radii, NTH), f32),
            pltpu.SemaphoreType.DMA((factors.shape[0] + 2,)),
        ],
        compiler_params=params(52),
        cost_estimate=cost(5),
        name="project",
    )(gathered, ustar, transform, factors, sines)
    return velocity_out.reshape(velocity.shape), parcels_out.T


def solution(mesh):
    in_specs = (
        P(None, "gz", None, "pa"),
        P("gz", None, "pa"),
        P(("gz", "pa"), None),
        P(("gz", "pa"), None),
        P(("gz", "pa")),
        P(("gz", "pa")),
    )
    out_specs = (P(None, "gz", None, "pa"), P(("gz", "pa"), None))
    return jax.shard_map(body, mesh=mesh, in_specs=in_specs, out_specs=out_specs, check_vma=False)
```

```python
import functools
import math

import jax
import jax.numpy as jnp
import numpy as np
from jax import lax
from jax.experimental import pallas as pl
from jax.experimental.pallas import tpu as pltpu
from jax.sharding import PartitionSpec as P

NR = 192
NTH = 512
time_step = 0.1
shift_plane = 0.0001
step_angle = 2.0 * math.pi / NTH
LANES = 128
FEATURES = 16
SUBLANES = 8
EDGE_ROWS = 16
CORRECTION_ROWS = 64
f32 = jnp.float32
bf16 = jnp.bfloat16


def cas(numbers):
    phase = 2.0 * np.pi / NTH * (numbers % NTH)
    return np.cos(phase) + np.sin(phase)


def paired_modes():
    half, even, odd = NTH // 2, np.arange(0, NTH // 2, 2), np.arange(1, NTH // 2, 2)
    return np.concatenate([even, [half], NTH - even[1:], odd, NTH - odd])


@functools.cache
def transform_table(ring, columns):
    modes = paired_modes()[None, :]
    plain = cas(np.arange(NTH // 2)[:, None] * modes)
    faces = np.zeros((CORRECTION_ROWS, NTH))
    for q in range(ring):
        last, at = q * columns + columns - 1, q * EDGE_ROWS

        def wave(offset):
            return cas((last + offset) * modes)

        faces[at + 5] = wave(0) - wave(1)
        faces[at + 6] = wave(-1) - wave(1) - wave(0) + wave(2)
        faces[at + 8] = wave(0)
        faces[at + 9] = wave(1)
    table = np.concatenate([plain, faces], 0)
    high = table.astype(jnp.bfloat16)
    low = (table - high.astype(np.float64)).astype(jnp.bfloat16)
    return np.concatenate([high, low], 1)


@functools.cache
def solve_tables():
    radius = NR + np.arange(NR) + 0.5
    arc = 1.0 / (radius * step_angle) ** 2
    up = (radius + 0.5) / radius
    down = (radius - 0.5) / radius
    up[-1] = 0.0
    down[0] = 0.0
    spectrum = 2.0 - 2.0 * np.cos(step_angle * paired_modes())
    diagonal = shift_plane + arc[:, None] * spectrum[None, :] + up[:, None] + down[:, None]
    lower = np.broadcast_to(-down[:, None], diagonal.shape)
    upper = np.broadcast_to(-up[:, None], diagonal.shape)

    def moved(x, by, fill):
        filled = np.full((abs(by),) + x.shape[1:], fill)
        return np.concatenate([filled, x[:-by]], 0) if by > 0 else np.concatenate([x[-by:], filled], 0)

    tables, stride = [], 1
    while stride < SUBLANES:
        low = lower / moved(diagonal, stride, 1.0)
        high = upper / moved(diagonal, -stride, 1.0)
        diagonal = diagonal - low * moved(upper, stride, 0.0) - high * moved(lower, -stride, 0.0)
        lower = -low * moved(lower, stride, 0.0)
        upper = -high * moved(upper, -stride, 0.0)
        tables += [low, high]
        stride *= 2
    multiplier = np.zeros_like(diagonal)
    pivot = diagonal.copy()
    for i in range(SUBLANES, NR):
        multiplier[i] = lower[i] / pivot[i - SUBLANES]
        pivot[i] = diagonal[i] - multiplier[i] * upper[i - SUBLANES]
    tables += [multiplier, 1.0 / pivot, upper / pivot]
    sine = 2.0 * np.sin(step_angle * paired_modes())
    tables.append(np.broadcast_to(sine, (SUBLANES, NTH)))
    return np.concatenate(tables, 0)[:, : 3 * NTH // 4].astype(np.float32)


def pieces(x, count):
    out = []
    for _ in range(count):
        part = x.astype(bf16).astype(f32)
        out.append(part)
        x = x - part
    return out


def dot(a, b, contract=((1,), (0,))):
    return lax.dot_general(a, b, (contract, ((), ())), preferred_element_type=f32)


def iota(shape, dim):
    return lax.broadcasted_iota(jnp.int32, shape, dim)


def shifted(x, by):
    length = x.shape[0]
    rolled = pltpu.roll(x, by % length, 0)
    row = iota(x.shape, 0)
    return jnp.where(row >= by if by > 0 else row < length + by, rolled, 0.0)


def pack_kernel(
    capacity, slabs, counts_in, parcels_in, target_in, cell_in, velocity_in, viscosity_in, send, fields,
    counts, parcels, target, cell, spread, hot, sems,
):
    radii3 = velocity_in.shape[0]
    copies = [
        pltpu.make_async_copy(source, target_ref, sems.at[k])
        for k, (source, target_ref) in enumerate(
            (
                (counts_in, counts),
                (target_in, target),
                (parcels_in, parcels),
                (cell_in, cell),
                (velocity_in, fields.at[:radii3]),
                (viscosity_in, fields.at[radii3:]),
            )
        )
    ]
    for copy in copies:
        copy.start()
    rows = parcels.shape[1]
    width = 256
    earlier = (iota((width, width), 0) < iota((width, width), 1)).astype(bf16)
    ones = jnp.ones((width, width), bf16)
    features = FEATURES * capacity
    total = features + 2 * capacity
    copies[0].wait()
    copies[1].wait()
    live = iota((1, rows), 1) < counts[0]
    wanted = jnp.where(live, target[...], -1)
    copies[2].wait()
    copies[3].wait()
    cells = cell[...]
    line = (cells // LANES + 1).astype(f32)
    column = (cells % LANES).astype(f32)
    passed = None
    for block in range(rows // width):
        here = slice(block * width, (block + 1) * width)
        mine = iota((slabs, width), 0) == wanted[:, here]
        mark = mine.astype(f32)
        before = dot(mark.astype(bf16), earlier)
        if passed is not None:
            before = before + dot(passed.astype(bf16), ones)
        passed = mark if passed is None else passed + mark
        slot = jnp.sum(mark * before, axis=0, keepdims=True).astype(jnp.int32)
        chosen = iota((capacity, width), 0) == slot
        hot[:, here] = mark.astype(bf16)
        split = pieces(parcels[:, here], 2)

        def placed(row):
            return jnp.where(chosen, row, 0.0)

        for k, part in enumerate(split):
            base = 0 if k == 0 else total + (k - 1) * features
            for f in range(0, FEATURES, 2):
                pair = jnp.concatenate([placed(part[f : f + 1]), placed(part[f + 1 : f + 2])], 0)
                spread[base + f * capacity : base + (f + 2) * capacity, here] = pair.astype(bf16)
        pair = jnp.concatenate([placed(line[:, here]), placed(column[:, here])], 0)
        spread[features:total, here] = pair.astype(bf16)
    out = dot(spread[...], hot[...], ((1,), (1,)))
    values = out[:features] + out[total:]
    filler = jnp.zeros((send.shape[0] // slabs * LANES - total, slabs), f32)
    whole = jnp.concatenate([values, out[features:total], filler], 0)
    lines = send.shape[0] // slabs
    for c in range(lines):
        send[pl.ds(c, slabs, stride=lines), :] = whole[c * LANES : (c + 1) * LANES].T
    copies[4].wait()
    copies[5].wait()


def stencil_kernel(fields, near, far, partial, halves, edges):
    radii = fields.shape[0] // 4
    columns = fields.shape[1]
    radius = iota((radii, columns), 0).astype(f32) + (NR + 0.5)
    arc = 1.0 / (radius * step_angle) ** 2
    lane = iota((radii, columns), 1)
    own = [fields[c * radii : (c + 1) * radii, :] for c in range(4)]

    def around(c):
        x = own[c]
        return (
            near[c * radii : (c + 1) * radii, :],
            far[c * radii : (c + 1) * radii, :],
            shifted(x, -1),
            shifted(x, 1),
            pltpu.roll(x, columns - 1, 1),
            pltpu.roll(x, 1, 1),
        )

    weights = (
        0.5,
        0.5,
        0.5 * (radius + 0.5) / radius,
        0.5 * (radius - 0.5) / radius,
        jnp.where(lane == columns - 1, 0.0, 0.5 * arc),
        jnp.where(lane == 0, 0.0, 0.5 * arc),
    )
    faces = [w * (own[3] + n) for w, n in zip(weights, around(3))]
    for c in range(3):
        u = own[c]
        total = jnp.zeros_like(u)
        for face, beside in zip(faces, around(c)):
            total = total + face * (beside - u)
        partial[c * radii : (c + 1) * radii, :] = u + time_step * total
    edges[...] = jnp.zeros_like(edges)
    for c in range(4):
        put_edges(edges, own[c], c, 4 + c)
        if c < 3:
            turned = own[c].T
            parts = [p.astype(bf16) for p in pieces(turned, 2)]
            halves[c * columns : (c + 1) * columns, :] = jnp.concatenate(parts, 1)


def put_edges(edges, x, first, last):
    turned = x.T
    for part in range(2):
        piece = turned[:, part * LANES : min((part + 1) * LANES, x.shape[0])]
        width = piece.shape[1]
        edges[part * EDGE_ROWS + first : part * EDGE_ROWS + first + 1, :width] = piece[:1]
        edges[part * EDGE_ROWS + last : part * EDGE_ROWS + last + 1, :width] = piece[LANES - 1 :]


def momentum_kernel(
    capacity, slabs, received, partial, halves, edges_in, ustar, payload, moved, line_hot, pulled, pushed, edges
):
    lines = received.shape[0] // slabs
    radii = partial.shape[0] // 3
    columns = partial.shape[1]
    turned = jnp.concatenate([received[pl.ds(c, slabs, stride=lines), :].T for c in range(lines)], 0)
    features = FEATURES * capacity
    line_of = turned[features : features + capacity].astype(jnp.int32) - 1
    column_of = turned[features + capacity : features + 2 * capacity].astype(jnp.int32)
    group = 2
    for j in range(0, capacity, group):
        here = slice(j * LANES, (j + group) * LANES)
        lane_line = jnp.concatenate([line_of[s : s + 1] for s in range(j, j + group)], 1)
        lane_column = jnp.concatenate([column_of[s : s + 1] for s in range(j, j + group)], 1)
        hot = (iota((radii, group * LANES), 0) == lane_line).astype(bf16)
        line_hot[:, here] = hot
        picked = dot(halves[...], jnp.concatenate([hot, hot], 0))
        match = iota((columns, group * LANES), 0) == lane_column
        for c in range(3):
            got = jnp.sum(jnp.where(match, picked[c * columns : (c + 1) * columns], 0.0), axis=0, keepdims=True)
            for s in range(group):
                pulled[c, j + s : j + s + 1, :] = got[:, s * LANES : (s + 1) * LANES]
    fluid = [pulled[c] for c in range(3)]
    drag = [jnp.zeros_like(fluid[0]) for _ in range(3)]
    for k in range(4):
        rate = turned[(4 * k + 3) * capacity : (4 * k + 4) * capacity]
        weight = time_step * rate
        scale = 1.0 / (1.0 + weight)
        moved[(4 * k + 3) * capacity : (4 * k + 4) * capacity, :] = rate
        for c in range(3):
            at = (4 * k + c) * capacity
            after = (turned[at : at + capacity] + weight * fluid[c]) * scale
            moved[at : at + capacity, :] = after
            drag[c] = drag[c] + rate * (after - fluid[c])
    drag = [d.astype(bf16).astype(f32) for d in drag]
    for j in range(capacity):
        match = iota((columns, LANES), 0) == column_of[j : j + 1]
        for c in range(3):
            pushed[c * columns : (c + 1) * columns, j * LANES : (j + 1) * LANES] = jnp.where(
                match, drag[c][j : j + 1], 0.0
            ).astype(bf16)
    deposit = dot(line_hot[...], pushed[...], ((1,), (1,)))
    stars = []
    for c in range(3):
        rows = slice(c * radii, (c + 1) * radii)
        star = partial[rows, :] + time_step * deposit[:, c * columns : (c + 1) * columns]
        ustar[rows, :] = star
        stars.append(star)
    row = iota((radii, columns), 0)
    lane = iota((radii, columns), 1)
    radius = row.astype(f32) + (NR + 0.5)
    flux = jnp.where(row < radii - 1, (radius + 0.5) * 0.5 * (stars[1] + shifted(stars[1], -1)), 0.0)
    ahead = jnp.where(lane == columns - 1, 0.0, pltpu.roll(stars[2], columns - 1, 1))
    behind = jnp.where(lane == 0, 0.0, pltpu.roll(stars[2], 1, 1))
    source = (shifted(flux, 1) - flux - (0.5 / step_angle) * (ahead - behind)) / radius
    edges[...] = edges_in[...]
    put_edges(edges, stars[2], 8, 9)
    for q in range(payload.shape[0]):
        payload[q, :radii, :] = source
        payload[q, radii:, :] = edges[...]


def project_kernel(gathered, ustar, transform, solve_a, solve_b, solve_c, out, solve, state, sems):
    me = lax.axis_index("pa")
    steps = 3 * NR
    fetches = [
        pltpu.make_async_copy(solve_b, solve.at[:steps], sems.at[0]),
        pltpu.make_async_copy(solve_c, solve.at[steps:], sems.at[1]),
    ]
    for fetch in fetches:
        fetch.start()
    ring = gathered.shape[0]
    radii = out.shape[0] // 3
    columns = out.shape[1]
    half = NTH // 2

    def turned(part):
        base = radii + part * EDGE_ROWS
        rows = [gathered[q % ring, base : base + EDGE_ROWS, :] for q in range(ring + 1)]
        rows.append(jnp.zeros((LANES - (ring + 1) * EDGE_ROWS, LANES), f32))
        return jnp.concatenate(rows, 0).T

    sides = jnp.concatenate([turned(0), turned(1)[: radii - LANES]], 0)
    row = iota((radii, LANES), 0)
    lane = iota((radii, LANES), 1)
    kind = lane % EDGE_ROWS
    radius = row.astype(f32) + (NR + 0.5)
    inverse = 1.0 / radius

    def lanes_from(x, by):
        return pltpu.roll(x, LANES - by, 1)

    beyond = lanes_from(sides, EDGE_ROWS - 4)
    both = sides + beyond
    face = jnp.where(kind == 4, lanes_from(both, 3), jnp.where(kind == 5, lanes_from(both, 2), lanes_from(both, 1)))
    arc = inverse * inverse * (0.5 * time_step / step_angle**2)
    used = lane < ring * EDGE_ROWS
    crossing = jnp.where(used & (kind >= 4) & (kind < 7), arc * face * (beyond - sides), 0.0)
    flux = jnp.where(row < radii - 1, (radius + 0.5) * 0.5 * (crossing + shifted(crossing, -1)), 0.0)
    outward = (shifted(flux, 1) - flux) * inverse
    turning = inverse * (0.5 / step_angle)
    coefficients = jnp.where(
        kind == 5,
        outward,
        turning * jnp.where(kind == 6, -crossing, jnp.where(kind == 8, -lanes_from(sides, EDGE_ROWS), sides)),
    )
    used = used & ((kind == 5) | (kind == 6) | (kind == 8) | (kind == 9))
    coefficients = jnp.where(used, coefficients, 0.0)[:, :CORRECTION_ROWS]

    width = 3 * columns
    wide_row = iota((LANES, width), 0)
    wide_lane = iota((LANES, width), 1)
    before = lax.rem(me + ring - 1, ring)
    inside = wide_lane % columns
    at = wide_lane // columns + 4
    pick = jnp.where((inside == columns - 1) & (wide_row == at + me * EDGE_ROWS), 1.0, 0.0) - jnp.where(
        (inside == 0) & (wide_row == at + before * EDGE_ROWS), 1.0, 0.0
    )
    pick = pick.astype(bf16)
    crossing_parts = [p.astype(bf16) for p in pieces(crossing, 2)]
    delta = dot(crossing_parts[0], pick) + dot(crossing_parts[1], pick)

    near = jnp.concatenate([gathered[q, :radii, :] for q in range(ring // 2)], 1)
    distant = jnp.concatenate([gathered[q, :radii, :] for q in range(ring // 2, ring)], 1)

    def product(x, rows, cols, contract=((1,), (0,))):
        high, low = [p.astype(bf16) for p in pieces(x, 2)]
        table_high = transform[rows, cols]
        table_low = transform[rows, slice(cols.start + NTH, cols.stop + NTH)]
        return dot(high, table_high, contract) + (dot(high, table_low, contract) + dot(low, table_high, contract))

    angles = slice(0, half)
    corrections = slice(half, half + CORRECTION_ROWS)
    even = slice(0, half)
    odd = slice(half, NTH)
    modes_even = product(near + distant, angles, even) + product(coefficients, corrections, even)
    modes_odd = product(near - distant, angles, odd) + product(coefficients, corrections, odd)
    blocks = [m[:, b * LANES : (b + 1) * LANES] for m in (modes_even, modes_odd) for b in range(2)]
    total = sum(NR + i + 0.5 for i in range(NR))
    mean = jnp.sum(radius * blocks[0], axis=0, keepdims=True) * (1.0 / total)
    blocks[0] = blocks[0] - jnp.where(iota((1, LANES), 1) == 0, mean, 0.0)
    held = (0, 1, 2, 2)

    def factor(k, cols):
        at = k % 3 * radii
        return (solve_a if k < 3 else solve)[at : at + radii, cols]

    fetches[0].wait()
    for b in range(ring):
        x = blocks[b]
        cols = slice(held[b] * LANES, (held[b] + 1) * LANES)
        stride, k = 1, 0
        while stride < SUBLANES:
            x = (
                x
                - factor(k, cols) * pltpu.roll(x, stride, 0)
                - factor(k + 1, cols) * pltpu.roll(x, radii - stride, 0)
            )
            stride *= 2
            k += 2
        state[:, b * LANES : (b + 1) * LANES] = x

    fetches[1].wait()

    def factors(k, v):
        rows = slice((k - 3) * radii + v * SUBLANES, (k - 3) * radii + (v + 1) * SUBLANES)
        return jnp.concatenate([solve[rows, : 3 * LANES], solve[rows, 2 * LANES : 3 * LANES]], 1)

    steps = radii // SUBLANES
    y = state[:SUBLANES, :]
    for v in range(1, steps):
        rows = slice(v * SUBLANES, (v + 1) * SUBLANES)
        y = state[rows, :] - factors(6, v) * y
        state[rows, :] = y
    x = y * factors(7, steps - 1)
    state[(steps - 1) * SUBLANES :, :] = x
    for v in range(steps - 2, -1, -1):
        rows = slice(v * SUBLANES, (v + 1) * SUBLANES)
        x = state[rows, :] * factors(7, v) - factors(8, v) * x
        state[rows, :] = x

    potential = [state[:, b * LANES : (b + 1) * LANES] for b in range(ring)]

    def gradient(x):
        above = jnp.where(row == radii - 1, x, pltpu.roll(x, radii - 1, 0))
        below = jnp.where(row == 0, x, pltpu.roll(x, 1, 0))
        return above - below

    mine = pl.ds(pl.multiple_of(me % 2 * columns, columns), columns)
    result = []
    for group, cols in ((0, even), (1, odd)):
        plain, mirror = potential[2 * group], potential[2 * group + 1]
        sine = solve[6 * radii : 6 * radii + 1, 2 * group * LANES : (2 * group + 1) * LANES]
        slopes = jnp.concatenate([gradient(plain), gradient(mirror)], 1)
        turns = jnp.concatenate([-sine * mirror, sine * plain], 1)
        result.append(product(jnp.concatenate([slopes, turns], 0), mine, cols, ((1,), (1,))))
    result = result[0] + jnp.where(me >= ring // 2, -1.0, 1.0) * result[1]
    out[:radii, :] = ustar[:radii, :] + delta[:, :columns]
    out[radii : 2 * radii, :] = ustar[radii : 2 * radii, :] + delta[:, columns : 2 * columns] - result[:radii] * (0.5 / NTH)
    out[2 * radii :, :] = ustar[2 * radii :, :] + delta[:, 2 * columns :] - result[radii:] * (turning * (1.0 / NTH))


def place_kernel(capacity, slabs, moved, out):
    rows = slabs * capacity
    width = 768
    split = jnp.concatenate([p.astype(bf16) for p in pieces(moved[...], 3)], 1)
    for start in range(0, rows, width):
        place = start + iota((slabs, width), 1)
        hot = (place // capacity == iota((slabs, width), 0)).astype(bf16)
        spread = dot(split, jnp.concatenate([hot, hot, hot], 0))
        match = (start + iota((capacity, width), 1)) % capacity == iota((capacity, width), 0)
        for f in range(FEATURES):
            block = spread[f * capacity : (f + 1) * capacity]
            out[f : f + 1, start : start + width] = jnp.sum(jnp.where(match, block, 0.0), axis=0, keepdims=True)


def shape(*dims):
    return jax.ShapeDtypeStruct(dims, f32)


def params(mib):
    return pltpu.CompilerParams(vmem_limit_bytes=int(mib * 1024 * 1024))


def cost(microseconds):
    return pl.CostEstimate(flops=0, bytes_accessed=int(microseconds * 3.0e6), transcendentals=0)


def body(velocity, viscosity, parcels, dest_rank, dest_cell, counts):
    slabs = lax.axis_size("gz")
    ring = lax.axis_size("pa")
    planes, radii, columns = viscosity.shape
    block = parcels.shape[0]
    capacity = 3 * block // slabs
    lines = -(-(FEATURES + 2) * capacity // LANES)
    vmem = pl.BlockSpec(memory_space=pltpu.VMEM)
    hbm = pl.BlockSpec(memory_space=pltpu.HBM)
    u = velocity.reshape(3 * radii, columns)
    nu = viscosity.reshape(radii, columns)
    features = FEATURES * capacity
    send, fields = pl.pallas_call(
        functools.partial(pack_kernel, capacity, slabs),
        out_shape=(shape(slabs * lines, LANES), shape(4 * radii, columns)),
        in_specs=[hbm] * 6,
        out_specs=(vmem,) * 2,
        scratch_shapes=[
            pltpu.SMEM((1,), jnp.int32),
            pltpu.VMEM((FEATURES, block), f32),
            pltpu.VMEM((1, block), jnp.int32),
            pltpu.VMEM((1, block), jnp.int32),
            pltpu.VMEM((2 * features + 2 * capacity, block), bf16),
            pltpu.VMEM((slabs, block), bf16),
            pltpu.SemaphoreType.DMA((6,)),
        ],
        compiler_params=params(60),
        cost_estimate=cost(3),
        name="pack",
    )(counts, parcels.T, dest_rank.reshape(1, block), dest_cell.reshape(1, block), u, nu)
    received = lax.all_to_all(
        send.reshape(slabs, lines, LANES), "gz", split_axis=0, concat_axis=0, tiled=True
    ).reshape(slabs * lines, LANES)

    near = lax.ppermute(fields, "gz", [(i, i ^ 1) for i in range(slabs)])
    pairs = [(i, i + 1) for i in range(1, slabs - 1, 2)]
    far = lax.ppermute(fields, "gz", pairs + [(j, i) for i, j in pairs])
    transform = jnp.asarray(transform_table(ring, columns))
    factors = solve_tables()
    partial, halves, edges = pl.pallas_call(
        stencil_kernel,
        out_shape=(
            shape(3 * radii, columns),
            jax.ShapeDtypeStruct((3 * columns, 2 * radii), bf16),
            shape(2 * EDGE_ROWS, LANES),
        ),
        in_specs=[vmem] * 3,
        out_specs=(vmem,) * 3,
        compiler_params=params(16),
        cost_estimate=cost(2),
        name="stencil",
    )(fields, near, far)

    ustar, payload, moved = pl.pallas_call(
        functools.partial(momentum_kernel, capacity, slabs),
        out_shape=(
            shape(3 * radii, columns),
            shape(ring, radii + 2 * EDGE_ROWS, columns),
            shape(features, slabs),
        ),
        in_specs=[vmem] * 4,
        out_specs=(vmem,) * 3,
        scratch_shapes=[
            pltpu.VMEM((radii, capacity * slabs), bf16),
            pltpu.VMEM((3, capacity, slabs), f32),
            pltpu.VMEM((3 * columns, capacity * slabs), bf16),
            pltpu.VMEM((2 * EDGE_ROWS, LANES), f32),
        ],
        compiler_params=params(16),
        cost_estimate=cost(4),
        name="momentum",
    )(received, partial, halves, edges)

    gathered = lax.all_to_all(payload, "pa", split_axis=0, concat_axis=0, tiled=True)
    parcels_out = pl.pallas_call(
        functools.partial(place_kernel, capacity, slabs),
        out_shape=shape(FEATURES, slabs * capacity),
        in_specs=[vmem],
        out_specs=vmem,
        compiler_params=params(16),
        cost_estimate=cost(3),
        name="place",
    )(moved)
    velocity_out = pl.pallas_call(
        project_kernel,
        out_shape=shape(3 * radii, columns),
        in_specs=[vmem] * 4 + [hbm] * 2,
        out_specs=vmem,
        scratch_shapes=[
            pltpu.VMEM((factors.shape[0] - 3 * radii, factors.shape[1]), f32),
            pltpu.VMEM((radii, NTH), f32),
            pltpu.SemaphoreType.DMA((2,)),
        ],
        compiler_params=params(51.5),
        cost_estimate=cost(5),
        name="project",
    )(gathered, ustar, transform, factors[: 3 * radii], factors[3 * radii : 6 * radii], factors[6 * radii :])
    return velocity_out.reshape(velocity.shape), parcels_out.T


def solution(mesh):
    in_specs = (
        P(None, "gz", None, "pa"),
        P("gz", None, "pa"),
        P(("gz", "pa"), None),
        P(("gz", "pa"), None),
        P(("gz", "pa")),
        P(("gz", "pa")),
    )
    out_specs = (P(None, "gz", None, "pa"), P(("gz", "pa"), None))
    return jax.shard_map(body, mesh=mesh, in_specs=in_specs, out_specs=out_specs, check_vma=False)
```

```python
import functools
import math

import jax
import jax.numpy as jnp
import numpy as np
from jax import lax
from jax.experimental import pallas as pl
from jax.experimental.pallas import tpu as pltpu
from jax.sharding import PartitionSpec as P

NR = 192
NTH = 512
time_step = 0.1
shift_plane = 0.0001
step_angle = 2.0 * math.pi / NTH
LANES = 128
FEATURES = 16
SUBLANES = 8
EDGE_ROWS = 16
CORRECTION_ROWS = 64
f32 = jnp.float32
bf16 = jnp.bfloat16


def cas(numbers):
    phase = 2.0 * np.pi / NTH * (numbers % NTH)
    return np.cos(phase) + np.sin(phase)


def paired_modes():
    half, even, odd = NTH // 2, np.arange(0, NTH // 2, 2), np.arange(1, NTH // 2, 2)
    return np.concatenate([even, [half], NTH - even[1:], odd, NTH - odd])


def split_table(table):
    high = table.astype(jnp.bfloat16)
    return high, (table - high.astype(np.float64)).astype(jnp.bfloat16)


@functools.cache
def transform_table(ring, columns):
    modes = paired_modes()[None, :]
    plain = cas(np.arange(NTH // 2)[:, None] * modes)
    faces = np.zeros((CORRECTION_ROWS, NTH))
    for q in range(ring):
        last, at = q * columns + columns - 1, q * EDGE_ROWS

        def wave(offset):
            return cas((last + offset) * modes)

        faces[at + 5] = wave(0) - wave(1)
        faces[at + 6] = wave(-1) - wave(1) - wave(0) + wave(2)
        faces[at + 8] = wave(0)
        faces[at + 9] = wave(1)
    high, low = split_table(plain)
    face_high, face_low = split_table(faces)
    return np.concatenate([high, low, face_high, face_low, face_high], 0)


@functools.cache
def solve_tables():
    radius = NR + np.arange(NR) + 0.5
    arc = 1.0 / (radius * step_angle) ** 2
    up, down = radius + 0.5, radius - 0.5
    up[-1] = 0.0
    down[0] = 0.0
    spectrum = 2.0 - 2.0 * np.cos(step_angle * paired_modes())
    diagonal = radius[:, None] * (shift_plane + arc[:, None] * spectrum[None, :]) + up[:, None] + down[:, None]
    lower = np.broadcast_to(-down[:, None], diagonal.shape)
    upper = np.broadcast_to(-up[:, None], diagonal.shape)

    def moved(x, by, fill):
        filled = np.full((abs(by),) + x.shape[1:], fill)
        return np.concatenate([filled, x[:-by]], 0) if by > 0 else np.concatenate([x[-by:], filled], 0)

    tables, stride = [1.0 / diagonal], 1
    while stride < SUBLANES:
        low = lower / moved(diagonal, stride, 1.0)
        high = upper / moved(diagonal, -stride, 1.0)
        diagonal = diagonal - low * moved(upper, stride, 0.0) - high * moved(lower, -stride, 0.0)
        lower = -low * moved(lower, stride, 0.0)
        upper = -high * moved(upper, -stride, 0.0)
        if stride > 1:
            tables += [low, high]
        stride *= 2
    pivot = diagonal.copy()
    for i in range(SUBLANES, NR):
        pivot[i] = diagonal[i] - upper[i - SUBLANES] ** 2 / pivot[i - SUBLANES]
    middle = np.zeros((NR, 2 * LANES))
    for k, table in enumerate(tables):
        middle[:, k] = table[:, LANES]
    reduction = np.concatenate(tables, 0)
    reduction = np.concatenate([reduction[:, :LANES], reduction[:, 2 * LANES : 3 * LANES]], 1)
    sine = np.broadcast_to(2.0 * np.sin(step_angle * paired_modes()), (SUBLANES, NTH))
    elimination = np.concatenate([1.0 / pivot, upper / pivot, sine] + tables, 0)[:, : 3 * LANES]
    return np.concatenate([reduction, middle], 0).astype(np.float32), elimination.astype(np.float32)


def pieces(x, count):
    out = []
    for _ in range(count):
        part = x.astype(bf16).astype(f32)
        out.append(part)
        x = x - part
    return out


def dot(a, b, contract=((1,), (0,))):
    return lax.dot_general(a, b, (contract, ((), ())), preferred_element_type=f32)


def iota(shape, dim):
    return lax.broadcasted_iota(jnp.int32, shape, dim)


def shifted(x, by):
    length = x.shape[0]
    rolled = pltpu.roll(x, by % length, 0)
    row = iota(x.shape, 0)
    return jnp.where(row >= by if by > 0 else row < length + by, rolled, 0.0)


def pack_kernel(
    capacity, slabs, counts_in, parcels_in, target_in, cell_in, velocity_in, viscosity_in, send, fields,
    counts, parcels, target, cell, spread, hot, sems,
):
    radii3 = velocity_in.shape[0]
    copies = [
        pltpu.make_async_copy(source, target_ref, sems.at[k])
        for k, (source, target_ref) in enumerate(
            (
                (counts_in, counts),
                (target_in, target),
                (parcels_in, parcels),
                (cell_in, cell),
                (velocity_in, fields.at[:radii3]),
                (viscosity_in, fields.at[radii3:]),
            )
        )
    ]
    for copy in copies:
        copy.start()
    rows = parcels.shape[1]
    width = 256
    earlier = (iota((width, width), 0) < iota((width, width), 1)).astype(bf16)
    ones = jnp.ones((width, width), bf16)
    features = FEATURES * capacity
    total = features + 2 * capacity
    copies[0].wait()
    copies[1].wait()
    live = iota((1, rows), 1) < counts[0]
    wanted = jnp.where(live, target[...], -1)
    copies[2].wait()
    copies[3].wait()
    cells = cell[...]
    line = (cells // LANES + 1).astype(f32)
    column = (cells % LANES).astype(f32)
    passed = None
    for block in range(rows // width):
        here = slice(block * width, (block + 1) * width)
        mine = iota((slabs, width), 0) == wanted[:, here]
        mark = mine.astype(f32)
        before = dot(mark.astype(bf16), earlier)
        if passed is not None:
            before = before + dot(passed.astype(bf16), ones)
        passed = mark if passed is None else passed + mark
        slot = jnp.sum(mark * before, axis=0, keepdims=True).astype(jnp.int32)
        chosen = iota((capacity, width), 0) == slot
        hot[:, here] = mark.astype(bf16)
        split = pieces(parcels[:, here], 2)

        def placed(row):
            return jnp.where(chosen, row, 0.0)

        for k, part in enumerate(split):
            base = 0 if k == 0 else total + (k - 1) * features
            for f in range(0, FEATURES, 2):
                pair = jnp.concatenate([placed(part[f : f + 1]), placed(part[f + 1 : f + 2])], 0)
                spread[base + f * capacity : base + (f + 2) * capacity, here] = pair.astype(bf16)
        pair = jnp.concatenate([placed(line[:, here]), placed(column[:, here])], 0)
        spread[features:total, here] = pair.astype(bf16)
    out = dot(spread[...], hot[...], ((1,), (1,)))
    values = out[:features] + out[total:]
    filler = jnp.zeros((send.shape[0] // slabs * LANES - total, slabs), f32)
    whole = jnp.concatenate([values, out[features:total], filler], 0)
    lines = send.shape[0] // slabs
    for c in range(lines):
        send[pl.ds(c, slabs, stride=lines), :] = whole[c * LANES : (c + 1) * LANES].T
    copies[4].wait()
    copies[5].wait()


def stencil_kernel(fields, near, far, partial, halves, edges):
    radii = fields.shape[0] // 4
    columns = fields.shape[1]
    radius = iota((radii, columns), 0).astype(f32) + (NR + 0.5)
    arc = 1.0 / (radius * step_angle) ** 2
    lane = iota((radii, columns), 1)
    own = [fields[c * radii : (c + 1) * radii, :] for c in range(4)]

    def around(c):
        x = own[c]
        return (
            near[c * radii : (c + 1) * radii, :],
            far[c * radii : (c + 1) * radii, :],
            shifted(x, -1),
            shifted(x, 1),
            pltpu.roll(x, columns - 1, 1),
            pltpu.roll(x, 1, 1),
        )

    weights = (
        0.5,
        0.5,
        0.5 * (radius + 0.5) / radius,
        0.5 * (radius - 0.5) / radius,
        jnp.where(lane == columns - 1, 0.0, 0.5 * arc),
        jnp.where(lane == 0, 0.0, 0.5 * arc),
    )
    faces = [w * (own[3] + n) for w, n in zip(weights, around(3))]
    for c in range(3):
        u = own[c]
        total = jnp.zeros_like(u)
        for face, beside in zip(faces, around(c)):
            total = total + face * (beside - u)
        partial[c * radii : (c + 1) * radii, :] = u + time_step * total
    edges[...] = jnp.zeros_like(edges)
    for c in range(4):
        put_edges(edges, own[c], c, 4 + c)
        if c < 3:
            turned = own[c].T
            parts = [p.astype(bf16) for p in pieces(turned, 2)]
            halves[c * columns : (c + 1) * columns, :] = jnp.concatenate(parts, 1)


def put_edges(edges, x, first, last):
    turned = x.T
    rest = x.shape[0] - LANES
    for column, row in ((first, turned[:1]), (last, turned[LANES - 1 :])):
        edges[column : column + 1, :] = row[:, :LANES]
        at = 10 + column % 5
        start = column // 5 * rest
        edges[at : at + 1, start : start + rest] = row[:, LANES:]


def momentum_kernel(
    capacity, slabs, received, partial, halves, edges_in, ustar, payload, moved, line_hot, pulled, pushed, edges
):
    lines = received.shape[0] // slabs
    radii = partial.shape[0] // 3
    columns = partial.shape[1]
    turned = jnp.concatenate([received[pl.ds(c, slabs, stride=lines), :].T for c in range(lines)], 0)
    features = FEATURES * capacity
    line_of = turned[features : features + capacity].astype(jnp.int32) - 1
    column_of = turned[features + capacity : features + 2 * capacity].astype(jnp.int32)
    group = 2
    for j in range(0, capacity, group):
        here = slice(j * LANES, (j + group) * LANES)
        lane_line = jnp.concatenate([line_of[s : s + 1] for s in range(j, j + group)], 1)
        lane_column = jnp.concatenate([column_of[s : s + 1] for s in range(j, j + group)], 1)
        hot = (iota((radii, group * LANES), 0) == lane_line).astype(bf16)
        line_hot[:, here] = hot
        picked = dot(halves[...], jnp.concatenate([hot, hot], 0))
        match = iota((columns, group * LANES), 0) == lane_column
        for c in range(3):
            got = jnp.sum(jnp.where(match, picked[c * columns : (c + 1) * columns], 0.0), axis=0, keepdims=True)
            for s in range(group):
                pulled[c, j + s : j + s + 1, :] = got[:, s * LANES : (s + 1) * LANES]
    fluid = [pulled[c] for c in range(3)]
    drag = [jnp.zeros_like(fluid[0]) for _ in range(3)]
    for k in range(4):
        rate = turned[(4 * k + 3) * capacity : (4 * k + 4) * capacity]
        weight = time_step * rate
        scale = 1.0 / (1.0 + weight)
        moved[(4 * k + 3) * capacity : (4 * k + 4) * capacity, :] = rate
        for c in range(3):
            at = (4 * k + c) * capacity
            after = (turned[at : at + capacity] + weight * fluid[c]) * scale
            moved[at : at + capacity, :] = after
            drag[c] = drag[c] + rate * (after - fluid[c])
    drag = [d.astype(bf16).astype(f32) for d in drag]
    for j in range(capacity):
        match = iota((columns, LANES), 0) == column_of[j : j + 1]
        for c in range(3):
            pushed[c * columns : (c + 1) * columns, j * LANES : (j + 1) * LANES] = jnp.where(
                match, drag[c][j : j + 1], 0.0
            ).astype(bf16)
    deposit = dot(line_hot[...], pushed[...], ((1,), (1,)))
    stars = []
    for c in range(3):
        rows = slice(c * radii, (c + 1) * radii)
        star = partial[rows, :] + time_step * deposit[:, c * columns : (c + 1) * columns]
        ustar[rows, :] = star
        stars.append(star)
    row = iota((radii, columns), 0)
    lane = iota((radii, columns), 1)
    radius = row.astype(f32) + (NR + 0.5)
    flux = jnp.where(row < radii - 1, (radius + 0.5) * 0.5 * (stars[1] + shifted(stars[1], -1)), 0.0)
    ahead = jnp.where(lane == columns - 1, 0.0, pltpu.roll(stars[2], columns - 1, 1))
    behind = jnp.where(lane == 0, 0.0, pltpu.roll(stars[2], 1, 1))
    source = shifted(flux, 1) - flux - (0.5 / step_angle) * (ahead - behind)
    edges[...] = edges_in[...]
    put_edges(edges, stars[2], 8, 9)
    for q in range(payload.shape[0]):
        payload[q, :radii, :] = source
        payload[q, radii:, :] = edges[...]


def project_kernel(gathered, ustar, transform, reduction, elimination_in, out, elimination, state, sem):
    me = lax.axis_index("pa")
    fetch = pltpu.make_async_copy(elimination_in.at[: elimination.shape[0]], elimination, sem)
    fetch.start()
    ring = gathered.shape[0]
    radii = out.shape[0] // 3
    columns = out.shape[1]
    half = NTH // 2

    rows = [gathered[q % ring, radii:, :] for q in range(ring + 1)]
    rows.append(jnp.zeros((LANES - (ring + 1) * EDGE_ROWS, LANES), f32))
    turned = jnp.concatenate(rows, 0).T
    rest = radii - LANES
    fifth = iota((rest, LANES), 1) % EDGE_ROWS < 5
    others = jnp.where(
        fifth, pltpu.roll(turned[:rest], LANES - 10, 1), pltpu.roll(turned[rest : 2 * rest], LANES - 5, 1)
    )

    sides = jnp.concatenate([turned, others], 0)
    row = iota((radii, LANES), 0)
    lane = iota((radii, LANES), 1)
    kind = lane % EDGE_ROWS
    radius = row.astype(f32) + (NR + 0.5)
    inverse = 1.0 / radius

    def lanes_from(x, by):
        return pltpu.roll(x, LANES - by, 1)

    beyond = lanes_from(sides, EDGE_ROWS - 4)
    both = sides + beyond
    face = jnp.where(kind == 4, lanes_from(both, 3), jnp.where(kind == 5, lanes_from(both, 2), lanes_from(both, 1)))
    arc = inverse * inverse * (0.5 * time_step / step_angle**2)
    used = lane < ring * EDGE_ROWS
    crossing = jnp.where(used & (kind >= 4) & (kind < 7), arc * face * (beyond - sides), 0.0)
    flux = jnp.where(row < radii - 1, (radius + 0.5) * 0.5 * (crossing + shifted(crossing, -1)), 0.0)
    outward = shifted(flux, 1) - flux
    turning = 0.5 / step_angle
    coefficients = jnp.where(
        kind == 5,
        outward,
        turning * jnp.where(kind == 6, -crossing, jnp.where(kind == 8, -lanes_from(sides, EDGE_ROWS), sides)),
    )
    used = used & ((kind == 5) | (kind == 6) | (kind == 8) | (kind == 9))
    coefficients = jnp.where(used, coefficients, 0.0)[:, :CORRECTION_ROWS]

    width = 3 * columns
    wide_row = iota((LANES, width), 0)
    wide_lane = iota((LANES, width), 1)
    before = lax.rem(me + ring - 1, ring)
    inside = wide_lane % columns
    at = wide_lane // columns + 4
    pick = jnp.where((inside == columns - 1) & (wide_row == at + me * EDGE_ROWS), 1.0, 0.0) - jnp.where(
        (inside == 0) & (wide_row == at + before * EDGE_ROWS), 1.0, 0.0
    )
    pick = pick.astype(bf16)
    crossing_parts = [p.astype(bf16) for p in pieces(crossing, 2)]
    delta = dot(jnp.concatenate(crossing_parts, 1), jnp.concatenate([pick, pick], 0))

    near = jnp.concatenate([gathered[q, :radii, :] for q in range(ring // 2)], 1)
    distant = jnp.concatenate([gathered[q, :radii, :] for q in range(ring // 2, ring)], 1)

    def forward(x, cols):
        high, low = [p.astype(bf16) for p in pieces(x, 2)]
        table_high, table_low = transform[:half, cols], transform[half : 2 * half, cols]
        return dot(high, table_high) + (dot(high, table_low) + dot(low, table_high)) + dot(corrections, transform[2 * half :, cols])

    parts = [p.astype(bf16) for p in pieces(coefficients, 2)]
    corrections = jnp.concatenate([parts[0], parts[0], parts[1]], 1)
    even = slice(0, half)
    odd = slice(half, NTH)
    modes_even = forward(near + distant, even)
    modes_odd = forward(near - distant, odd)
    blocks = [m[:, b * LANES : (b + 1) * LANES] for m in (modes_even, modes_odd) for b in range(2)]
    total = sum(NR + i + 0.5 for i in range(NR))
    mean = jnp.sum(blocks[0], axis=0, keepdims=True) * (1.0 / total)
    blocks[0] = blocks[0] - radius * jnp.where(iota((1, LANES), 1) == 0, mean, 0.0)
    middle = reduction[5 * radii :, :LANES]

    def factor(k, b):
        table = reduction[k * radii : (k + 1) * radii, b // 2 * LANES : (b // 2 + 1) * LANES]
        return jnp.where(lane == 0, pltpu.roll(middle, (LANES - k) % LANES, 1), table) if b == 1 else table

    inner = jnp.where(row > 0, radius - 0.5, 0.0)
    outer = jnp.where(row < radii - 1, radius + 0.5, 0.0)
    for b in range(ring):
        x = blocks[b]
        scaled = x * factor(0, b)
        x = x + inner * pltpu.roll(scaled, 1, 0) + outer * pltpu.roll(scaled, radii - 1, 0)
        for stride, k in ((2, 1), (4, 3)):
            x = x - factor(k, b) * pltpu.roll(x, stride, 0) - factor(k + 1, b) * pltpu.roll(x, radii - stride, 0)
        state[:, b * LANES : (b + 1) * LANES] = x
    fetch.wait()

    def factors(k, v):
        at = k * radii + v * SUBLANES
        table = elimination[at : at + SUBLANES, :]
        return jnp.concatenate([table, table[:, 2 * LANES :]], 1)

    steps = radii // SUBLANES
    y = state[:SUBLANES, :]
    for v in range(1, steps):
        rows = slice(v * SUBLANES, (v + 1) * SUBLANES)
        y = state[rows, :] - factors(1, v - 1) * y
        state[rows, :] = y
    x = y * factors(0, steps - 1)
    state[(steps - 1) * SUBLANES :, :] = x
    for v in range(steps - 2, -1, -1):
        rows = slice(v * SUBLANES, (v + 1) * SUBLANES)
        x = state[rows, :] * factors(0, v) - factors(1, v) * x
        state[rows, :] = x

    potential = [state[:, b * LANES : (b + 1) * LANES] for b in range(ring)]

    def gradient(x):
        above = jnp.where(row == radii - 1, x, pltpu.roll(x, radii - 1, 0))
        below = jnp.where(row == 0, x, pltpu.roll(x, 1, 0))
        return above - below

    mine = pl.multiple_of(me % 2 * columns, columns)
    result = []
    for group, cols in ((0, even), (1, odd)):
        plain, mirror = potential[2 * group], potential[2 * group + 1]
        sine = elimination[2 * radii : 2 * radii + 1, 2 * group * LANES : (2 * group + 1) * LANES]
        slopes = jnp.concatenate([gradient(plain), gradient(mirror)], 1)
        turns = jnp.concatenate([-sine * mirror, sine * plain], 1)
        high, low = [p.astype(bf16) for p in pieces(jnp.concatenate([slopes, turns], 0), 2)]
        own_high, own_low = transform[pl.ds(mine, columns), cols], transform[pl.ds(half + mine, columns), cols]
        both = dot(high, jnp.concatenate([own_high, own_low], 0), ((1,), (1,)))
        result.append(both[:, :columns] + (both[:, columns:] + dot(low, own_high, ((1,), (1,)))))
    result = result[0] + jnp.where(me >= ring // 2, -1.0, 1.0) * result[1]
    out[:radii, :] = ustar[:radii, :] + delta[:, :columns]
    out[radii : 2 * radii, :] = ustar[radii : 2 * radii, :] + delta[:, columns : 2 * columns] - result[:radii] * (0.5 / NTH)
    out[2 * radii :, :] = ustar[2 * radii :, :] + delta[:, 2 * columns :] - result[radii:] * (inverse * (turning / NTH))


def place_kernel(capacity, slabs, moved, out):
    rows = slabs * capacity
    width = 768
    split = jnp.concatenate([p.astype(bf16) for p in pieces(moved[...], 3)], 1)
    for start in range(0, rows, width):
        place = start + iota((slabs, width), 1)
        hot = (place // capacity == iota((slabs, width), 0)).astype(bf16)
        spread = dot(split, jnp.concatenate([hot, hot, hot], 0))
        match = (start + iota((capacity, width), 1)) % capacity == iota((capacity, width), 0)
        for f in range(FEATURES):
            block = spread[f * capacity : (f + 1) * capacity]
            out[f : f + 1, start : start + width] = jnp.sum(jnp.where(match, block, 0.0), axis=0, keepdims=True)


def shape(*dims):
    return jax.ShapeDtypeStruct(dims, f32)


def params(mib):
    return pltpu.CompilerParams(vmem_limit_bytes=int(mib * 1024 * 1024))


def cost(microseconds):
    return pl.CostEstimate(flops=0, bytes_accessed=int(microseconds * 3.0e6), transcendentals=0)


def body(velocity, viscosity, parcels, dest_rank, dest_cell, counts):
    slabs = lax.axis_size("gz")
    ring = lax.axis_size("pa")
    planes, radii, columns = viscosity.shape
    block = parcels.shape[0]
    capacity = 3 * block // slabs
    lines = -(-(FEATURES + 2) * capacity // LANES)
    vmem = pl.BlockSpec(memory_space=pltpu.VMEM)
    hbm = pl.BlockSpec(memory_space=pltpu.HBM)
    u = velocity.reshape(3 * radii, columns)
    nu = viscosity.reshape(radii, columns)
    features = FEATURES * capacity
    send, fields = pl.pallas_call(
        functools.partial(pack_kernel, capacity, slabs),
        out_shape=(shape(slabs * lines, LANES), shape(4 * radii, columns)),
        in_specs=[hbm] * 6,
        out_specs=(vmem,) * 2,
        scratch_shapes=[
            pltpu.SMEM((1,), jnp.int32),
            pltpu.VMEM((FEATURES, block), f32),
            pltpu.VMEM((1, block), jnp.int32),
            pltpu.VMEM((1, block), jnp.int32),
            pltpu.VMEM((2 * features + 2 * capacity, block), bf16),
            pltpu.VMEM((slabs, block), bf16),
            pltpu.SemaphoreType.DMA((6,)),
        ],
        compiler_params=params(60),
        cost_estimate=cost(3),
        name="pack",
    )(counts, parcels.T, dest_rank.reshape(1, block), dest_cell.reshape(1, block), u, nu)
    received = lax.all_to_all(
        send.reshape(slabs, lines, LANES), "gz", split_axis=0, concat_axis=0, tiled=True
    ).reshape(slabs * lines, LANES)

    near = lax.ppermute(fields, "gz", [(i, i ^ 1) for i in range(slabs)])
    pairs = [(i, i + 1) for i in range(1, slabs - 1, 2)]
    far = lax.ppermute(fields, "gz", pairs + [(j, i) for i, j in pairs])
    transform = jnp.asarray(transform_table(ring, columns))
    reduction, elimination = [jnp.asarray(table) for table in solve_tables()]
    partial, halves, edges = pl.pallas_call(
        stencil_kernel,
        out_shape=(
            shape(3 * radii, columns),
            jax.ShapeDtypeStruct((3 * columns, 2 * radii), bf16),
            shape(EDGE_ROWS, LANES),
        ),
        in_specs=[vmem] * 3,
        out_specs=(vmem,) * 3,
        compiler_params=params(16),
        cost_estimate=cost(2),
        name="stencil",
    )(fields, near, far)

    ustar, payload, moved = pl.pallas_call(
        functools.partial(momentum_kernel, capacity, slabs),
        out_shape=(
            shape(3 * radii, columns),
            shape(ring, radii + EDGE_ROWS, columns),
            shape(features, slabs),
        ),
        in_specs=[vmem] * 4,
        out_specs=(vmem,) * 3,
        scratch_shapes=[
            pltpu.VMEM((radii, capacity * slabs), bf16),
            pltpu.VMEM((3, capacity, slabs), f32),
            pltpu.VMEM((3 * columns, capacity * slabs), bf16),
            pltpu.VMEM((EDGE_ROWS, LANES), f32),
        ],
        compiler_params=params(16),
        cost_estimate=cost(4),
        name="momentum",
    )(received, partial, halves, edges)

    gathered = lax.all_to_all(payload, "pa", split_axis=0, concat_axis=0, tiled=True)
    parcels_out = pl.pallas_call(
        functools.partial(place_kernel, capacity, slabs),
        out_shape=shape(FEATURES, slabs * capacity),
        in_specs=[vmem],
        out_specs=vmem,
        compiler_params=params(16),
        cost_estimate=cost(3),
        name="place",
    )(moved)
    velocity_out = pl.pallas_call(
        project_kernel,
        out_shape=shape(3 * radii, columns),
        in_specs=[vmem] * 4 + [hbm],
        out_specs=vmem,
        scratch_shapes=[
            pltpu.VMEM((2 * radii + SUBLANES, elimination.shape[1]), f32),
            pltpu.VMEM((radii, NTH), f32),
            pltpu.SemaphoreType.DMA,
        ],
        compiler_params=params(51.25),
        cost_estimate=cost(5),
        name="project",
    )(gathered, ustar, transform, reduction, elimination)
    return velocity_out.reshape(velocity.shape), parcels_out.T


def solution(mesh):
    in_specs = (
        P(None, "gz", None, "pa"),
        P("gz", None, "pa"),
        P(("gz", "pa"), None),
        P(("gz", "pa"), None),
        P(("gz", "pa")),
        P(("gz", "pa")),
    )
    out_specs = (P(None, "gz", None, "pa"), P(("gz", "pa"), None))
    return jax.shard_map(body, mesh=mesh, in_specs=in_specs, out_specs=out_specs, check_vma=False)
```

```python
import functools
import math

import jax
import jax.numpy as jnp
import numpy as np
from jax import lax
from jax.experimental import pallas as pl
from jax.experimental.pallas import tpu as pltpu
from jax.sharding import PartitionSpec as P

NR = 192
NTH = 512
time_step = 0.1
shift_plane = 0.0001
step_angle = 2.0 * math.pi / NTH
LANES = 128
FEATURES = 16
SUBLANES = 8
EDGE_ROWS = 16
CORRECTION_ROWS = 64
f32 = jnp.float32
bf16 = jnp.bfloat16


def cas(numbers):
    phase = 2.0 * np.pi / NTH * (numbers % NTH)
    return np.cos(phase) + np.sin(phase)


def paired_modes():
    half, even, odd = NTH // 2, np.arange(0, NTH // 2, 2), np.arange(1, NTH // 2, 2)
    return np.concatenate([even, [half], NTH - even[1:], odd, NTH - odd])


def split_table(table):
    high = table.astype(jnp.bfloat16)
    return high, (table - high.astype(np.float64)).astype(jnp.bfloat16)


@functools.cache
def transform_table(ring, columns):
    modes = paired_modes()[None, :]
    plain = cas(np.arange(NTH // 2)[:, None] * modes)
    faces = np.zeros((CORRECTION_ROWS, NTH))
    for q in range(ring):
        last, at = q * columns + columns - 1, q * EDGE_ROWS

        def wave(offset):
            return cas((last + offset) * modes)

        faces[at + 5] = wave(0) - wave(1)
        faces[at + 6] = wave(-1) - wave(1) - wave(0) + wave(2)
        faces[at + 8] = wave(0)
        faces[at + 9] = wave(1)
    high, low = split_table(plain)
    face_high, face_low = split_table(faces)
    return np.concatenate([high, low, face_high, face_low, face_high], 0)


@functools.cache
def solve_tables():
    radius = NR + np.arange(NR) + 0.5
    arc = 1.0 / (radius * step_angle) ** 2
    up, down = radius + 0.5, radius - 0.5
    up[-1] = 0.0
    down[0] = 0.0
    spectrum = 2.0 - 2.0 * np.cos(step_angle * paired_modes())
    diagonal = radius[:, None] * (shift_plane + arc[:, None] * spectrum[None, :]) + up[:, None] + down[:, None]
    lower = np.broadcast_to(-down[:, None], diagonal.shape)
    upper = np.broadcast_to(-up[:, None], diagonal.shape)

    def moved(x, by, fill):
        filled = np.full((abs(by),) + x.shape[1:], fill)
        return np.concatenate([filled, x[:-by]], 0) if by > 0 else np.concatenate([x[-by:], filled], 0)

    tables, stride = [1.0 / diagonal], 1
    while stride < SUBLANES:
        low = lower / moved(diagonal, stride, 1.0)
        high = upper / moved(diagonal, -stride, 1.0)
        diagonal = diagonal - low * moved(upper, stride, 0.0) - high * moved(lower, -stride, 0.0)
        lower = -low * moved(lower, stride, 0.0)
        upper = -high * moved(upper, -stride, 0.0)
        if stride > 1:
            tables += [low, high]
        stride *= 2
    pivot = diagonal.copy()
    for i in range(SUBLANES, NR):
        pivot[i] = diagonal[i] - upper[i - SUBLANES] ** 2 / pivot[i - SUBLANES]
    middle = np.zeros((NR, 2 * LANES))
    for k, table in enumerate(tables):
        middle[:, k] = table[:, LANES]
    reduction = np.concatenate(tables, 0)
    reduction = np.concatenate([reduction[:, :LANES], reduction[:, 2 * LANES : 3 * LANES]], 1)
    sine = np.broadcast_to(2.0 * np.sin(step_angle * paired_modes()), (SUBLANES, NTH))
    elimination = np.concatenate([1.0 / pivot, upper / pivot, sine] + tables, 0)[:, : 3 * LANES]
    return np.concatenate([reduction, middle], 0).astype(np.float32), elimination.astype(np.float32)


def pieces(x, count):
    out = []
    for _ in range(count):
        part = x.astype(bf16).astype(f32)
        out.append(part)
        x = x - part
    return out


def dot(a, b, contract=((1,), (0,))):
    return lax.dot_general(a, b, (contract, ((), ())), preferred_element_type=f32)


def iota(shape, dim):
    return lax.broadcasted_iota(jnp.int32, shape, dim)


def shifted(x, by):
    length = x.shape[0]
    rolled = pltpu.roll(x, by % length, 0)
    row = iota(x.shape, 0)
    return jnp.where(row >= by if by > 0 else row < length + by, rolled, 0.0)


def pack_kernel(
    capacity, slabs, counts_in, parcels_in, target_in, cell_in, velocity_in, viscosity_in, send, fields,
    counts, parcels, target, cell, spread, hot, sems,
):
    radii3 = velocity_in.shape[0]
    copies = [
        pltpu.make_async_copy(source, target_ref, sems.at[k])
        for k, (source, target_ref) in enumerate(
            (
                (counts_in, counts),
                (target_in, target),
                (parcels_in, parcels),
                (cell_in, cell),
                (velocity_in, fields.at[:radii3]),
                (viscosity_in, fields.at[radii3:]),
            )
        )
    ]
    for copy in copies:
        copy.start()
    rows = parcels.shape[1]
    width = 256
    earlier = (iota((width, width), 0) < iota((width, width), 1)).astype(bf16)
    ones = jnp.ones((width, width), bf16)
    features = FEATURES * capacity
    total = features + 2 * capacity
    copies[0].wait()
    copies[1].wait()
    live = iota((1, rows), 1) < counts[0]
    wanted = jnp.where(live, target[...], -1)
    copies[2].wait()
    copies[3].wait()
    cells = cell[...]
    line = (cells // LANES + 1).astype(f32)
    column = (cells % LANES).astype(f32)
    passed = None
    for block in range(rows // width):
        here = slice(block * width, (block + 1) * width)
        mine = iota((slabs, width), 0) == wanted[:, here]
        mark = mine.astype(f32)
        before = dot(mark.astype(bf16), earlier)
        if passed is not None:
            before = before + dot(passed.astype(bf16), ones)
        passed = mark if passed is None else passed + mark
        slot = jnp.sum(mark * before, axis=0, keepdims=True).astype(jnp.int32)
        chosen = iota((capacity, width), 0) == slot
        hot[:, here] = mark.astype(bf16)
        split = pieces(parcels[:, here], 2)

        def placed(row):
            return jnp.where(chosen, row, 0.0)

        for k, part in enumerate(split):
            base = 0 if k == 0 else total + (k - 1) * features
            for f in range(0, FEATURES, 2):
                pair = jnp.concatenate([placed(part[f : f + 1]), placed(part[f + 1 : f + 2])], 0)
                spread[base + f * capacity : base + (f + 2) * capacity, here] = pair.astype(bf16)
        pair = jnp.concatenate([placed(line[:, here]), placed(column[:, here])], 0)
        spread[features:total, here] = pair.astype(bf16)
    out = dot(spread[...], hot[...], ((1,), (1,)))
    values = out[:features] + out[total:]
    filler = jnp.zeros((send.shape[0] // slabs * LANES - total, slabs), f32)
    whole = jnp.concatenate([values, out[features:total], filler], 0)
    lines = send.shape[0] // slabs
    for c in range(lines):
        send[pl.ds(c, slabs, stride=lines), :] = whole[c * LANES : (c + 1) * LANES].T
    copies[4].wait()
    copies[5].wait()


def hold_kernel(fields, held):
    held[...] = fields[...]


def stencil_kernel(fields, near, far, partial, halves, edges):
    radii = fields.shape[0] // 4
    columns = fields.shape[1]
    radius = iota((radii, columns), 0).astype(f32) + (NR + 0.5)
    arc = 1.0 / (radius * step_angle) ** 2
    lane = iota((radii, columns), 1)
    own = [fields[c * radii : (c + 1) * radii, :] for c in range(4)]

    def around(c):
        x = own[c]
        return (
            near[c * radii : (c + 1) * radii, :],
            far[c * radii : (c + 1) * radii, :],
            shifted(x, -1),
            shifted(x, 1),
            pltpu.roll(x, columns - 1, 1),
            pltpu.roll(x, 1, 1),
        )

    weights = (
        0.5,
        0.5,
        0.5 * (radius + 0.5) / radius,
        0.5 * (radius - 0.5) / radius,
        jnp.where(lane == columns - 1, 0.0, 0.5 * arc),
        jnp.where(lane == 0, 0.0, 0.5 * arc),
    )
    faces = [w * (own[3] + n) for w, n in zip(weights, around(3))]
    for c in range(3):
        u = own[c]
        total = jnp.zeros_like(u)
        for face, beside in zip(faces, around(c)):
            total = total + face * (beside - u)
        partial[c * radii : (c + 1) * radii, :] = u + time_step * total
    edges[...] = jnp.zeros_like(edges)
    for c in range(4):
        put_edges(edges, own[c], c, 4 + c)
        if c < 3:
            parts = [p.astype(bf16) for p in pieces(own[c], 2)]
            halves[c * radii : (c + 1) * radii, :] = jnp.concatenate(parts, 1)


def put_edges(edges, x, first, last):
    turned = x.T
    rest = x.shape[0] - LANES
    for column, row in ((first, turned[:1]), (last, turned[LANES - 1 :])):
        edges[column : column + 1, :] = row[:, :LANES]
        at = 10 + column % 5
        start = column // 5 * rest
        edges[at : at + 1, start : start + rest] = row[:, LANES:]


def momentum_kernel(
    capacity, slabs, received, partial, halves, edges_in, ustar, payload, moved, line_hot, pulled, pushed, edges
):
    lines = received.shape[0] // slabs
    radii = partial.shape[0] // 3
    columns = partial.shape[1]
    turned = jnp.concatenate([received[pl.ds(c, slabs, stride=lines), :].T for c in range(lines)], 0)
    features = FEATURES * capacity
    line_of = turned[features : features + capacity].astype(jnp.int32) - 1
    column_of = turned[features + capacity : features + 2 * capacity].astype(jnp.int32)
    group = 2
    for j in range(0, capacity, group):
        here = slice(j * LANES, (j + group) * LANES)
        lane_line = jnp.concatenate([line_of[s : s + 1] for s in range(j, j + group)], 1)
        lane_column = jnp.concatenate([column_of[s : s + 1] for s in range(j, j + group)], 1)
        match = iota((radii, group * LANES), 0) == lane_line
        line_hot[:, here] = match.astype(bf16)
        hot = (iota((columns, group * LANES), 0) == lane_column).astype(bf16)
        picked = dot(halves[...], jnp.concatenate([hot, hot], 0))
        for c in range(3):
            got = jnp.sum(jnp.where(match, picked[c * radii : (c + 1) * radii], 0.0), axis=0, keepdims=True)
            for s in range(group):
                pulled[c, j + s : j + s + 1, :] = got[:, s * LANES : (s + 1) * LANES]
    fluid = [pulled[c] for c in range(3)]
    drag = [jnp.zeros_like(fluid[0]) for _ in range(3)]
    for k in range(4):
        rate = turned[(4 * k + 3) * capacity : (4 * k + 4) * capacity]
        weight = time_step * rate
        scale = 1.0 / (1.0 + weight)
        moved[(4 * k + 3) * capacity : (4 * k + 4) * capacity, :] = rate
        for c in range(3):
            at = (4 * k + c) * capacity
            after = (turned[at : at + capacity] + weight * fluid[c]) * scale
            moved[at : at + capacity, :] = after
            drag[c] = drag[c] + rate * (after - fluid[c])
    drag = [d.astype(bf16).astype(f32) for d in drag]
    for j in range(capacity):
        match = iota((columns, LANES), 0) == column_of[j : j + 1]
        for c in range(3):
            pushed[c * columns : (c + 1) * columns, j * LANES : (j + 1) * LANES] = jnp.where(
                match, drag[c][j : j + 1], 0.0
            ).astype(bf16)
    deposit = dot(line_hot[...], pushed[...], ((1,), (1,)))
    stars = []
    for c in range(3):
        rows = slice(c * radii, (c + 1) * radii)
        star = partial[rows, :] + time_step * deposit[:, c * columns : (c + 1) * columns]
        ustar[rows, :] = star
        stars.append(star)
    row = iota((radii, columns), 0)
    lane = iota((radii, columns), 1)
    radius = row.astype(f32) + (NR + 0.5)
    flux = jnp.where(row < radii - 1, (radius + 0.5) * 0.5 * (stars[1] + shifted(stars[1], -1)), 0.0)
    ahead = jnp.where(lane == columns - 1, 0.0, pltpu.roll(stars[2], columns - 1, 1))
    behind = jnp.where(lane == 0, 0.0, pltpu.roll(stars[2], 1, 1))
    source = shifted(flux, 1) - flux - (0.5 / step_angle) * (ahead - behind)
    edges[...] = edges_in[...]
    put_edges(edges, stars[2], 8, 9)
    for q in range(payload.shape[0]):
        payload[q, :radii, :] = source
        payload[q, radii:, :] = edges[...]


def project_kernel(gathered, ustar, transform, reduction, elimination_in, out, elimination, state, sem):
    me = lax.axis_index("pa")
    fetch = pltpu.make_async_copy(elimination_in.at[: elimination.shape[0]], elimination, sem)
    fetch.start()
    ring = gathered.shape[0]
    radii = out.shape[0] // 3
    columns = out.shape[1]
    half = NTH // 2

    rows = [gathered[q % ring, radii:, :] for q in range(ring + 1)]
    rows.append(jnp.zeros((LANES - (ring + 1) * EDGE_ROWS, LANES), f32))
    turned = jnp.concatenate(rows, 0).T
    rest = radii - LANES
    fifth = iota((rest, LANES), 1) % EDGE_ROWS < 5
    others = jnp.where(
        fifth, pltpu.roll(turned[:rest], LANES - 10, 1), pltpu.roll(turned[rest : 2 * rest], LANES - 5, 1)
    )

    sides = jnp.concatenate([turned, others], 0)
    row = iota((radii, LANES), 0)
    lane = iota((radii, LANES), 1)
    kind = lane % EDGE_ROWS
    radius = row.astype(f32) + (NR + 0.5)
    inverse = 1.0 / radius

    def lanes_from(x, by):
        return pltpu.roll(x, LANES - by, 1)

    beyond = lanes_from(sides, EDGE_ROWS - 4)
    both = sides + beyond
    face = jnp.where(kind == 4, lanes_from(both, 3), jnp.where(kind == 5, lanes_from(both, 2), lanes_from(both, 1)))
    arc = inverse * inverse * (0.5 * time_step / step_angle**2)
    used = lane < ring * EDGE_ROWS
    crossing = jnp.where(used & (kind >= 4) & (kind < 7), arc * face * (beyond - sides), 0.0)
    flux = jnp.where(row < radii - 1, (radius + 0.5) * 0.5 * (crossing + shifted(crossing, -1)), 0.0)
    outward = shifted(flux, 1) - flux
    turning = 0.5 / step_angle
    coefficients = jnp.where(
        kind == 5,
        outward,
        turning * jnp.where(kind == 6, -crossing, jnp.where(kind == 8, -lanes_from(sides, EDGE_ROWS), sides)),
    )
    used = used & ((kind == 5) | (kind == 6) | (kind == 8) | (kind == 9))
    coefficients = jnp.where(used, coefficients, 0.0)[:, :CORRECTION_ROWS]

    width = 3 * columns
    wide_row = iota((LANES, width), 0)
    wide_lane = iota((LANES, width), 1)
    before = lax.rem(me + ring - 1, ring)
    inside = wide_lane % columns
    at = wide_lane // columns + 4
    pick = jnp.where((inside == columns - 1) & (wide_row == at + me * EDGE_ROWS), 1.0, 0.0) - jnp.where(
        (inside == 0) & (wide_row == at + before * EDGE_ROWS), 1.0, 0.0
    )
    pick = pick.astype(bf16)
    crossing_parts = [p.astype(bf16) for p in pieces(crossing, 2)]
    delta = dot(jnp.concatenate(crossing_parts, 1), jnp.concatenate([pick, pick], 0))

    near = jnp.concatenate([gathered[q, :radii, :] for q in range(ring // 2)], 1)
    distant = jnp.concatenate([gathered[q, :radii, :] for q in range(ring // 2, ring)], 1)

    def forward(x, cols):
        high, low = [p.astype(bf16) for p in pieces(x, 2)]
        table_high, table_low = transform[:half, cols], transform[half : 2 * half, cols]
        return dot(high, table_high) + (dot(high, table_low) + dot(low, table_high)) + dot(corrections, transform[2 * half :, cols])

    parts = [p.astype(bf16) for p in pieces(coefficients, 2)]
    corrections = jnp.concatenate([parts[0], parts[0], parts[1]], 1)
    even = slice(0, half)
    odd = slice(half, NTH)
    modes_even = forward(near + distant, even)
    modes_odd = forward(near - distant, odd)
    blocks = [m[:, b * LANES : (b + 1) * LANES] for m in (modes_even, modes_odd) for b in range(2)]
    total = sum(NR + i + 0.5 for i in range(NR))
    mean = jnp.sum(blocks[0], axis=0, keepdims=True) * (1.0 / total)
    blocks[0] = blocks[0] - radius * jnp.where(iota((1, LANES), 1) == 0, mean, 0.0)
    middle = reduction[5 * radii :, :LANES]

    def factor(k, b):
        table = reduction[k * radii : (k + 1) * radii, b // 2 * LANES : (b // 2 + 1) * LANES]
        return jnp.where(lane == 0, pltpu.roll(middle, (LANES - k) % LANES, 1), table) if b == 1 else table

    inner = jnp.where(row > 0, radius - 0.5, 0.0)
    outer = jnp.where(row < radii - 1, radius + 0.5, 0.0)
    for b in range(ring):
        x = blocks[b]
        scaled = x * factor(0, b)
        x = x + inner * pltpu.roll(scaled, 1, 0) + outer * pltpu.roll(scaled, radii - 1, 0)
        for stride, k in ((2, 1), (4, 3)):
            x = x - factor(k, b) * pltpu.roll(x, stride, 0) - factor(k + 1, b) * pltpu.roll(x, radii - stride, 0)
        state[:, b * LANES : (b + 1) * LANES] = x
    fetch.wait()

    def factors(k, v):
        at = k * radii + v * SUBLANES
        table = elimination[at : at + SUBLANES, :]
        return jnp.concatenate([table, table[:, 2 * LANES :]], 1)

    steps = radii // SUBLANES
    y = state[:SUBLANES, :]
    for v in range(1, steps):
        rows = slice(v * SUBLANES, (v + 1) * SUBLANES)
        y = state[rows, :] - factors(1, v - 1) * y
        state[rows, :] = y
    x = y * factors(0, steps - 1)
    state[(steps - 1) * SUBLANES :, :] = x
    for v in range(steps - 2, -1, -1):
        rows = slice(v * SUBLANES, (v + 1) * SUBLANES)
        x = state[rows, :] * factors(0, v) - factors(1, v) * x
        state[rows, :] = x

    potential = [state[:, b * LANES : (b + 1) * LANES] for b in range(ring)]

    def gradient(x):
        above = jnp.where(row == radii - 1, x, pltpu.roll(x, radii - 1, 0))
        below = jnp.where(row == 0, x, pltpu.roll(x, 1, 0))
        return above - below

    mine = pl.multiple_of(me % 2 * columns, columns)
    result = []
    for group, cols in ((0, even), (1, odd)):
        plain, mirror = potential[2 * group], potential[2 * group + 1]
        sine = elimination[2 * radii : 2 * radii + 1, 2 * group * LANES : (2 * group + 1) * LANES]
        slopes = jnp.concatenate([gradient(plain), gradient(mirror)], 1)
        turns = jnp.concatenate([-sine * mirror, sine * plain], 1)
        high, low = [p.astype(bf16) for p in pieces(jnp.concatenate([slopes, turns], 0), 2)]
        own_high, own_low = transform[pl.ds(mine, columns), cols], transform[pl.ds(half + mine, columns), cols]
        both = dot(high, jnp.concatenate([own_high, own_low], 0), ((1,), (1,)))
        result.append(both[:, :columns] + (both[:, columns:] + dot(low, own_high, ((1,), (1,)))))
    result = result[0] + jnp.where(me >= ring // 2, -1.0, 1.0) * result[1]
    out[:radii, :] = ustar[:radii, :] + delta[:, :columns]
    out[radii : 2 * radii, :] = ustar[radii : 2 * radii, :] + delta[:, columns : 2 * columns] - result[:radii] * (0.5 / NTH)
    out[2 * radii :, :] = ustar[2 * radii :, :] + delta[:, 2 * columns :] - result[radii:] * (inverse * (turning / NTH))


def place_kernel(capacity, slabs, moved, out):
    rows = slabs * capacity
    width = 768
    split = jnp.concatenate([p.astype(bf16) for p in pieces(moved[...], 3)], 1)
    for start in range(0, rows, width):
        place = start + iota((slabs, width), 1)
        hot = (place // capacity == iota((slabs, width), 0)).astype(bf16)
        spread = dot(split, jnp.concatenate([hot, hot, hot], 0))
        match = (start + iota((capacity, width), 1)) % capacity == iota((capacity, width), 0)
        for f in range(FEATURES):
            block = spread[f * capacity : (f + 1) * capacity]
            out[f : f + 1, start : start + width] = jnp.sum(jnp.where(match, block, 0.0), axis=0, keepdims=True)


def shape(*dims):
    return jax.ShapeDtypeStruct(dims, f32)


def params(mib):
    return pltpu.CompilerParams(vmem_limit_bytes=int(mib * 1024 * 1024))


def cost(microseconds):
    return pl.CostEstimate(flops=0, bytes_accessed=int(microseconds * 3.0e6), transcendentals=0)


def body(velocity, viscosity, parcels, dest_rank, dest_cell, counts):
    slabs = lax.axis_size("gz")
    ring = lax.axis_size("pa")
    planes, radii, columns = viscosity.shape
    block = parcels.shape[0]
    capacity = 3 * block // slabs
    lines = -(-(FEATURES + 2) * capacity // LANES)
    vmem = pl.BlockSpec(memory_space=pltpu.VMEM)
    hbm = pl.BlockSpec(memory_space=pltpu.HBM)
    u = velocity.reshape(3 * radii, columns)
    nu = viscosity.reshape(radii, columns)
    features = FEATURES * capacity
    send, fields = pl.pallas_call(
        functools.partial(pack_kernel, capacity, slabs),
        out_shape=(shape(slabs * lines, LANES), shape(4 * radii, columns)),
        in_specs=[hbm] * 6,
        out_specs=(vmem,) * 2,
        scratch_shapes=[
            pltpu.SMEM((1,), jnp.int32),
            pltpu.VMEM((FEATURES, block), f32),
            pltpu.VMEM((1, block), jnp.int32),
            pltpu.VMEM((1, block), jnp.int32),
            pltpu.VMEM((2 * features + 2 * capacity, block), bf16),
            pltpu.VMEM((slabs, block), bf16),
            pltpu.SemaphoreType.DMA((6,)),
        ],
        compiler_params=params(60),
        cost_estimate=cost(3),
        name="pack",
    )(counts, parcels.T, dest_rank.reshape(1, block), dest_cell.reshape(1, block), u, nu)
    received = lax.all_to_all(
        send.reshape(slabs, lines, LANES), "gz", split_axis=0, concat_axis=0, tiled=True
    ).reshape(slabs * lines, LANES)

    near = lax.ppermute(fields, "gz", [(i, i ^ 1) for i in range(slabs)])
    pairs = [(i, i + 1) for i in range(1, slabs - 1, 2)]
    far = lax.ppermute(fields, "gz", pairs + [(j, i) for i, j in pairs])
    transform = jnp.asarray(transform_table(ring, columns))
    reduction, elimination = [jnp.asarray(table) for table in solve_tables()]
    held = pl.pallas_call(
        hold_kernel,
        out_shape=shape(*fields.shape),
        in_specs=[vmem],
        out_specs=vmem,
        compiler_params=params(16),
        cost_estimate=cost(1),
        name="hold",
    )(fields)
    partial, halves, edges = pl.pallas_call(
        stencil_kernel,
        out_shape=(
            shape(3 * radii, columns),
            jax.ShapeDtypeStruct((3 * radii, 2 * columns), bf16),
            shape(EDGE_ROWS, LANES),
        ),
        in_specs=[vmem] * 3,
        out_specs=(vmem,) * 3,
        compiler_params=params(16),
        cost_estimate=cost(2),
        name="stencil",
    )(held, near, far)

    ustar, payload, moved = pl.pallas_call(
        functools.partial(momentum_kernel, capacity, slabs),
        out_shape=(
            shape(3 * radii, columns),
            shape(ring, radii + EDGE_ROWS, columns),
            shape(features, slabs),
        ),
        in_specs=[vmem] * 4,
        out_specs=(vmem,) * 3,
        scratch_shapes=[
            pltpu.VMEM((radii, capacity * slabs), bf16),
            pltpu.VMEM((3, capacity, slabs), f32),
            pltpu.VMEM((3 * columns, capacity * slabs), bf16),
            pltpu.VMEM((EDGE_ROWS, LANES), f32),
        ],
        compiler_params=params(16),
        cost_estimate=cost(4),
        name="momentum",
    )(received, partial, halves, edges)

    gathered = lax.all_to_all(payload, "pa", split_axis=0, concat_axis=0, tiled=True)
    parcels_out = pl.pallas_call(
        functools.partial(place_kernel, capacity, slabs),
        out_shape=shape(FEATURES, slabs * capacity),
        in_specs=[vmem],
        out_specs=vmem,
        compiler_params=params(16),
        cost_estimate=cost(3),
        name="place",
    )(moved)
    velocity_out = pl.pallas_call(
        project_kernel,
        out_shape=shape(3 * radii, columns),
        in_specs=[vmem] * 4 + [hbm],
        out_specs=vmem,
        scratch_shapes=[
            pltpu.VMEM((2 * radii + SUBLANES, elimination.shape[1]), f32),
            pltpu.VMEM((radii, NTH), f32),
            pltpu.SemaphoreType.DMA,
        ],
        compiler_params=params(51.25),
        cost_estimate=cost(5),
        name="project",
    )(gathered, ustar, transform, reduction, elimination)
    return velocity_out.reshape(velocity.shape), parcels_out.T


def solution(mesh):
    in_specs = (
        P(None, "gz", None, "pa"),
        P("gz", None, "pa"),
        P(("gz", "pa"), None),
        P(("gz", "pa"), None),
        P(("gz", "pa")),
        P(("gz", "pa")),
    )
    out_specs = (P(None, "gz", None, "pa"), P(("gz", "pa"), None))
    return jax.shard_map(body, mesh=mesh, in_specs=in_specs, out_specs=out_specs, check_vma=False)
```

```python
import functools
import math

import jax
import jax.numpy as jnp
import numpy as np
from jax import lax
from jax.experimental import pallas as pl
from jax.experimental.pallas import tpu as pltpu
from jax.sharding import PartitionSpec as P

NR = 192
NTH = 512
time_step = 0.1
shift_plane = 0.0001
step_angle = 2.0 * math.pi / NTH
LANES = 128
FEATURES = 16
SUBLANES = 8
EDGE_ROWS = 16
CORRECTION_ROWS = 64
f32 = jnp.float32
bf16 = jnp.bfloat16


def cas(numbers):
    phase = 2.0 * np.pi / NTH * (numbers % NTH)
    return np.cos(phase) + np.sin(phase)


def paired_modes():
    half, even, odd = NTH // 2, np.arange(0, NTH // 2, 2), np.arange(1, NTH // 2, 2)
    return np.concatenate([even, [half], NTH - even[1:], odd, NTH - odd])


def split_table(table):
    high = table.astype(jnp.bfloat16)
    return high, (table - high.astype(np.float64)).astype(jnp.bfloat16)


@functools.cache
def transform_table(ring, columns):
    modes = paired_modes()[None, :]
    plain = cas(np.arange(NTH // 2)[:, None] * modes)
    faces = np.zeros((CORRECTION_ROWS, NTH))
    for q in range(ring):
        last, at = q * columns + columns - 1, q * EDGE_ROWS

        def wave(offset):
            return cas((last + offset) * modes)

        faces[at + 5] = wave(0) - wave(1)
        faces[at + 6] = wave(-1) - wave(1) - wave(0) + wave(2)
        faces[at + 8] = wave(0)
        faces[at + 9] = wave(1)
    high, low = split_table(plain)
    face_high, face_low = split_table(faces)
    return np.concatenate([high, low, face_high, face_low, face_high], 0)


@functools.cache
def solve_tables():
    radius = NR + np.arange(NR) + 0.5
    arc = 1.0 / (radius * step_angle) ** 2
    up, down = radius + 0.5, radius - 0.5
    up[-1] = 0.0
    down[0] = 0.0
    spectrum = 2.0 - 2.0 * np.cos(step_angle * paired_modes())
    diagonal = radius[:, None] * (shift_plane + arc[:, None] * spectrum[None, :]) + up[:, None] + down[:, None]
    lower = np.broadcast_to(-down[:, None], diagonal.shape)
    upper = np.broadcast_to(-up[:, None], diagonal.shape)

    def moved(x, by, fill):
        filled = np.full((abs(by),) + x.shape[1:], fill)
        return np.concatenate([filled, x[:-by]], 0) if by > 0 else np.concatenate([x[-by:], filled], 0)

    tables, stride = [1.0 / diagonal], 1
    while stride < SUBLANES:
        low = lower / moved(diagonal, stride, 1.0)
        high = upper / moved(diagonal, -stride, 1.0)
        diagonal = diagonal - low * moved(upper, stride, 0.0) - high * moved(lower, -stride, 0.0)
        lower = -low * moved(lower, stride, 0.0)
        upper = -high * moved(upper, -stride, 0.0)
        if stride > 1:
            tables += [low, high]
        stride *= 2
    pivot = diagonal.copy()
    for i in range(SUBLANES, NR):
        pivot[i] = diagonal[i] - upper[i - SUBLANES] ** 2 / pivot[i - SUBLANES]
    middle = np.zeros((NR, 2 * LANES))
    for k, table in enumerate(tables):
        middle[:, k] = table[:, LANES]
    reduction = np.concatenate(tables, 0)
    reduction = np.concatenate([reduction[:, :LANES], reduction[:, 2 * LANES : 3 * LANES]], 1)
    sine = np.broadcast_to(2.0 * np.sin(step_angle * paired_modes()), (SUBLANES, NTH))
    elimination = np.concatenate([1.0 / pivot, upper / pivot, sine] + tables, 0)[:, : 3 * LANES]
    return np.concatenate([reduction, middle], 0).astype(np.float32), elimination.astype(np.float32)


def pieces(x, count):
    out = []
    for _ in range(count):
        part = x.astype(bf16).astype(f32)
        out.append(part)
        x = x - part
    return out


def dot(a, b, contract=((1,), (0,))):
    return lax.dot_general(a, b, (contract, ((), ())), preferred_element_type=f32)


def iota(shape, dim):
    return lax.broadcasted_iota(jnp.int32, shape, dim)


def shifted(x, by):
    length = x.shape[0]
    rolled = pltpu.roll(x, by % length, 0)
    row = iota(x.shape, 0)
    return jnp.where(row >= by if by > 0 else row < length + by, rolled, 0.0)


def pack_kernel(
    capacity, slabs, counts_in, parcels_in, target_in, cell_in, velocity_in, viscosity_in, send, fields,
    counts, parcels, target, cell, spread, hot, sems,
):
    radii3 = velocity_in.shape[0]
    copies = [
        pltpu.make_async_copy(source, target_ref, sems.at[k])
        for k, (source, target_ref) in enumerate(
            (
                (counts_in, counts),
                (target_in, target),
                (parcels_in, parcels),
                (cell_in, cell),
                (velocity_in, fields.at[:radii3]),
                (viscosity_in, fields.at[radii3:]),
            )
        )
    ]
    for copy in copies:
        copy.start()
    rows = parcels.shape[1]
    width = 256
    earlier = (iota((width, width), 0) < iota((width, width), 1)).astype(bf16)
    ones = jnp.ones((width, width), bf16)
    thirds = capacity // SUBLANES
    features = FEATURES * SUBLANES
    total = features + 2 * SUBLANES
    copies[0].wait()
    copies[1].wait()
    live = iota((1, rows), 1) < counts[0]
    wanted = jnp.where(live, target[...], -1)
    copies[2].wait()
    copies[3].wait()
    cells = cell[...]
    line = (cells // LANES + 1).astype(f32)
    column = (cells % LANES).astype(f32)
    passed = None
    for block in range(rows // width):
        here = slice(block * width, (block + 1) * width)
        mine = iota((slabs, width), 0) == wanted[:, here]
        mark = mine.astype(f32)
        before = dot(mark.astype(bf16), earlier)
        if passed is not None:
            before = before + dot(passed.astype(bf16), ones)
        passed = mark if passed is None else passed + mark
        slot = jnp.sum(mark * before, axis=0, keepdims=True).astype(jnp.int32)
        chosen = iota((SUBLANES, width), 0) == slot % SUBLANES
        for h in range(thirds):
            hot[h * slabs : (h + 1) * slabs, here] = jnp.where(slot // SUBLANES == h, mark, 0.0).astype(bf16)
        split = pieces(parcels[:, here], 2)

        def placed(row):
            return jnp.where(chosen, row, 0.0)

        for k, part in enumerate(split):
            base = 0 if k == 0 else total + (k - 1) * features
            for f in range(0, FEATURES, 2):
                pair = jnp.concatenate([placed(part[f : f + 1]), placed(part[f + 1 : f + 2])], 0)
                spread[base + f * SUBLANES : base + (f + 2) * SUBLANES, here] = pair.astype(bf16)
        pair = jnp.concatenate([placed(line[:, here]), placed(column[:, here])], 0)
        spread[features:total, here] = pair.astype(bf16)
    out = dot(spread[...], hot[...], ((1,), (1,)))
    values = jnp.concatenate([out[:features] + out[total:], out[features:total]], 0)
    words = [
        values[at : at + SUBLANES, h * slabs : (h + 1) * slabs] for at in range(0, total, SUBLANES) for h in range(thirds)
    ]
    lines = send.shape[0] // slabs
    words.append(jnp.zeros((lines * LANES - total * thirds, slabs), f32))
    whole = jnp.concatenate(words, 0)
    for c in range(lines):
        send[pl.ds(c, slabs, stride=lines), :] = whole[c * LANES : (c + 1) * LANES].T
    copies[4].wait()
    copies[5].wait()


def hold_kernel(fields, held):
    held[...] = fields[...]


def stencil_kernel(fields, near, far, partial, halves, edges):
    radii = fields.shape[0] // 4
    columns = fields.shape[1]
    radius = iota((radii, columns), 0).astype(f32) + (NR + 0.5)
    arc = 1.0 / (radius * step_angle) ** 2
    lane = iota((radii, columns), 1)
    own = [fields[c * radii : (c + 1) * radii, :] for c in range(4)]

    def around(c):
        x = own[c]
        return (
            near[c * radii : (c + 1) * radii, :],
            far[c * radii : (c + 1) * radii, :],
            shifted(x, -1),
            shifted(x, 1),
            pltpu.roll(x, columns - 1, 1),
            pltpu.roll(x, 1, 1),
        )

    weights = (
        0.5,
        0.5,
        0.5 * (radius + 0.5) / radius,
        0.5 * (radius - 0.5) / radius,
        jnp.where(lane == columns - 1, 0.0, 0.5 * arc),
        jnp.where(lane == 0, 0.0, 0.5 * arc),
    )
    faces = [w * (own[3] + n) for w, n in zip(weights, around(3))]
    for c in range(3):
        u = own[c]
        total = jnp.zeros_like(u)
        for face, beside in zip(faces, around(c)):
            total = total + face * (beside - u)
        partial[c * radii : (c + 1) * radii, :] = u + time_step * total
    edges[...] = jnp.zeros_like(edges)
    for c in range(4):
        put_edges(edges, own[c], c, 4 + c)
        if c < 3:
            parts = [p.astype(bf16) for p in pieces(own[c], 2)]
            halves[c * radii : (c + 1) * radii, :] = jnp.concatenate(parts, 1)


def put_edges(edges, x, first, last):
    turned = x.T
    rest = x.shape[0] - LANES
    for column, row in ((first, turned[:1]), (last, turned[LANES - 1 :])):
        edges[column : column + 1, :] = row[:, :LANES]
        at = 10 + column % 5
        start = column // 5 * rest
        edges[at : at + 1, start : start + rest] = row[:, LANES:]


def momentum_kernel(
    capacity, slabs, received, partial, halves, edges_in, ustar, payload, moved, line_hot, pulled, pushed, edges
):
    lines = received.shape[0] // slabs
    radii = partial.shape[0] // 3
    columns = partial.shape[1]
    turned = jnp.concatenate([received[pl.ds(c, slabs, stride=lines), :].T for c in range(lines)], 0)
    features = FEATURES * capacity
    line_of = turned[features : features + capacity].astype(jnp.int32) - 1
    column_of = turned[features + capacity : features + 2 * capacity].astype(jnp.int32)
    group = 2
    for j in range(0, capacity, group):
        here = slice(j * LANES, (j + group) * LANES)
        lane_line = jnp.concatenate([line_of[s : s + 1] for s in range(j, j + group)], 1)
        lane_column = jnp.concatenate([column_of[s : s + 1] for s in range(j, j + group)], 1)
        match = iota((radii, group * LANES), 0) == lane_line
        line_hot[:, here] = match.astype(bf16)
        hot = (iota((columns, group * LANES), 0) == lane_column).astype(bf16)
        picked = dot(halves[...], jnp.concatenate([hot, hot], 0))
        for c in range(3):
            got = jnp.sum(jnp.where(match, picked[c * radii : (c + 1) * radii], 0.0), axis=0, keepdims=True)
            for s in range(group):
                pulled[c, j + s : j + s + 1, :] = got[:, s * LANES : (s + 1) * LANES]
    fluid = [pulled[c] for c in range(3)]
    drag = [jnp.zeros_like(fluid[0]) for _ in range(3)]
    for k in range(4):
        rate = turned[(4 * k + 3) * capacity : (4 * k + 4) * capacity]
        weight = time_step * rate
        scale = 1.0 / (1.0 + weight)
        moved[(4 * k + 3) * capacity : (4 * k + 4) * capacity, :] = rate
        for c in range(3):
            at = (4 * k + c) * capacity
            after = (turned[at : at + capacity] + weight * fluid[c]) * scale
            moved[at : at + capacity, :] = after
            drag[c] = drag[c] + rate * (after - fluid[c])
    drag = [d.astype(bf16).astype(f32) for d in drag]
    for j in range(capacity):
        match = iota((columns, LANES), 0) == column_of[j : j + 1]
        for c in range(3):
            pushed[c * columns : (c + 1) * columns, j * LANES : (j + 1) * LANES] = jnp.where(
                match, drag[c][j : j + 1], 0.0
            ).astype(bf16)
    deposit = dot(line_hot[...], pushed[...], ((1,), (1,)))
    stars = []
    for c in range(3):
        rows = slice(c * radii, (c + 1) * radii)
        star = partial[rows, :] + time_step * deposit[:, c * columns : (c + 1) * columns]
        ustar[rows, :] = star
        stars.append(star)
    row = iota((radii, columns), 0)
    lane = iota((radii, columns), 1)
    radius = row.astype(f32) + (NR + 0.5)
    flux = jnp.where(row < radii - 1, (radius + 0.5) * 0.5 * (stars[1] + shifted(stars[1], -1)), 0.0)
    ahead = jnp.where(lane == columns - 1, 0.0, pltpu.roll(stars[2], columns - 1, 1))
    behind = jnp.where(lane == 0, 0.0, pltpu.roll(stars[2], 1, 1))
    source = shifted(flux, 1) - flux - (0.5 / step_angle) * (ahead - behind)
    edges[...] = edges_in[...]
    put_edges(edges, stars[2], 8, 9)
    for q in range(payload.shape[0]):
        payload[q, :radii, :] = source
        payload[q, radii:, :] = edges[...]


def project_kernel(gathered, ustar, transform, reduction, elimination_in, out_hbm, elimination, state, out, sems):
    me = lax.axis_index("pa")
    fetch = pltpu.make_async_copy(elimination_in.at[: elimination.shape[0]], elimination, sems.at[0])
    fetch.start()
    ring = gathered.shape[0]
    radii = out.shape[0] // 3
    columns = out.shape[1]
    half = NTH // 2

    rows = [gathered[q % ring, radii:, :] for q in range(ring + 1)]
    rows.append(jnp.zeros((LANES - (ring + 1) * EDGE_ROWS, LANES), f32))
    turned = jnp.concatenate(rows, 0).T
    rest = radii - LANES
    fifth = iota((rest, LANES), 1) % EDGE_ROWS < 5
    others = jnp.where(
        fifth, pltpu.roll(turned[:rest], LANES - 10, 1), pltpu.roll(turned[rest : 2 * rest], LANES - 5, 1)
    )

    sides = jnp.concatenate([turned, others], 0)
    row = iota((radii, LANES), 0)
    lane = iota((radii, LANES), 1)
    kind = lane % EDGE_ROWS
    radius = row.astype(f32) + (NR + 0.5)
    inverse = 1.0 / radius

    def lanes_from(x, by):
        return pltpu.roll(x, LANES - by, 1)

    beyond = lanes_from(sides, EDGE_ROWS - 4)
    both = sides + beyond
    face = jnp.where(kind == 4, lanes_from(both, 3), jnp.where(kind == 5, lanes_from(both, 2), lanes_from(both, 1)))
    arc = inverse * inverse * (0.5 * time_step / step_angle**2)
    used = lane < ring * EDGE_ROWS
    crossing = jnp.where(used & (kind >= 4) & (kind < 7), arc * face * (beyond - sides), 0.0)
    flux = jnp.where(row < radii - 1, (radius + 0.5) * 0.5 * (crossing + shifted(crossing, -1)), 0.0)
    outward = shifted(flux, 1) - flux
    turning = 0.5 / step_angle
    coefficients = jnp.where(
        kind == 5,
        outward,
        turning * jnp.where(kind == 6, -crossing, jnp.where(kind == 8, -lanes_from(sides, EDGE_ROWS), sides)),
    )
    used = used & ((kind == 5) | (kind == 6) | (kind == 8) | (kind == 9))
    coefficients = jnp.where(used, coefficients, 0.0)[:, :CORRECTION_ROWS]

    width = 3 * columns
    wide_row = iota((LANES, width), 0)
    wide_lane = iota((LANES, width), 1)
    before = lax.rem(me + ring - 1, ring)
    inside = wide_lane % columns
    at = wide_lane // columns + 4
    pick = jnp.where((inside == columns - 1) & (wide_row == at + me * EDGE_ROWS), 1.0, 0.0) - jnp.where(
        (inside == 0) & (wide_row == at + before * EDGE_ROWS), 1.0, 0.0
    )
    pick = pick.astype(bf16)
    crossing_parts = [p.astype(bf16) for p in pieces(crossing, 2)]
    delta = dot(jnp.concatenate(crossing_parts, 1), jnp.concatenate([pick, pick], 0))

    out[:radii, :] = ustar[:radii, :] + delta[:, :columns]
    whole = [pltpu.make_async_copy(out.at[k : k + radii], out_hbm.at[k : k + radii], sems.at[1 + k // radii]) for k in range(0, 3 * radii, radii)]
    whole[0].start()
    near = jnp.concatenate([gathered[q, :radii, :] for q in range(ring // 2)], 1)
    distant = jnp.concatenate([gathered[q, :radii, :] for q in range(ring // 2, ring)], 1)

    def forward(x, cols):
        high, low = [p.astype(bf16) for p in pieces(x, 2)]
        table_high, table_low = transform[:half, cols], transform[half : 2 * half, cols]
        return dot(high, table_high) + (dot(high, table_low) + dot(low, table_high)) + dot(corrections, transform[2 * half :, cols])

    parts = [p.astype(bf16) for p in pieces(coefficients, 2)]
    corrections = jnp.concatenate([parts[0], parts[0], parts[1]], 1)
    even = slice(0, half)
    odd = slice(half, NTH)
    modes_even = forward(near + distant, even)
    modes_odd = forward(near - distant, odd)
    blocks = [m[:, b * LANES : (b + 1) * LANES] for m in (modes_even, modes_odd) for b in range(2)]
    total = sum(NR + i + 0.5 for i in range(NR))
    mean = jnp.sum(blocks[0], axis=0, keepdims=True) * (1.0 / total)
    blocks[0] = blocks[0] - radius * jnp.where(iota((1, LANES), 1) == 0, mean, 0.0)
    middle = reduction[5 * radii :, :LANES]

    def factor(k, b):
        table = reduction[k * radii : (k + 1) * radii, b // 2 * LANES : (b // 2 + 1) * LANES]
        return jnp.where(lane == 0, pltpu.roll(middle, (LANES - k) % LANES, 1), table) if b == 1 else table

    inner = jnp.where(row > 0, radius - 0.5, 0.0)
    outer = jnp.where(row < radii - 1, radius + 0.5, 0.0)
    for b in range(ring):
        x = blocks[b]
        scaled = x * factor(0, b)
        x = x + inner * pltpu.roll(scaled, 1, 0) + outer * pltpu.roll(scaled, radii - 1, 0)
        for stride, k in ((2, 1), (4, 3)):
            x = x - factor(k, b) * pltpu.roll(x, stride, 0) - factor(k + 1, b) * pltpu.roll(x, radii - stride, 0)
        state[:, b * LANES : (b + 1) * LANES] = x
    fetch.wait()

    def factors(k, v):
        at = k * radii + v * SUBLANES
        table = elimination[at : at + SUBLANES, :]
        return jnp.concatenate([table, table[:, 2 * LANES :]], 1)

    steps = radii // SUBLANES
    y = state[:SUBLANES, :]
    for v in range(1, steps):
        rows = slice(v * SUBLANES, (v + 1) * SUBLANES)
        y = state[rows, :] - factors(1, v - 1) * y
        state[rows, :] = y
    x = y * factors(0, steps - 1)
    state[(steps - 1) * SUBLANES :, :] = x
    for v in range(steps - 2, -1, -1):
        rows = slice(v * SUBLANES, (v + 1) * SUBLANES)
        x = state[rows, :] * factors(0, v) - factors(1, v) * x
        state[rows, :] = x

    potential = [state[:, b * LANES : (b + 1) * LANES] for b in range(ring)]

    def gradient(x):
        above = jnp.where(row == radii - 1, x, pltpu.roll(x, radii - 1, 0))
        below = jnp.where(row == 0, x, pltpu.roll(x, 1, 0))
        return above - below

    mine = pl.multiple_of(me % 2 * columns, columns)
    result = []
    for group, cols in ((0, even), (1, odd)):
        plain, mirror = potential[2 * group], potential[2 * group + 1]
        sine = elimination[2 * radii : 2 * radii + 1, 2 * group * LANES : (2 * group + 1) * LANES]
        slopes = jnp.concatenate([gradient(plain), gradient(mirror)], 1)
        turns = jnp.concatenate([-sine * mirror, sine * plain], 1)
        high, low = [p.astype(bf16) for p in pieces(jnp.concatenate([slopes, turns], 0), 2)]
        own_high, own_low = transform[pl.ds(mine, columns), cols], transform[pl.ds(half + mine, columns), cols]
        both = dot(high, jnp.concatenate([own_high, own_low], 0), ((1,), (1,)))
        result.append(both[:, :columns] + (both[:, columns:] + dot(low, own_high, ((1,), (1,)))))
    result = result[0] + jnp.where(me >= ring // 2, -1.0, 1.0) * result[1]
    out[radii : 2 * radii, :] = ustar[radii : 2 * radii, :] + delta[:, columns : 2 * columns] - result[:radii] * (0.5 / NTH)
    whole[1].start()
    out[2 * radii :, :] = ustar[2 * radii :, :] + delta[:, 2 * columns :] - result[radii:] * (inverse * (turning / NTH))
    whole[2].start()
    for copy in whole:
        copy.wait()


def place_kernel(capacity, slabs, moved, out):
    rows = slabs * capacity
    width = 768
    split = jnp.concatenate([p.astype(bf16) for p in pieces(moved[...], 3)], 1)
    for start in range(0, rows, width):
        place = start + iota((slabs, width), 1)
        hot = (place // capacity == iota((slabs, width), 0)).astype(bf16)
        spread = dot(split, jnp.concatenate([hot, hot, hot], 0))
        match = (start + iota((capacity, width), 1)) % capacity == iota((capacity, width), 0)
        for f in range(FEATURES):
            block = spread[f * capacity : (f + 1) * capacity]
            out[f : f + 1, start : start + width] = jnp.sum(jnp.where(match, block, 0.0), axis=0, keepdims=True)


def shape(*dims):
    return jax.ShapeDtypeStruct(dims, f32)


def params(mib):
    return pltpu.CompilerParams(vmem_limit_bytes=int(mib * 1024 * 1024))


def cost(microseconds):
    return pl.CostEstimate(flops=0, bytes_accessed=int(microseconds * 3.0e6), transcendentals=0)


def body(velocity, viscosity, parcels, dest_rank, dest_cell, counts):
    slabs = lax.axis_size("gz")
    ring = lax.axis_size("pa")
    planes, radii, columns = viscosity.shape
    block = parcels.shape[0]
    capacity = 3 * block // slabs
    lines = -(-(FEATURES + 2) * capacity // LANES)
    vmem = pl.BlockSpec(memory_space=pltpu.VMEM)
    hbm = pl.BlockSpec(memory_space=pltpu.HBM)
    u = velocity.reshape(3 * radii, columns)
    nu = viscosity.reshape(radii, columns)
    features = FEATURES * capacity
    send, fields = pl.pallas_call(
        functools.partial(pack_kernel, capacity, slabs),
        out_shape=(shape(slabs * lines, LANES), shape(4 * radii, columns)),
        in_specs=[hbm] * 6,
        out_specs=(vmem,) * 2,
        scratch_shapes=[
            pltpu.SMEM((1,), jnp.int32),
            pltpu.VMEM((FEATURES, block), f32),
            pltpu.VMEM((1, block), jnp.int32),
            pltpu.VMEM((1, block), jnp.int32),
            pltpu.VMEM((2 * (FEATURES + 1) * SUBLANES, block), bf16),
            pltpu.VMEM((capacity // SUBLANES * slabs, block), bf16),
            pltpu.SemaphoreType.DMA((6,)),
        ],
        compiler_params=params(60),
        cost_estimate=cost(3),
        name="pack",
    )(counts, parcels.T, dest_rank.reshape(1, block), dest_cell.reshape(1, block), u, nu)
    received = lax.all_to_all(
        send.reshape(slabs, lines, LANES), "gz", split_axis=0, concat_axis=0, tiled=True
    ).reshape(slabs * lines, LANES)

    near = lax.ppermute(fields, "gz", [(i, i ^ 1) for i in range(slabs)])
    pairs = [(i, i + 1) for i in range(1, slabs - 1, 2)]
    far = lax.ppermute(fields, "gz", pairs + [(j, i) for i, j in pairs])
    transform = jnp.asarray(transform_table(ring, columns))
    reduction, elimination = [jnp.asarray(table) for table in solve_tables()]
    held = pl.pallas_call(
        hold_kernel,
        out_shape=shape(*fields.shape),
        in_specs=[vmem],
        out_specs=vmem,
        compiler_params=params(16),
        cost_estimate=cost(1),
        name="hold",
    )(fields)
    partial, halves, edges = pl.pallas_call(
        stencil_kernel,
        out_shape=(
            shape(3 * radii, columns),
            jax.ShapeDtypeStruct((3 * radii, 2 * columns), bf16),
            shape(EDGE_ROWS, LANES),
        ),
        in_specs=[vmem] * 3,
        out_specs=(vmem,) * 3,
        compiler_params=params(16),
        cost_estimate=cost(2),
        name="stencil",
    )(held, near, far)

    ustar, payload, moved = pl.pallas_call(
        functools.partial(momentum_kernel, capacity, slabs),
        out_shape=(
            shape(3 * radii, columns),
            shape(ring, radii + EDGE_ROWS, columns),
            shape(features, slabs),
        ),
        in_specs=[vmem] * 4,
        out_specs=(vmem,) * 3,
        scratch_shapes=[
            pltpu.VMEM((radii, capacity * slabs), bf16),
            pltpu.VMEM((3, capacity, slabs), f32),
            pltpu.VMEM((3 * columns, capacity * slabs), bf16),
            pltpu.VMEM((EDGE_ROWS, LANES), f32),
        ],
        compiler_params=params(16),
        cost_estimate=cost(4),
        name="momentum",
    )(received, partial, halves, edges)

    gathered = lax.all_to_all(payload, "pa", split_axis=0, concat_axis=0, tiled=True)
    parcels_out = pl.pallas_call(
        functools.partial(place_kernel, capacity, slabs),
        out_shape=shape(FEATURES, slabs * capacity),
        in_specs=[vmem],
        out_specs=vmem,
        compiler_params=params(16),
        cost_estimate=cost(3),
        name="place",
    )(moved)
    velocity_out = pl.pallas_call(
        project_kernel,
        out_shape=shape(3 * radii, columns),
        in_specs=[vmem] * 4 + [hbm],
        out_specs=hbm,
        scratch_shapes=[
            pltpu.VMEM((2 * radii + SUBLANES, elimination.shape[1]), f32),
            pltpu.VMEM((radii, NTH), f32),
            pltpu.VMEM((3 * radii, columns), f32),
            pltpu.SemaphoreType.DMA((4,)),
        ],
        compiler_params=params(51.25),
        cost_estimate=cost(5),
        name="project",
    )(gathered, ustar, transform, reduction, elimination)
    return velocity_out.reshape(velocity.shape), parcels_out.T


def solution(mesh):
    in_specs = (
        P(None, "gz", None, "pa"),
        P("gz", None, "pa"),
        P(("gz", "pa"), None),
        P(("gz", "pa"), None),
        P(("gz", "pa")),
        P(("gz", "pa")),
    )
    out_specs = (P(None, "gz", None, "pa"), P(("gz", "pa"), None))
    return jax.shard_map(body, mesh=mesh, in_specs=in_specs, out_specs=out_specs, check_vma=False)
```

```python
import functools
import math

import jax
import jax.numpy as jnp
import numpy as np
from jax import lax
from jax.experimental import pallas as pl
from jax.experimental.pallas import tpu as pltpu
from jax.sharding import PartitionSpec as P

NR = 192
NTH = 512
time_step = 0.1
shift_plane = 0.0001
step_angle = 2.0 * math.pi / NTH
LANES = 128
FEATURES = 16
SUBLANES = 8
EDGE_ROWS = 16
CORRECTION_ROWS = 64
f32 = jnp.float32
bf16 = jnp.bfloat16


def cas(numbers):
    phase = 2.0 * np.pi / NTH * (numbers % NTH)
    return np.cos(phase) + np.sin(phase)


def paired_modes():
    half, even, odd = NTH // 2, np.arange(0, NTH // 2, 2), np.arange(1, NTH // 2, 2)
    return np.concatenate([even, [half], NTH - even[1:], odd, NTH - odd])


def split_table(table):
    high = table.astype(jnp.bfloat16)
    return high, (table - high.astype(np.float64)).astype(jnp.bfloat16)


@functools.cache
def transform_table(ring, columns):
    modes = paired_modes()[None, :]
    plain = cas(np.arange(NTH // 2)[:, None] * modes)
    faces = np.zeros((CORRECTION_ROWS, NTH))
    for q in range(ring):
        last, at = q * columns + columns - 1, q * EDGE_ROWS

        def wave(offset):
            return cas((last + offset) * modes)

        faces[at + 5] = wave(0) - wave(1)
        faces[at + 6] = wave(-1) - wave(1) - wave(0) + wave(2)
        faces[at + 8] = wave(0)
        faces[at + 9] = wave(1)
    high, low = split_table(plain)
    face_high, face_low = split_table(faces)
    return np.concatenate([high, low, face_high, face_low, face_high], 0)


@functools.cache
def solve_tables():
    radius = NR + np.arange(NR) + 0.5
    arc = 1.0 / (radius * step_angle) ** 2
    up, down = radius + 0.5, radius - 0.5
    up[-1] = 0.0
    down[0] = 0.0
    spectrum = 2.0 - 2.0 * np.cos(step_angle * paired_modes())
    diagonal = radius[:, None] * (shift_plane + arc[:, None] * spectrum[None, :]) + up[:, None] + down[:, None]
    lower = np.broadcast_to(-down[:, None], diagonal.shape)
    upper = np.broadcast_to(-up[:, None], diagonal.shape)

    def moved(x, by, fill):
        filled = np.full((abs(by),) + x.shape[1:], fill)
        return np.concatenate([filled, x[:-by]], 0) if by > 0 else np.concatenate([x[-by:], filled], 0)

    tables, stride = [1.0 / diagonal], 1
    while stride < SUBLANES:
        low = lower / moved(diagonal, stride, 1.0)
        high = upper / moved(diagonal, -stride, 1.0)
        diagonal = diagonal - low * moved(upper, stride, 0.0) - high * moved(lower, -stride, 0.0)
        lower = -low * moved(lower, stride, 0.0)
        upper = -high * moved(upper, -stride, 0.0)
        if stride > 1:
            tables += [low, high]
        stride *= 2
    pivot = diagonal.copy()
    for i in range(SUBLANES, NR):
        pivot[i] = diagonal[i] - upper[i - SUBLANES] ** 2 / pivot[i - SUBLANES]
    middle = np.zeros((NR, 2 * LANES))
    for k, table in enumerate(tables):
        middle[:, k] = table[:, LANES]
    reduction = np.concatenate(tables, 0)
    reduction = np.concatenate([reduction[:, :LANES], reduction[:, 2 * LANES : 3 * LANES]], 1)
    sine = np.broadcast_to(2.0 * np.sin(step_angle * paired_modes()), (SUBLANES, NTH))
    elimination = np.concatenate([1.0 / pivot, upper / pivot, sine] + tables, 0)[:, : 3 * LANES]
    return np.concatenate([reduction, middle], 0).astype(np.float32), elimination.astype(np.float32)


def pieces(x, count):
    out = []
    for _ in range(count):
        part = x.astype(bf16).astype(f32)
        out.append(part)
        x = x - part
    return out


def dot(a, b, contract=((1,), (0,))):
    return lax.dot_general(a, b, (contract, ((), ())), preferred_element_type=f32)


def iota(shape, dim):
    return lax.broadcasted_iota(jnp.int32, shape, dim)


def shifted(x, by):
    length = x.shape[0]
    rolled = pltpu.roll(x, by % length, 0)
    row = iota(x.shape, 0)
    return jnp.where(row >= by if by > 0 else row < length + by, rolled, 0.0)


def pack_kernel(
    capacity, slabs, counts_in, parcels_in, target_in, cell_in, velocity_in, viscosity_in, send, fields,
    counts, parcels, target, cell, spread, hot, sems,
):
    radii3 = velocity_in.shape[0]
    copies = [
        pltpu.make_async_copy(source, target_ref, sems.at[k])
        for k, (source, target_ref) in enumerate(
            (
                (counts_in, counts),
                (target_in, target),
                (parcels_in, parcels),
                (cell_in, cell),
                (velocity_in, fields.at[:radii3]),
                (viscosity_in, fields.at[radii3:]),
            )
        )
    ]
    for copy in copies:
        copy.start()
    rows = parcels.shape[1]
    width = 256
    earlier = (iota((width, width), 0) < iota((width, width), 1)).astype(bf16)
    ones = jnp.ones((width, width), bf16)
    thirds = capacity // SUBLANES
    features = FEATURES * SUBLANES
    total = features + 2 * SUBLANES
    copies[0].wait()
    copies[1].wait()
    live = iota((1, rows), 1) < counts[0]
    wanted = jnp.where(live, target[...], -1)
    copies[2].wait()
    copies[3].wait()
    cells = cell[...]
    line = (cells // LANES + 1).astype(f32)
    column = (cells % LANES).astype(f32)
    passed = None
    for block in range(rows // width):
        here = slice(block * width, (block + 1) * width)
        mine = iota((slabs, width), 0) == wanted[:, here]
        mark = mine.astype(f32)
        before = dot(mark.astype(bf16), earlier)
        if passed is not None:
            before = before + dot(passed.astype(bf16), ones)
        passed = mark if passed is None else passed + mark
        slot = jnp.sum(mark * before, axis=0, keepdims=True).astype(jnp.int32)
        chosen = iota((SUBLANES, width), 0) == slot % SUBLANES
        for h in range(thirds):
            hot[h * slabs : (h + 1) * slabs, here] = jnp.where(slot // SUBLANES == h, mark, 0.0).astype(bf16)
        split = pieces(parcels[:, here], 2)

        def placed(row):
            return jnp.where(chosen, row, 0.0)

        for k, part in enumerate(split):
            base = 0 if k == 0 else total + (k - 1) * features
            for f in range(0, FEATURES, 2):
                pair = jnp.concatenate([placed(part[f : f + 1]), placed(part[f + 1 : f + 2])], 0)
                spread[base + f * SUBLANES : base + (f + 2) * SUBLANES, here] = pair.astype(bf16)
        pair = jnp.concatenate([placed(line[:, here]), placed(column[:, here])], 0)
        spread[features:total, here] = pair.astype(bf16)
    out = dot(spread[...], hot[...], ((1,), (1,)))
    values = jnp.concatenate([out[:features] + out[total:], out[features:total]], 0)
    words = [
        values[at : at + SUBLANES, h * slabs : (h + 1) * slabs] for at in range(0, total, SUBLANES) for h in range(thirds)
    ]
    lines = send.shape[0] // slabs
    words.append(jnp.zeros((lines * LANES - total * thirds, slabs), f32))
    whole = jnp.concatenate(words, 0)
    for c in range(lines):
        send[pl.ds(c, slabs, stride=lines), :] = whole[c * LANES : (c + 1) * LANES].T
    copies[4].wait()
    copies[5].wait()


def hold_kernel(fields, held):
    held[...] = fields[...]


def stencil_kernel(fields, near, far, partial, halves, edges):
    radii = fields.shape[0] // 4
    columns = fields.shape[1]
    radius = iota((radii, columns), 0).astype(f32) + (NR + 0.5)
    arc = 1.0 / (radius * step_angle) ** 2
    lane = iota((radii, columns), 1)
    own = [fields[c * radii : (c + 1) * radii, :] for c in range(4)]

    def around(c):
        x = own[c]
        return (
            near[c * radii : (c + 1) * radii, :],
            far[c * radii : (c + 1) * radii, :],
            shifted(x, -1),
            shifted(x, 1),
            pltpu.roll(x, columns - 1, 1),
            pltpu.roll(x, 1, 1),
        )

    weights = (
        0.5,
        0.5,
        0.5 * (radius + 0.5) / radius,
        0.5 * (radius - 0.5) / radius,
        jnp.where(lane == columns - 1, 0.0, 0.5 * arc),
        jnp.where(lane == 0, 0.0, 0.5 * arc),
    )
    faces = [w * (own[3] + n) for w, n in zip(weights, around(3))]
    for c in range(3):
        u = own[c]
        total = jnp.zeros_like(u)
        for face, beside in zip(faces, around(c)):
            total = total + face * (beside - u)
        partial[c * radii : (c + 1) * radii, :] = u + time_step * total
    edges[...] = jnp.zeros_like(edges)
    for c in range(4):
        put_edges(edges, own[c], c, 4 + c)
        if c < 3:
            parts = [p.astype(bf16) for p in pieces(own[c], 2)]
            halves[c * radii : (c + 1) * radii, :] = jnp.concatenate(parts, 1)


def put_edges(edges, x, first, last):
    turned = x.T
    rest = x.shape[0] - LANES
    for column, row in ((first, turned[:1]), (last, turned[LANES - 1 :])):
        edges[column : column + 1, :] = row[:, :LANES]
        at = 10 + column % 5
        start = column // 5 * rest
        edges[at : at + 1, start : start + rest] = row[:, LANES:]


def momentum_kernel(
    capacity, slabs, received, partial, halves, edges_in, ustar, payload, moved, line_hot, pulled, pushed, edges
):
    lines = received.shape[0] // slabs
    radii = partial.shape[0] // 3
    columns = partial.shape[1]
    turned = jnp.concatenate([received[pl.ds(c, slabs, stride=lines), :].T for c in range(lines)], 0)
    features = FEATURES * capacity
    line_of = turned[features : features + capacity].astype(jnp.int32) - 1
    column_of = turned[features + capacity : features + 2 * capacity].astype(jnp.int32)
    group = 4
    for j in range(0, capacity, group):
        here = slice(j * LANES, (j + group) * LANES)
        lane_line = jnp.concatenate([line_of[s : s + 1] for s in range(j, j + group)], 1)
        lane_column = jnp.concatenate([column_of[s : s + 1] for s in range(j, j + group)], 1)
        match = iota((radii, group * LANES), 0) == lane_line
        line_hot[:, here] = match.astype(bf16)
        hot = (iota((columns, group * LANES), 0) == lane_column).astype(bf16)
        picked = dot(halves[...], jnp.concatenate([hot, hot], 0))
        for c in range(3):
            got = jnp.sum(jnp.where(match, picked[c * radii : (c + 1) * radii], 0.0), axis=0, keepdims=True)
            for s in range(group):
                pulled[c, j + s : j + s + 1, :] = got[:, s * LANES : (s + 1) * LANES]
    fluid = [pulled[c] for c in range(3)]
    drag = [jnp.zeros_like(fluid[0]) for _ in range(3)]
    for k in range(4):
        rate = turned[(4 * k + 3) * capacity : (4 * k + 4) * capacity]
        weight = time_step * rate
        scale = 1.0 / (1.0 + weight)
        moved[(4 * k + 3) * capacity : (4 * k + 4) * capacity, :] = rate
        for c in range(3):
            at = (4 * k + c) * capacity
            after = (turned[at : at + capacity] + weight * fluid[c]) * scale
            moved[at : at + capacity, :] = after
            drag[c] = drag[c] + rate * (after - fluid[c])
    drag = [d.astype(bf16).astype(f32) for d in drag]
    for j in range(capacity):
        match = iota((columns, LANES), 0) == column_of[j : j + 1]
        for c in range(3):
            pushed[c * columns : (c + 1) * columns, j * LANES : (j + 1) * LANES] = jnp.where(
                match, drag[c][j : j + 1], 0.0
            ).astype(bf16)
    deposit = dot(line_hot[...], pushed[...], ((1,), (1,)))
    stars = []
    for c in range(3):
        rows = slice(c * radii, (c + 1) * radii)
        star = partial[rows, :] + time_step * deposit[:, c * columns : (c + 1) * columns]
        ustar[rows, :] = star
        stars.append(star)
    row = iota((radii, columns), 0)
    lane = iota((radii, columns), 1)
    radius = row.astype(f32) + (NR + 0.5)
    flux = jnp.where(row < radii - 1, (radius + 0.5) * 0.5 * (stars[1] + shifted(stars[1], -1)), 0.0)
    ahead = jnp.where(lane == columns - 1, 0.0, pltpu.roll(stars[2], columns - 1, 1))
    behind = jnp.where(lane == 0, 0.0, pltpu.roll(stars[2], 1, 1))
    source = shifted(flux, 1) - flux - (0.5 / step_angle) * (ahead - behind)
    edges[...] = edges_in[...]
    put_edges(edges, stars[2], 8, 9)
    for q in range(payload.shape[0]):
        payload[q, :radii, :] = source
        payload[q, radii:, :] = edges[...]


def project_kernel(gathered, ustar, transform, reduction, elimination_in, out_hbm, elimination, state, out, sems):
    me = lax.axis_index("pa")
    fetch = pltpu.make_async_copy(elimination_in.at[: elimination.shape[0]], elimination, sems.at[0])
    fetch.start()
    ring = gathered.shape[0]
    radii = out.shape[0] // 3
    columns = out.shape[1]
    half = NTH // 2

    rows = [gathered[q % ring, radii:, :] for q in range(ring + 1)]
    rows.append(jnp.zeros((LANES - (ring + 1) * EDGE_ROWS, LANES), f32))
    turned = jnp.concatenate(rows, 0).T
    rest = radii - LANES
    fifth = iota((rest, LANES), 1) % EDGE_ROWS < 5
    others = jnp.where(
        fifth, pltpu.roll(turned[:rest], LANES - 10, 1), pltpu.roll(turned[rest : 2 * rest], LANES - 5, 1)
    )

    sides = jnp.concatenate([turned, others], 0)
    row = iota((radii, LANES), 0)
    lane = iota((radii, LANES), 1)
    kind = lane % EDGE_ROWS
    radius = row.astype(f32) + (NR + 0.5)
    inverse = 1.0 / radius

    def lanes_from(x, by):
        return pltpu.roll(x, LANES - by, 1)

    beyond = lanes_from(sides, EDGE_ROWS - 4)
    both = sides + beyond
    face = jnp.where(kind == 4, lanes_from(both, 3), jnp.where(kind == 5, lanes_from(both, 2), lanes_from(both, 1)))
    arc = inverse * inverse * (0.5 * time_step / step_angle**2)
    used = lane < ring * EDGE_ROWS
    crossing = jnp.where(used & (kind >= 4) & (kind < 7), arc * face * (beyond - sides), 0.0)
    flux = jnp.where(row < radii - 1, (radius + 0.5) * 0.5 * (crossing + shifted(crossing, -1)), 0.0)
    outward = shifted(flux, 1) - flux
    turning = 0.5 / step_angle
    coefficients = jnp.where(
        kind == 5,
        outward,
        turning * jnp.where(kind == 6, -crossing, jnp.where(kind == 8, -lanes_from(sides, EDGE_ROWS), sides)),
    )
    used = used & ((kind == 5) | (kind == 6) | (kind == 8) | (kind == 9))
    coefficients = jnp.where(used, coefficients, 0.0)[:, :CORRECTION_ROWS]

    width = 3 * columns
    wide_row = iota((LANES, width), 0)
    wide_lane = iota((LANES, width), 1)
    before = lax.rem(me + ring - 1, ring)
    inside = wide_lane % columns
    at = wide_lane // columns + 4
    pick = jnp.where((inside == columns - 1) & (wide_row == at + me * EDGE_ROWS), 1.0, 0.0) - jnp.where(
        (inside == 0) & (wide_row == at + before * EDGE_ROWS), 1.0, 0.0
    )
    pick = pick.astype(bf16)
    crossing_parts = [p.astype(bf16) for p in pieces(crossing, 2)]
    delta = dot(jnp.concatenate(crossing_parts, 1), jnp.concatenate([pick, pick], 0))

    out[:radii, :] = ustar[:radii, :] + delta[:, :columns]
    whole = [pltpu.make_async_copy(out.at[k : k + radii], out_hbm.at[k : k + radii], sems.at[1 + k // radii]) for k in range(0, 3 * radii, radii)]
    whole[0].start()
    near = jnp.concatenate([gathered[q, :radii, :] for q in range(ring // 2)], 1)
    distant = jnp.concatenate([gathered[q, :radii, :] for q in range(ring // 2, ring)], 1)

    def forward(x, cols):
        high, low = [p.astype(bf16) for p in pieces(x, 2)]
        table_high, table_low = transform[:half, cols], transform[half : 2 * half, cols]
        return dot(high, table_high) + (dot(high, table_low) + dot(low, table_high)) + dot(corrections, transform[2 * half :, cols])

    parts = [p.astype(bf16) for p in pieces(coefficients, 2)]
    corrections = jnp.concatenate([parts[0], parts[0], parts[1]], 1)
    even = slice(0, half)
    odd = slice(half, NTH)
    modes_even = forward(near + distant, even)
    modes_odd = forward(near - distant, odd)
    blocks = [m[:, b * LANES : (b + 1) * LANES] for m in (modes_even, modes_odd) for b in range(2)]
    total = sum(NR + i + 0.5 for i in range(NR))
    mean = jnp.sum(blocks[0], axis=0, keepdims=True) * (1.0 / total)
    blocks[0] = blocks[0] - radius * jnp.where(iota((1, LANES), 1) == 0, mean, 0.0)
    middle = reduction[5 * radii :, :LANES]

    def factor(k, b):
        table = reduction[k * radii : (k + 1) * radii, b // 2 * LANES : (b // 2 + 1) * LANES]
        return jnp.where(lane == 0, pltpu.roll(middle, (LANES - k) % LANES, 1), table) if b == 1 else table

    inner = jnp.where(row > 0, radius - 0.5, 0.0)
    outer = jnp.where(row < radii - 1, radius + 0.5, 0.0)
    for b in range(ring):
        x = blocks[b]
        scaled = x * factor(0, b)
        x = x + inner * pltpu.roll(scaled, 1, 0) + outer * pltpu.roll(scaled, radii - 1, 0)
        for stride, k in ((2, 1), (4, 3)):
            x = x - factor(k, b) * pltpu.roll(x, stride, 0) - factor(k + 1, b) * pltpu.roll(x, radii - stride, 0)
        state[:, b * LANES : (b + 1) * LANES] = x
    fetch.wait()

    def factors(k, v):
        at = k * radii + v * SUBLANES
        table = elimination[at : at + SUBLANES, :]
        return jnp.concatenate([table, table[:, 2 * LANES :]], 1)

    steps = radii // SUBLANES
    y = state[:SUBLANES, :]
    for v in range(1, steps):
        rows = slice(v * SUBLANES, (v + 1) * SUBLANES)
        y = state[rows, :] - factors(1, v - 1) * y
        state[rows, :] = y
    x = y * factors(0, steps - 1)
    state[(steps - 1) * SUBLANES :, :] = x
    for v in range(steps - 2, -1, -1):
        rows = slice(v * SUBLANES, (v + 1) * SUBLANES)
        x = state[rows, :] * factors(0, v) - factors(1, v) * x
        state[rows, :] = x

    potential = [state[:, b * LANES : (b + 1) * LANES] for b in range(ring)]

    def gradient(x):
        above = jnp.where(row == radii - 1, x, pltpu.roll(x, radii - 1, 0))
        below = jnp.where(row == 0, x, pltpu.roll(x, 1, 0))
        return above - below

    mine = pl.multiple_of(me % 2 * columns, columns)
    result = []
    for group, cols in ((0, even), (1, odd)):
        plain, mirror = potential[2 * group], potential[2 * group + 1]
        sine = elimination[2 * radii : 2 * radii + 1, 2 * group * LANES : (2 * group + 1) * LANES]
        slopes = jnp.concatenate([gradient(plain), gradient(mirror)], 1)
        turns = jnp.concatenate([-sine * mirror, sine * plain], 1)
        high, low = [p.astype(bf16) for p in pieces(jnp.concatenate([slopes, turns], 0), 2)]
        own_high, own_low = transform[pl.ds(mine, columns), cols], transform[pl.ds(half + mine, columns), cols]
        both = dot(high, jnp.concatenate([own_high, own_low], 0), ((1,), (1,)))
        result.append(both[:, :columns] + (both[:, columns:] + dot(low, own_high, ((1,), (1,)))))
    result = result[0] + jnp.where(me >= ring // 2, -1.0, 1.0) * result[1]
    out[radii : 2 * radii, :] = ustar[radii : 2 * radii, :] + delta[:, columns : 2 * columns] - result[:radii] * (0.5 / NTH)
    whole[1].start()
    out[2 * radii :, :] = ustar[2 * radii :, :] + delta[:, 2 * columns :] - result[radii:] * (inverse * (turning / NTH))
    whole[2].start()
    for copy in whole:
        copy.wait()


def place_kernel(capacity, slabs, moved, out):
    rows = slabs * capacity
    width = 768
    split = jnp.concatenate([p.astype(bf16) for p in pieces(moved[...], 2)], 1)
    for start in range(0, rows, width):
        place = start + iota((slabs, width), 1)
        hot = (place // capacity == iota((slabs, width), 0)).astype(bf16)
        spread = dot(split, jnp.concatenate([hot, hot], 0))
        match = (start + iota((capacity, width), 1)) % capacity == iota((capacity, width), 0)
        for f in range(FEATURES):
            block = spread[f * capacity : (f + 1) * capacity]
            out[f : f + 1, start : start + width] = jnp.sum(jnp.where(match, block, 0.0), axis=0, keepdims=True)


def shape(*dims):
    return jax.ShapeDtypeStruct(dims, f32)


def params(mib):
    return pltpu.CompilerParams(vmem_limit_bytes=int(mib * 1024 * 1024))


def cost(microseconds):
    return pl.CostEstimate(flops=0, bytes_accessed=int(microseconds * 3.0e6), transcendentals=0)


def body(velocity, viscosity, parcels, dest_rank, dest_cell, counts):
    slabs = lax.axis_size("gz")
    ring = lax.axis_size("pa")
    planes, radii, columns = viscosity.shape
    block = parcels.shape[0]
    capacity = 3 * block // slabs
    lines = -(-(FEATURES + 2) * capacity // LANES)
    vmem = pl.BlockSpec(memory_space=pltpu.VMEM)
    hbm = pl.BlockSpec(memory_space=pltpu.HBM)
    u = velocity.reshape(3 * radii, columns)
    nu = viscosity.reshape(radii, columns)
    features = FEATURES * capacity
    send, fields = pl.pallas_call(
        functools.partial(pack_kernel, capacity, slabs),
        out_shape=(shape(slabs * lines, LANES), shape(4 * radii, columns)),
        in_specs=[hbm] * 6,
        out_specs=(vmem,) * 2,
        scratch_shapes=[
            pltpu.SMEM((1,), jnp.int32),
            pltpu.VMEM((FEATURES, block), f32),
            pltpu.VMEM((1, block), jnp.int32),
            pltpu.VMEM((1, block), jnp.int32),
            pltpu.VMEM((2 * (FEATURES + 1) * SUBLANES, block), bf16),
            pltpu.VMEM((capacity // SUBLANES * slabs, block), bf16),
            pltpu.SemaphoreType.DMA((6,)),
        ],
        compiler_params=params(60),
        cost_estimate=cost(3),
        name="pack",
    )(counts, parcels.T, dest_rank.reshape(1, block), dest_cell.reshape(1, block), u, nu)
    received = lax.all_to_all(
        send.reshape(slabs, lines, LANES), "gz", split_axis=0, concat_axis=0, tiled=True
    ).reshape(slabs * lines, LANES)

    near = lax.ppermute(fields, "gz", [(i, i ^ 1) for i in range(slabs)])
    pairs = [(i, i + 1) for i in range(1, slabs - 1, 2)]
    far = lax.ppermute(fields, "gz", pairs + [(j, i) for i, j in pairs])
    transform = jnp.asarray(transform_table(ring, columns))
    reduction, elimination = [jnp.asarray(table) for table in solve_tables()]
    held = pl.pallas_call(
        hold_kernel,
        out_shape=shape(*fields.shape),
        in_specs=[vmem],
        out_specs=vmem,
        compiler_params=params(16),
        cost_estimate=cost(1),
        name="hold",
    )(fields)
    partial, halves, edges = pl.pallas_call(
        stencil_kernel,
        out_shape=(
            shape(3 * radii, columns),
            jax.ShapeDtypeStruct((3 * radii, 2 * columns), bf16),
            shape(EDGE_ROWS, LANES),
        ),
        in_specs=[vmem] * 3,
        out_specs=(vmem,) * 3,
        compiler_params=params(16),
        cost_estimate=cost(2),
        name="stencil",
    )(held, near, far)

    ustar, payload, moved = pl.pallas_call(
        functools.partial(momentum_kernel, capacity, slabs),
        out_shape=(
            shape(3 * radii, columns),
            shape(ring, radii + EDGE_ROWS, columns),
            shape(features, slabs),
        ),
        in_specs=[vmem] * 4,
        out_specs=(vmem,) * 3,
        scratch_shapes=[
            pltpu.VMEM((radii, capacity * slabs), bf16),
            pltpu.VMEM((3, capacity, slabs), f32),
            pltpu.VMEM((3 * columns, capacity * slabs), bf16),
            pltpu.VMEM((EDGE_ROWS, LANES), f32),
        ],
        compiler_params=params(16),
        cost_estimate=cost(4),
        name="momentum",
    )(received, partial, halves, edges)

    gathered = lax.all_to_all(payload, "pa", split_axis=0, concat_axis=0, tiled=True)
    parcels_out = pl.pallas_call(
        functools.partial(place_kernel, capacity, slabs),
        out_shape=shape(FEATURES, slabs * capacity),
        in_specs=[vmem],
        out_specs=vmem,
        compiler_params=params(16),
        cost_estimate=cost(3),
        name="place",
    )(moved)
    velocity_out = pl.pallas_call(
        project_kernel,
        out_shape=shape(3 * radii, columns),
        in_specs=[vmem] * 4 + [hbm],
        out_specs=hbm,
        scratch_shapes=[
            pltpu.VMEM((2 * radii + SUBLANES, elimination.shape[1]), f32),
            pltpu.VMEM((radii, NTH), f32),
            pltpu.VMEM((3 * radii, columns), f32),
            pltpu.SemaphoreType.DMA((4,)),
        ],
        compiler_params=params(51.25),
        cost_estimate=cost(5),
        name="project",
    )(gathered, ustar, transform, reduction, elimination)
    return velocity_out.reshape(velocity.shape), parcels_out.T


def solution(mesh):
    in_specs = (
        P(None, "gz", None, "pa"),
        P("gz", None, "pa"),
        P(("gz", "pa"), None),
        P(("gz", "pa"), None),
        P(("gz", "pa")),
        P(("gz", "pa")),
    )
    out_specs = (P(None, "gz", None, "pa"), P(("gz", "pa"), None))
    return jax.shard_map(body, mesh=mesh, in_specs=in_specs, out_specs=out_specs, check_vma=False)
```

```python
import functools
import math

import jax
import jax.numpy as jnp
import numpy as np
from jax import lax
from jax.experimental import pallas as pl
from jax.experimental.pallas import tpu as pltpu
from jax.sharding import PartitionSpec as P

NR = 192
NTH = 512
time_step = 0.1
shift_plane = 0.0001
step_angle = 2.0 * math.pi / NTH
LANES = 128
FEATURES = 16
SUBLANES = 8
EDGE_ROWS = 16
CORRECTION_ROWS = 64
f32 = jnp.float32
bf16 = jnp.bfloat16


def cas(numbers):
    phase = 2.0 * np.pi / NTH * (numbers % NTH)
    return np.cos(phase) + np.sin(phase)


def paired_modes():
    half, even, odd = NTH // 2, np.arange(0, NTH // 2, 2), np.arange(1, NTH // 2, 2)
    return np.concatenate([even, [half], NTH - even[1:], odd, NTH - odd])


def split_table(table):
    high = table.astype(jnp.bfloat16)
    return high, (table - high.astype(np.float64)).astype(jnp.bfloat16)


@functools.cache
def transform_table(ring, columns):
    modes = paired_modes()[None, :]
    plain = cas(np.arange(NTH // 2)[:, None] * modes)
    faces = np.zeros((CORRECTION_ROWS, NTH))
    for q in range(ring):
        last, at = q * columns + columns - 1, q * EDGE_ROWS

        def wave(offset):
            return cas((last + offset) * modes)

        faces[at + 5] = wave(0) - wave(1)
        faces[at + 6] = wave(-1) - wave(1) - wave(0) + wave(2)
        faces[at + 8] = wave(0)
        faces[at + 9] = wave(1)
    high, low = split_table(plain)
    face_high, face_low = split_table(faces)
    return np.concatenate([high, low, face_high, face_low, face_high], 0)


@functools.cache
def solve_tables():
    radius = NR + np.arange(NR) + 0.5
    arc = 1.0 / (radius * step_angle) ** 2
    up, down = radius + 0.5, radius - 0.5
    up[-1] = 0.0
    down[0] = 0.0
    spectrum = 2.0 - 2.0 * np.cos(step_angle * paired_modes())
    diagonal = radius[:, None] * (shift_plane + arc[:, None] * spectrum[None, :]) + up[:, None] + down[:, None]
    lower = np.broadcast_to(-down[:, None], diagonal.shape)
    upper = np.broadcast_to(-up[:, None], diagonal.shape)

    def moved(x, by, fill):
        filled = np.full((abs(by),) + x.shape[1:], fill)
        return np.concatenate([filled, x[:-by]], 0) if by > 0 else np.concatenate([x[-by:], filled], 0)

    tables, stride = [1.0 / diagonal], 1
    while stride < SUBLANES:
        low = lower / moved(diagonal, stride, 1.0)
        high = upper / moved(diagonal, -stride, 1.0)
        diagonal = diagonal - low * moved(upper, stride, 0.0) - high * moved(lower, -stride, 0.0)
        lower = -low * moved(lower, stride, 0.0)
        upper = -high * moved(upper, -stride, 0.0)
        if stride > 1:
            tables += [low, high]
        stride *= 2
    pivot = diagonal.copy()
    for i in range(SUBLANES, NR):
        pivot[i] = diagonal[i] - upper[i - SUBLANES] ** 2 / pivot[i - SUBLANES]
    middle = np.zeros((NR, 2 * LANES))
    for k, table in enumerate(tables):
        middle[:, k] = table[:, LANES]
    reduction = np.concatenate(tables, 0)
    reduction = np.concatenate([reduction[:, :LANES], reduction[:, 2 * LANES : 3 * LANES]], 1)
    sine = np.broadcast_to(2.0 * np.sin(step_angle * paired_modes()), (SUBLANES, NTH))
    elimination = np.concatenate([1.0 / pivot, upper / pivot, sine] + tables, 0)[:, : 3 * LANES]
    return np.concatenate([reduction, middle], 0).astype(np.float32), elimination.astype(np.float32)


def pieces(x, count):
    out = []
    for _ in range(count):
        part = x.astype(bf16).astype(f32)
        out.append(part)
        x = x - part
    return out


def dot(a, b, contract=((1,), (0,))):
    return lax.dot_general(a, b, (contract, ((), ())), preferred_element_type=f32)


def iota(shape, dim):
    return lax.broadcasted_iota(jnp.int32, shape, dim)


def shifted(x, by):
    length = x.shape[0]
    rolled = pltpu.roll(x, by % length, 0)
    row = iota(x.shape, 0)
    return jnp.where(row >= by if by > 0 else row < length + by, rolled, 0.0)


def pack_kernel(
    capacity, slabs, counts_in, parcels_in, target_in, cell_in, velocity_in, viscosity_in, send, fields,
    counts, parcels, target, cell, spread, hot, sems,
):
    radii3 = velocity_in.shape[0]
    copies = [
        pltpu.make_async_copy(source, target_ref, sems.at[k])
        for k, (source, target_ref) in enumerate(
            (
                (counts_in, counts),
                (target_in, target),
                (parcels_in, parcels),
                (cell_in, cell),
                (velocity_in, fields.at[:radii3]),
                (viscosity_in, fields.at[radii3:]),
            )
        )
    ]
    for copy in copies:
        copy.start()
    rows = parcels.shape[1]
    width = 256
    earlier = (iota((width, width), 0) < iota((width, width), 1)).astype(bf16)
    ones = jnp.ones((width, width), bf16)
    thirds = capacity // SUBLANES
    features = FEATURES * SUBLANES
    total = features + 2 * SUBLANES
    copies[0].wait()
    copies[1].wait()
    live = iota((1, rows), 1) < counts[0]
    wanted = jnp.where(live, target[...], -1)
    copies[2].wait()
    copies[3].wait()
    cells = cell[...]
    line = (cells // LANES + 1).astype(f32)
    column = (cells % LANES).astype(f32)
    passed = None
    for block in range(rows // width):
        here = slice(block * width, (block + 1) * width)
        mine = iota((slabs, width), 0) == wanted[:, here]
        mark = mine.astype(f32)
        before = dot(mark.astype(bf16), earlier)
        if passed is not None:
            before = before + dot(passed.astype(bf16), ones)
        passed = mark if passed is None else passed + mark
        slot = jnp.sum(mark * before, axis=0, keepdims=True).astype(jnp.int32)
        chosen = iota((SUBLANES, width), 0) == slot % SUBLANES
        for h in range(thirds):
            hot[h * slabs : (h + 1) * slabs, here] = jnp.where(slot // SUBLANES == h, mark, 0.0).astype(bf16)
        split = pieces(parcels[:, here], 2)

        def placed(row):
            return jnp.where(chosen, row, 0.0)

        for k, part in enumerate(split):
            base = 0 if k == 0 else total + (k - 1) * features
            for f in range(0, FEATURES, 2):
                pair = jnp.concatenate([placed(part[f : f + 1]), placed(part[f + 1 : f + 2])], 0)
                spread[base + f * SUBLANES : base + (f + 2) * SUBLANES, here] = pair.astype(bf16)
        pair = jnp.concatenate([placed(line[:, here]), placed(column[:, here])], 0)
        spread[features:total, here] = pair.astype(bf16)
    out = dot(spread[...], hot[...], ((1,), (1,)))
    values = jnp.concatenate([out[:features] + out[total:], out[features:total]], 0)
    words = [
        values[at : at + SUBLANES, h * slabs : (h + 1) * slabs] for at in range(0, total, SUBLANES) for h in range(thirds)
    ]
    lines = send.shape[0] // slabs
    words.append(jnp.zeros((lines * LANES - total * thirds, slabs), f32))
    whole = jnp.concatenate(words, 0)
    for c in range(lines):
        send[pl.ds(c, slabs, stride=lines), :] = whole[c * LANES : (c + 1) * LANES].T
    copies[4].wait()
    copies[5].wait()


def hold_kernel(fields, held):
    held[...] = fields[...]


def stencil_kernel(fields, near, far, partial, halves, edges):
    radii = fields.shape[0] // 4
    columns = fields.shape[1]
    radius = iota((radii, columns), 0).astype(f32) + (NR + 0.5)
    arc = 1.0 / (radius * step_angle) ** 2
    lane = iota((radii, columns), 1)
    own = [fields[c * radii : (c + 1) * radii, :] for c in range(4)]

    def around(c):
        x = own[c]
        return (
            near[c * radii : (c + 1) * radii, :],
            far[c * radii : (c + 1) * radii, :],
            shifted(x, -1),
            shifted(x, 1),
            pltpu.roll(x, columns - 1, 1),
            pltpu.roll(x, 1, 1),
        )

    weights = (
        0.5,
        0.5,
        0.5 * (radius + 0.5) / radius,
        0.5 * (radius - 0.5) / radius,
        jnp.where(lane == columns - 1, 0.0, 0.5 * arc),
        jnp.where(lane == 0, 0.0, 0.5 * arc),
    )
    faces = [w * (own[3] + n) for w, n in zip(weights, around(3))]
    for c in range(3):
        u = own[c]
        total = jnp.zeros_like(u)
        for face, beside in zip(faces, around(c)):
            total = total + face * (beside - u)
        partial[c * radii : (c + 1) * radii, :] = u + time_step * total
    edges[...] = jnp.zeros_like(edges)
    for c in range(4):
        put_edges(edges, own[c], c, 4 + c)
        if c < 3:
            parts = [p.astype(bf16) for p in pieces(own[c], 2)]
            halves[c * radii : (c + 1) * radii, :] = jnp.concatenate(parts, 1)


def put_edges(edges, x, first, last):
    turned = x.T
    rest = x.shape[0] - LANES
    for column, row in ((first, turned[:1]), (last, turned[LANES - 1 :])):
        edges[column : column + 1, :] = row[:, :LANES]
        at = 10 + column % 5
        start = column // 5 * rest
        edges[at : at + 1, start : start + rest] = row[:, LANES:]


def momentum_kernel(
    capacity, slabs, received, partial, halves, edges_in, ustar, payload, moved, line_hot, pulled, pushed, edges
):
    lines = received.shape[0] // slabs
    radii = partial.shape[0] // 3
    columns = partial.shape[1]
    turned = jnp.concatenate([received[pl.ds(c, slabs, stride=lines), :].T for c in range(lines)], 0)
    features = FEATURES * capacity
    line_of = turned[features : features + capacity].astype(jnp.int32) - 1
    column_of = turned[features + capacity : features + 2 * capacity].astype(jnp.int32)
    group = 4
    for j in range(0, capacity, group):
        here = slice(j * LANES, (j + group) * LANES)
        lane_line = jnp.concatenate([line_of[s : s + 1] for s in range(j, j + group)], 1)
        lane_column = jnp.concatenate([column_of[s : s + 1] for s in range(j, j + group)], 1)
        match = iota((radii, group * LANES), 0) == lane_line
        line_hot[:, here] = match.astype(bf16)
        hot = (iota((columns, group * LANES), 0) == lane_column).astype(bf16)
        picked = dot(halves[...], jnp.concatenate([hot, hot], 0))
        for c in range(3):
            got = jnp.sum(jnp.where(match, picked[c * radii : (c + 1) * radii], 0.0), axis=0, keepdims=True)
            for s in range(group):
                pulled[c, j + s : j + s + 1, :] = got[:, s * LANES : (s + 1) * LANES]
    fluid = [pulled[c] for c in range(3)]
    drag = [jnp.zeros_like(fluid[0]) for _ in range(3)]
    for k in range(4):
        rate = turned[(4 * k + 3) * capacity : (4 * k + 4) * capacity]
        weight = time_step * rate
        scale = 1.0 / (1.0 + weight)
        moved[(4 * k + 3) * capacity : (4 * k + 4) * capacity, :] = rate
        for c in range(3):
            at = (4 * k + c) * capacity
            after = (turned[at : at + capacity] + weight * fluid[c]) * scale
            moved[at : at + capacity, :] = after
            drag[c] = drag[c] + rate * (after - fluid[c])
    drag = [d.astype(bf16).astype(f32) for d in drag]
    for j in range(capacity):
        match = iota((columns, LANES), 0) == column_of[j : j + 1]
        for c in range(3):
            pushed[c * columns : (c + 1) * columns, j * LANES : (j + 1) * LANES] = jnp.where(
                match, drag[c][j : j + 1], 0.0
            ).astype(bf16)
    deposit = dot(line_hot[...], pushed[...], ((1,), (1,)))
    stars = []
    for c in range(3):
        rows = slice(c * radii, (c + 1) * radii)
        star = partial[rows, :] + time_step * deposit[:, c * columns : (c + 1) * columns]
        ustar[rows, :] = star
        stars.append(star)
    row = iota((radii, columns), 0)
    lane = iota((radii, columns), 1)
    radius = row.astype(f32) + (NR + 0.5)
    flux = jnp.where(row < radii - 1, (radius + 0.5) * 0.5 * (stars[1] + shifted(stars[1], -1)), 0.0)
    ahead = jnp.where(lane == columns - 1, 0.0, pltpu.roll(stars[2], columns - 1, 1))
    behind = jnp.where(lane == 0, 0.0, pltpu.roll(stars[2], 1, 1))
    source = shifted(flux, 1) - flux - (0.5 / step_angle) * (ahead - behind)
    edges[...] = edges_in[...]
    put_edges(edges, stars[2], 8, 9)
    for q in range(payload.shape[0]):
        payload[q, :radii, :] = source
        payload[q, radii:, :] = edges[...]


def project_kernel(gathered, ustar, transform, reduction, elimination_in, out_hbm, elimination, state, out, sems):
    me = lax.axis_index("pa")
    fetch = pltpu.make_async_copy(elimination_in.at[: elimination.shape[0]], elimination, sems.at[0])
    fetch.start()
    ring = gathered.shape[0]
    radii = out.shape[0] // 3
    columns = out.shape[1]
    half = NTH // 2

    rows = [gathered[q % ring, radii:, :] for q in range(ring + 1)]
    rows.append(jnp.zeros((LANES - (ring + 1) * EDGE_ROWS, LANES), f32))
    turned = jnp.concatenate(rows, 0).T
    rest = radii - LANES
    fifth = iota((rest, LANES), 1) % EDGE_ROWS < 5
    others = jnp.where(
        fifth, pltpu.roll(turned[:rest], LANES - 10, 1), pltpu.roll(turned[rest : 2 * rest], LANES - 5, 1)
    )

    sides = jnp.concatenate([turned, others], 0)
    row = iota((radii, LANES), 0)
    lane = iota((radii, LANES), 1)
    kind = lane % EDGE_ROWS
    radius = row.astype(f32) + (NR + 0.5)
    inverse = 1.0 / radius

    def lanes_from(x, by):
        return pltpu.roll(x, LANES - by, 1)

    beyond = lanes_from(sides, EDGE_ROWS - 4)
    both = sides + beyond
    face = jnp.where(kind == 4, lanes_from(both, 3), jnp.where(kind == 5, lanes_from(both, 2), lanes_from(both, 1)))
    arc = inverse * inverse * (0.5 * time_step / step_angle**2)
    used = lane < ring * EDGE_ROWS
    crossing = jnp.where(used & (kind >= 4) & (kind < 7), arc * face * (beyond - sides), 0.0)
    flux = jnp.where(row < radii - 1, (radius + 0.5) * 0.5 * (crossing + shifted(crossing, -1)), 0.0)
    outward = shifted(flux, 1) - flux
    turning = 0.5 / step_angle
    coefficients = jnp.where(
        kind == 5,
        outward,
        turning * jnp.where(kind == 6, -crossing, jnp.where(kind == 8, -lanes_from(sides, EDGE_ROWS), sides)),
    )
    used = used & ((kind == 5) | (kind == 6) | (kind == 8) | (kind == 9))
    coefficients = jnp.where(used, coefficients, 0.0)[:, :CORRECTION_ROWS]

    width = 3 * columns
    wide_row = iota((LANES, width), 0) % (ring * EDGE_ROWS)
    wide_lane = iota((LANES, width), 1)
    before = lax.rem(me + ring - 1, ring)
    inside = wide_lane % columns
    at = wide_lane // columns + 4
    pick = jnp.where((inside == columns - 1) & (wide_row == at + me * EDGE_ROWS), 1.0, 0.0) - jnp.where(
        (inside == 0) & (wide_row == at + before * EDGE_ROWS), 1.0, 0.0
    )
    pick = pick.astype(bf16)
    crossing_high, crossing_low = pieces(crossing, 2)
    delta = dot((crossing_high + pltpu.roll(crossing_low, ring * EDGE_ROWS, 1)).astype(bf16), pick)

    out[:radii, :] = ustar[:radii, :] + delta[:, :columns]
    whole = [pltpu.make_async_copy(out.at[k : k + radii], out_hbm.at[k : k + radii], sems.at[1 + k // radii]) for k in range(0, 3 * radii, radii)]
    whole[0].start()
    near = jnp.concatenate([gathered[q, :radii, :] for q in range(ring // 2)], 1)
    distant = jnp.concatenate([gathered[q, :radii, :] for q in range(ring // 2, ring)], 1)

    def forward(x, cols):
        high, low = [p.astype(bf16) for p in pieces(x, 2)]
        table_high, table_low = transform[:half, cols], transform[half : 2 * half, cols]
        return dot(high, table_high) + (dot(high, table_low) + dot(low, table_high)) + dot(corrections, transform[2 * half :, cols])

    parts = [p.astype(bf16) for p in pieces(coefficients, 2)]
    corrections = jnp.concatenate([parts[0], parts[0], parts[1]], 1)
    even = slice(0, half)
    odd = slice(half, NTH)
    modes_even = forward(near + distant, even)
    modes_odd = forward(near - distant, odd)
    blocks = [m[:, b * LANES : (b + 1) * LANES] for m in (modes_even, modes_odd) for b in range(2)]
    total = sum(NR + i + 0.5 for i in range(NR))
    mean = jnp.sum(blocks[0], axis=0, keepdims=True) * (1.0 / total)
    blocks[0] = blocks[0] - radius * jnp.where(iota((1, LANES), 1) == 0, mean, 0.0)
    middle = reduction[5 * radii :, :LANES]

    def factor(k, b):
        table = reduction[k * radii : (k + 1) * radii, b // 2 * LANES : (b // 2 + 1) * LANES]
        return jnp.where(lane == 0, pltpu.roll(middle, (LANES - k) % LANES, 1), table) if b == 1 else table

    inner = jnp.where(row > 0, radius - 0.5, 0.0)
    outer = jnp.where(row < radii - 1, radius + 0.5, 0.0)
    for b in range(ring):
        x = blocks[b]
        scaled = x * factor(0, b)
        x = x + inner * pltpu.roll(scaled, 1, 0) + outer * pltpu.roll(scaled, radii - 1, 0)
        for stride, k in ((2, 1), (4, 3)):
            x = x - factor(k, b) * pltpu.roll(x, stride, 0) - factor(k + 1, b) * pltpu.roll(x, radii - stride, 0)
        state[:, b * LANES : (b + 1) * LANES] = x
    fetch.wait()

    def factors(k, v):
        at = k * radii + v * SUBLANES
        table = elimination[at : at + SUBLANES, :]
        return jnp.concatenate([table, table[:, 2 * LANES :]], 1)

    steps = radii // SUBLANES
    y = state[:SUBLANES, :]
    for v in range(1, steps):
        rows = slice(v * SUBLANES, (v + 1) * SUBLANES)
        y = state[rows, :] - factors(1, v - 1) * y
        state[rows, :] = y
    x = y * factors(0, steps - 1)
    state[(steps - 1) * SUBLANES :, :] = x
    for v in range(steps - 2, -1, -1):
        rows = slice(v * SUBLANES, (v + 1) * SUBLANES)
        x = state[rows, :] * factors(0, v) - factors(1, v) * x
        state[rows, :] = x

    potential = [state[:, b * LANES : (b + 1) * LANES] for b in range(ring)]

    def gradient(x):
        above = jnp.where(row == radii - 1, x, pltpu.roll(x, radii - 1, 0))
        below = jnp.where(row == 0, x, pltpu.roll(x, 1, 0))
        return above - below

    mine = pl.multiple_of(me % 2 * columns, columns)
    result = []
    for group, cols in ((0, even), (1, odd)):
        plain, mirror = potential[2 * group], potential[2 * group + 1]
        sine = elimination[2 * radii : 2 * radii + 1, 2 * group * LANES : (2 * group + 1) * LANES]
        slopes = jnp.concatenate([gradient(plain), gradient(mirror)], 1)
        turns = jnp.concatenate([-sine * mirror, sine * plain], 1)
        high, low = [p.astype(bf16) for p in pieces(jnp.concatenate([slopes, turns], 0), 2)]
        own_high, own_low = transform[pl.ds(mine, columns), cols], transform[pl.ds(half + mine, columns), cols]
        both = dot(high, jnp.concatenate([own_high, own_low], 0), ((1,), (1,)))
        result.append(both[:, :columns] + (both[:, columns:] + dot(low, own_high, ((1,), (1,)))))
    result = result[0] + jnp.where(me >= ring // 2, -1.0, 1.0) * result[1]
    out[radii : 2 * radii, :] = ustar[radii : 2 * radii, :] + delta[:, columns : 2 * columns] - result[:radii] * (0.5 / NTH)
    whole[1].start()
    out[2 * radii :, :] = ustar[2 * radii :, :] + delta[:, 2 * columns :] - result[radii:] * (inverse * (turning / NTH))
    whole[2].start()
    for copy in whole:
        copy.wait()


def place_kernel(capacity, slabs, moved, out):
    rows = slabs * capacity
    width = 768
    split = jnp.concatenate([p.astype(bf16) for p in pieces(moved[...], 2)], 1)
    for start in range(0, rows, width):
        place = start + iota((slabs, width), 1)
        hot = (place // capacity == iota((slabs, width), 0)).astype(bf16)
        spread = dot(split, jnp.concatenate([hot, hot], 0))
        match = (start + iota((capacity, width), 1)) % capacity == iota((capacity, width), 0)
        for f in range(FEATURES):
            block = spread[f * capacity : (f + 1) * capacity]
            out[f : f + 1, start : start + width] = jnp.sum(jnp.where(match, block, 0.0), axis=0, keepdims=True)


def shape(*dims):
    return jax.ShapeDtypeStruct(dims, f32)


def params(mib):
    return pltpu.CompilerParams(vmem_limit_bytes=int(mib * 1024 * 1024))


def cost(microseconds):
    return pl.CostEstimate(flops=0, bytes_accessed=int(microseconds * 3.0e6), transcendentals=0)


def body(velocity, viscosity, parcels, dest_rank, dest_cell, counts):
    slabs = lax.axis_size("gz")
    ring = lax.axis_size("pa")
    planes, radii, columns = viscosity.shape
    block = parcels.shape[0]
    capacity = 3 * block // slabs
    lines = -(-(FEATURES + 2) * capacity // LANES)
    vmem = pl.BlockSpec(memory_space=pltpu.VMEM)
    hbm = pl.BlockSpec(memory_space=pltpu.HBM)
    u = velocity.reshape(3 * radii, columns)
    nu = viscosity.reshape(radii, columns)
    features = FEATURES * capacity
    send, fields = pl.pallas_call(
        functools.partial(pack_kernel, capacity, slabs),
        out_shape=(shape(slabs * lines, LANES), shape(4 * radii, columns)),
        in_specs=[hbm] * 6,
        out_specs=(vmem,) * 2,
        scratch_shapes=[
            pltpu.SMEM((1,), jnp.int32),
            pltpu.VMEM((FEATURES, block), f32),
            pltpu.VMEM((1, block), jnp.int32),
            pltpu.VMEM((1, block), jnp.int32),
            pltpu.VMEM((2 * (FEATURES + 1) * SUBLANES, block), bf16),
            pltpu.VMEM((capacity // SUBLANES * slabs, block), bf16),
            pltpu.SemaphoreType.DMA((6,)),
        ],
        compiler_params=params(60),
        cost_estimate=cost(3),
        name="pack",
    )(counts, parcels.T, dest_rank.reshape(1, block), dest_cell.reshape(1, block), u, nu)
    received = lax.all_to_all(
        send.reshape(slabs, lines, LANES), "gz", split_axis=0, concat_axis=0, tiled=True
    ).reshape(slabs * lines, LANES)

    near = lax.ppermute(fields, "gz", [(i, i ^ 1) for i in range(slabs)])
    pairs = [(i, i + 1) for i in range(1, slabs - 1, 2)]
    far = lax.ppermute(fields, "gz", pairs + [(j, i) for i, j in pairs])
    transform = jnp.asarray(transform_table(ring, columns))
    reduction, elimination = [jnp.asarray(table) for table in solve_tables()]
    held = pl.pallas_call(
        hold_kernel,
        out_shape=shape(*fields.shape),
        in_specs=[vmem],
        out_specs=vmem,
        compiler_params=params(16),
        cost_estimate=cost(1),
        name="hold",
    )(fields)
    partial, halves, edges = pl.pallas_call(
        stencil_kernel,
        out_shape=(
            shape(3 * radii, columns),
            jax.ShapeDtypeStruct((3 * radii, 2 * columns), bf16),
            shape(EDGE_ROWS, LANES),
        ),
        in_specs=[vmem] * 3,
        out_specs=(vmem,) * 3,
        compiler_params=params(16),
        cost_estimate=cost(2),
        name="stencil",
    )(held, near, far)

    ustar, payload, moved = pl.pallas_call(
        functools.partial(momentum_kernel, capacity, slabs),
        out_shape=(
            shape(3 * radii, columns),
            shape(ring, radii + EDGE_ROWS, columns),
            shape(features, slabs),
        ),
        in_specs=[vmem] * 4,
        out_specs=(vmem,) * 3,
        scratch_shapes=[
            pltpu.VMEM((radii, capacity * slabs), bf16),
            pltpu.VMEM((3, capacity, slabs), f32),
            pltpu.VMEM((3 * columns, capacity * slabs), bf16),
            pltpu.VMEM((EDGE_ROWS, LANES), f32),
        ],
        compiler_params=params(16),
        cost_estimate=cost(4),
        name="momentum",
    )(received, partial, halves, edges)

    gathered = lax.all_to_all(payload, "pa", split_axis=0, concat_axis=0, tiled=True)
    parcels_out = pl.pallas_call(
        functools.partial(place_kernel, capacity, slabs),
        out_shape=shape(FEATURES, slabs * capacity),
        in_specs=[vmem],
        out_specs=vmem,
        compiler_params=params(16),
        cost_estimate=cost(3),
        name="place",
    )(moved)
    velocity_out = pl.pallas_call(
        project_kernel,
        out_shape=shape(3 * radii, columns),
        in_specs=[vmem] * 4 + [hbm],
        out_specs=hbm,
        scratch_shapes=[
            pltpu.VMEM((2 * radii + SUBLANES, elimination.shape[1]), f32),
            pltpu.VMEM((radii, NTH), f32),
            pltpu.VMEM((3 * radii, columns), f32),
            pltpu.SemaphoreType.DMA((4,)),
        ],
        compiler_params=params(51.25),
        cost_estimate=cost(5),
        name="project",
    )(gathered, ustar, transform, reduction, elimination)
    return velocity_out.reshape(velocity.shape), parcels_out.T


def solution(mesh):
    in_specs = (
        P(None, "gz", None, "pa"),
        P("gz", None, "pa"),
        P(("gz", "pa"), None),
        P(("gz", "pa"), None),
        P(("gz", "pa")),
        P(("gz", "pa")),
    )
    out_specs = (P(None, "gz", None, "pa"), P(("gz", "pa"), None))
    return jax.shard_map(body, mesh=mesh, in_specs=in_specs, out_specs=out_specs, check_vma=False)
```
